32 devices in a mesh: rows: 8 (over z, x), blk: 4 (over y, core).
Axes of the slice: x: 2, y: 2, z: 4, core: 2. Of those that a mesh axis runs over, the one named last changes fastest.
Arguments:
- inputs: bfloat16 [512, 48, 512], P('blk', 'rows'), may hold values from -6 to 6
- cotangent: bfloat16 [512, 48, 512], P('blk', 'rows'), may hold values from -12 to 12, as said below
- lengths: int32 [48, 4], P('rows'), may hold values from 1 to 448, as said below
- up_weight: float32 [512, 3072], P('rows'), may hold values from -0.25 to 0.25
- up_moment: float32 [512, 3072], P('rows'), may hold values from -0.0009765625 to 0.0009765625
- up_square: float32 [512, 3072], P('rows'), may hold values from 3.8028133e-10 to 1.5211253e-09
- down_weight: float32 [1536, 512], P('rows'), may hold values from -0.15625 to 0.15625
- down_moment: float32 [1536, 512], P('rows'), may hold values from -0.0009765625 to 0.0009765625
- down_square: float32 [1536, 512], P('rows'), may hold values from 3.8028133e-10 to 1.5211253e-09
- spatial_weight: float32 [512, 512], P('rows'), may hold values from -0.25 to 0.25
- spatial_moment: float32 [512, 512], P('rows'), may hold values from -0.0009765625 to 0.0009765625
- spatial_square: float32 [512, 512], P('rows'), may hold values from 3.8028133e-10 to 1.5211253e-09
- small_params: float32 [8192], P('rows'), may hold values from -1.2 to 6.5
- small_moment: float32 [8192], P('rows'), may hold values from -0.0009765625 to 0.0009765625
- small_square: float32 [8192], P('rows'), may hold values from 3.8028133e-10 to 1.5211253e-09
Outputs:
- output: bfloat16 [512, 48, 512], P('blk', 'rows')
- input_grad: bfloat16 [512, 48, 512], P('blk', 'rows')
- grad_norm: float32 [], replicated
- up_next: float32 [512, 3072], P('rows')
- up_moment_next: float32 [512, 3072], P('rows')
- up_square_next: float32 [512, 3072], P('rows')
- down_next: float32 [1536, 512], P('rows')
- down_moment_next: float32 [1536, 512], P('rows')
- down_square_next: float32 [1536, 512], P('rows')
- spatial_next: float32 [512, 512], P('rows')
- spatial_moment_next: float32 [512, 512], P('rows')
- spatial_square_next: float32 [512, 512], P('rows')
- small_next: float32 [8192], P('rows')
- small_moment_next: float32 [8192], P('rows')
- small_square_next: float32 [8192], P('rows')
The draws below stay inside these ranges and needn't reach their ends.
Inputs may be any that keep to these rules, and one draw needn't show every extreme that they name: `lengths`: each row's documents fill its first slots and together leave 0 to 16 slots of padding at its end; one document of every row holds 448 slots, at a place drawn for the row. `cotangent`: scale rises along the slots.
All inputs are finite; a program needn't handle non-finite values.
Results may differ from the reference program's by a relative error of at most 0.012.
Values may be sent and summed in bfloat16 or wider, within the bound.
A program may use at most 192 MiB of HBM per device.

```python
import math
import jax
import jax.numpy as jnp
from jax import lax

D = 512
FF = 3072
S = 512
G = 1536
NDOC = 4
STEP = 10
ROWS = 48
NSMALL = 8192
NPARAM = 2629632


def draw_cotangent(key, part):
    key = jax.random.fold_in(key, 7)
    position = (jnp.arange(S, dtype=jnp.float32) / S)[:, None, None]
    values = jax.random.truncated_normal(key, -4.0, 4.0, (S, ROWS, D), jnp.float32)
    rise = 1.0 + 2.0 * position
    return (values * rise).astype(jnp.bfloat16)


def draw_lengths(key, part):
    key = jax.random.fold_in(key, 11)
    keys = jax.random.split(key, 4)
    padding = jax.random.randint(keys[0], (ROWS,), 0, S // 32 + 1)
    rest = S // 8 - padding
    first = jax.random.randint(keys[1], (ROWS,), 1, rest - 1)
    second = jax.random.randint(keys[2], (ROWS,), 1, rest - first)
    third = rest - first - second
    longest = jnp.full((ROWS,), 7 * S // 8, jnp.int32)
    docs = jnp.stack([longest, first, second, third], axis=1).astype(jnp.int32)
    scores = jax.random.randint(keys[3], (ROWS, 4), 0, 1 << 20) * 4 + jnp.arange(4, dtype=jnp.int32)[None, :]
    order = jnp.argsort(scores, axis=1)
    return jnp.take_along_axis(docs, order, axis=1).astype(jnp.int32)


def draw_small_params(key, part):
    key = jax.random.fold_in(key, 13)
    keys = jax.random.split(key, 7)
    across_d = jnp.arange(D, dtype=jnp.float32) / D
    across_g = jnp.arange(G, dtype=jnp.float32) / G
    slope = 2.0
    wobble = 0.2
    gain_in = (1.0 + slope * across_d) * jax.random.uniform(keys[0], (D,), jnp.float32, 1.0 - wobble, 1.0 + wobble)
    shift_in = 0.3 * jax.random.truncated_normal(keys[1], -4.0, 4.0, (D,), jnp.float32)
    bias_up = 0.3 * jax.random.truncated_normal(keys[2], -4.0, 4.0, (FF,), jnp.float32)
    gain_gate = (1.0 + slope * across_g) * jax.random.uniform(keys[3], (G,), jnp.float32, 1.0 - wobble, 1.0 + wobble)
    shift_gate = 0.3 * jax.random.truncated_normal(keys[4], -4.0, 4.0, (G,), jnp.float32)
    bias_spatial = jax.random.uniform(keys[5], (S,), jnp.float32, 0.5, 1.5)
    bias_down = 0.3 * jax.random.truncated_normal(keys[6], -4.0, 4.0, (D,), jnp.float32)
    return jnp.concatenate([gain_in, shift_in, bias_up, gain_gate, shift_gate, bias_spatial, bias_down])


def shard_levels(key, shape, cuts, low, largest):
    factor_of, own = 1.0, jax.random.fold_in(key, 6)
    for dim, parts in cuts:
        draws = jnp.exp(jax.random.uniform(jax.random.fold_in(own, dim), (parts,), jnp.float32, low / len(cuts), largest / len(cuts)))
        factor_of = factor_of * jnp.repeat(draws, shape[dim] // parts).reshape([-1 if axis == dim else 1 for axis in range(len(shape))])
    return factor_of


def noise(key, dims, scale, most, cuts=(), held_as=jnp.bfloat16):
    loudness = shard_levels(key, dims, cuts, -0.22, 0.18) if cuts else 1.0
    values = jax.random.normal(key, dims, jnp.float32) * scale * loudness
    return jnp.minimum(jnp.maximum(values, -most), most).astype(held_as)


def setup_inputs(seed: int = 0) -> dict:
    seeds = jax.random.split(jax.random.key(seed), 16)
    inputs = noise(seeds[0], (S, ROWS, D), 1.0, 6.0, ((0, 4), (1, 8)))
    cotangent = draw_cotangent(jax.random.fold_in(seeds[15], 71), 0)
    lengths = draw_lengths(jax.random.fold_in(seeds[15], 71), 0)
    up_weight = noise(seeds[3], (D, FF), D ** -0.5, 0.25, ((0, 8),), jnp.float32)
    up_moment = noise(seeds[4], (D, FF), (0.11 / NPARAM ** 0.5), 0.0009765625, ((0, 8),), jnp.float32)
    up_square = jnp.clip(jnp.exp(math.log(1.5211253368008215e-09) - 1.3862944 * jax.random.uniform(seeds[5], (D, FF), jnp.float32) ** shard_levels(seeds[5], (D, FF), ((0, 8),), -0.2, 0.2)), 3.802813342002054e-10, 1.5211253368008215e-09)
    down_weight = noise(seeds[6], (G, D), G ** -0.5, 0.15625, ((0, 8),), jnp.float32)
    down_moment = noise(seeds[7], (G, D), (0.11 / NPARAM ** 0.5), 0.0009765625, ((0, 8),), jnp.float32)
    down_square = jnp.clip(jnp.exp(math.log(1.5211253368008215e-09) - 1.3862944 * jax.random.uniform(seeds[8], (G, D), jnp.float32) ** shard_levels(seeds[8], (G, D), ((0, 8),), -0.2, 0.2)), 3.802813342002054e-10, 1.5211253368008215e-09)
    spatial_weight = noise(seeds[9], (S, S), S ** -0.5, 0.25, ((0, 8),), jnp.float32)
    spatial_moment = noise(seeds[10], (S, S), (0.11 / NPARAM ** 0.5), 0.0009765625, ((0, 8),), jnp.float32)
    spatial_square = jnp.clip(jnp.exp(math.log(1.5211253368008215e-09) - 1.3862944 * jax.random.uniform(seeds[11], (S, S), jnp.float32) ** shard_levels(seeds[11], (S, S), ((0, 8),), -0.2, 0.2)), 3.802813342002054e-10, 1.5211253368008215e-09)
    small_params = draw_small_params(jax.random.fold_in(seeds[15], 71), 0)
    small_moment = noise(seeds[13], (NSMALL,), (0.11 / NPARAM ** 0.5), 0.0009765625, ((0, 8),), jnp.float32)
    small_square = jnp.clip(jnp.exp(math.log(1.5211253368008215e-09) - 1.3862944 * jax.random.uniform(seeds[14], (NSMALL,), jnp.float32) ** shard_levels(seeds[14], (NSMALL,), ((0, 8),), -0.2, 0.2)), 3.802813342002054e-10, 1.5211253368008215e-09)
    return dict(inputs=inputs, cotangent=cotangent, lengths=lengths, up_weight=up_weight, up_moment=up_moment, up_square=up_square, down_weight=down_weight, down_moment=down_moment, down_square=down_square, spatial_weight=spatial_weight, spatial_moment=spatial_moment, spatial_square=spatial_square, small_params=small_params, small_moment=small_moment, small_square=small_square)


@jax.custom_vjp
def low(v):
    return lax.optimization_barrier(v.astype(jnp.bfloat16)).astype(jnp.float32)

@jax.custom_vjp
def low_back(v):
    return v

def low_keep(v):
    return (low(v), None)

def low_pass(kept, grad):
    return (grad,)

def back_keep(v):
    return (v, None)

def back_low(kept, grad):
    return (low(grad),)
low.defvjp(low_keep, low_pass)
low_back.defvjp(back_keep, back_low)
group_rows = 8
beta_one = 0.9
beta_two = 0.999
max_norm = 1.0
weight_rate = 0.05
small_rate = 0.5
weight_decay = 0.01

def layer_norm(values, gain, shift):
    mean = lax.optimization_barrier(jnp.mean(values, axis=-1, keepdims=True))
    centred = values - mean
    spread = lax.optimization_barrier(jnp.mean(centred * centred, axis=-1, keepdims=True))
    return centred * lax.rsqrt(spread + 1e-05) * gain + shift

def split_small(small, width, hidden, half, slots):
    sizes_list = [width, width, hidden, half, half, slots, width]
    pieces = []
    offset = 0
    for length in sizes_list:
        pieces.append(small[offset:offset + length])
        offset = offset + length
    return pieces

def segment_ids(lengths, slots):
    ends = jnp.cumsum(lengths, axis=-1).astype(jnp.int32)
    places = jnp.arange(slots, dtype=jnp.int32)
    labels = lax.optimization_barrier(jnp.sum((places[None, None, :] >= ends[:, :, None]).astype(jnp.int32), axis=1))
    valid = places[None, :] < ends[:, -1:]
    return (labels, valid)

def source_mask(lengths, slots):
    labels, valid = segment_ids(lengths, slots)
    same = labels[:, :, None] == labels[:, None, :]
    return (same & valid[:, None, :]).astype(jnp.float32)

def adam_step(weight, moment, square, grad, rate, decay):
    moment_next = beta_one * moment + (1.0 - beta_one) * grad
    square_next = beta_two * square + (1.0 - beta_two) * grad * grad
    moment_hat = moment_next / (1.0 - beta_one ** STEP)
    square_hat = square_next / (1.0 - beta_two ** STEP)
    weight_next = weight - rate * (moment_hat / (jnp.sqrt(square_hat) + 1e-08) + decay * weight)
    return (weight_next, moment_next, square_next)

def reference(inputs, cotangent, lengths, up_weight, up_moment, up_square, down_weight, down_moment, down_square, spatial_weight, spatial_moment, spatial_square, small_params, small_moment, small_square):
    highest = lax.Precision.HIGHEST
    rows_first = jnp.transpose(inputs.astype(jnp.float32), (1, 0, 2))
    grads_first = jnp.transpose(cotangent.astype(jnp.float32), (1, 0, 2))
    groups = ROWS // group_rows

    def forward(params, values):
        up_low = low(params[0])
        down_low = low(params[1])
        spatial_low = low(params[2])
        small_low = low(params[3])
        gain_in, shift_in, bias_up, gain_gate, shift_gate, bias_spatial, bias_down = split_small(small_low, D, FF, G, S)

        def block_fn(pair):
            vals, lens = pair
            normed = low(layer_norm(vals, gain_in, shift_in))
            before = low_back(jnp.einsum('rsd,df->rsf', normed, up_low, precision=highest) + bias_up)
            active = jax.nn.gelu(before, approximate=False)
            content = active[..., :G]
            gate = low(layer_norm(active[..., G:], gain_gate, shift_gate))
            mask = source_mask(lens, S)
            mixed = jnp.einsum('rts,rsc->rtc', mask * spatial_low[None], gate, precision=highest)
            spatial_out = low_back(mixed + bias_spatial[None, :, None])
            product = low(content * spatial_out)
            return jnp.einsum('rsg,gd->rsd', product, down_low, precision=highest) + bias_down + vals
        stacked = lax.map(jax.checkpoint(block_fn), (values.reshape(groups, group_rows, S, D), lengths.reshape(groups, group_rows, NDOC)))
        return stacked.reshape(ROWS, S, D)
    result, pull = jax.vjp(forward, (up_weight, down_weight, spatial_weight, small_params), rows_first)
    grads, input_grad = pull(grads_first)
    grad_up, grad_down, grad_spatial, grad_small = grads
    total = jnp.sum(grad_up * grad_up) + jnp.sum(grad_down * grad_down) + jnp.sum(grad_spatial * grad_spatial) + jnp.sum(grad_small * grad_small)
    grad_norm = jnp.sqrt(total)
    factor = jnp.minimum(1.0, max_norm / (grad_norm + 1e-06))
    up_all = adam_step(up_weight, up_moment, up_square, factor * grad_up, weight_rate, weight_decay)
    down_all = adam_step(down_weight, down_moment, down_square, factor * grad_down, weight_rate, weight_decay)
    spatial_all = adam_step(spatial_weight, spatial_moment, spatial_square, factor * grad_spatial, weight_rate, weight_decay)
    small_all = adam_step(small_params, small_moment, small_square, factor * grad_small, small_rate, 0.0)
    output = jnp.transpose(result, (1, 0, 2)).astype(jnp.bfloat16)
    input_out = jnp.transpose(input_grad, (1, 0, 2)).astype(jnp.bfloat16)
    return (output, input_out, grad_norm, up_all[0], up_all[1], up_all[2], down_all[0], down_all[1], down_all[2], spatial_all[0], spatial_all[1], spatial_all[2], small_all[0], small_all[1], small_all[2])
```

```python
import functools
import math
import types

import jax
import jax.numpy as jnp
from jax import lax
from jax.experimental import pallas as pl
from jax.experimental.pallas import tpu as pltpu
from jax.sharding import PartitionSpec as P

STEP = 10

beta_one = 0.9
beta_two = 0.999
max_norm = 1.0
weight_rate = 0.05
small_rate = 0.5
weight_decay = 0.01

MESH = pl.DeviceIdType.MESH
VMEM = pltpu.VMEM
bf16 = jnp.bfloat16
f32 = jnp.float32
LANES = 128


def loop(count, body):
    def step(i, carry):
        body(i)
        return carry

    lax.fori_loop(0, count, step, 0)


def span(start, size):
    return pl.ds(pl.multiple_of(start, size), size)


def rows_of(value, count):
    return jnp.concatenate([value] * (count // value.shape[0]), axis=0)


def lanes_of(value, count):
    return jnp.concatenate([value] * (count // value.shape[1]), axis=1)


def fold_rows(value):
    total = value[0:8]
    for first in range(8, value.shape[0], 8):
        total = total + value[first : first + 8]
    return total


def fold_lanes(value):
    total = value[:, 0:LANES]
    for first in range(LANES, value.shape[1], LANES):
        total = total + value[:, first : first + LANES]
    return total


def dot_nn(a, b):
    return lax.dot_general(a, b, (((1,), (0,)), ((), ())), preferred_element_type=f32)


def dot_nt(a, b):
    return lax.dot_general(a, b, (((1,), (1,)), ((), ())), preferred_element_type=f32)


def dot_tn(a, b):
    return lax.dot_general(a, b, (((0,), (0,)), ((), ())), preferred_element_type=f32)


def plan_of(mesh, shapes):
    d = types.SimpleNamespace()
    d.R = mesh.shape["rows"]
    d.minor = 1
    while d.minor * d.minor * 2 <= d.R:
        d.minor *= 2
    if d.minor * d.minor > d.R:
        d.minor //= 2
    d.major = d.R // d.minor
    d.block, d.rows_here, d.D = shapes["inputs"]
    d.S = d.block * mesh.shape["blk"]
    d.H = d.S // 2
    d.T = d.S + d.H
    d.FF = shapes["up"][1]
    d.G = d.FF // 2
    d.su, d.sd, d.ss = shapes["up"][0], shapes["down"][0], shapes["spatial"][0]
    d.ks = shapes["small"][0] // LANES
    d.nsmall = d.ks * d.R * LANES
    d.wide = d.su % 16 != 0 or d.sd % 16 != 0 or d.ss % 16 != 0
    d.o_gain_in = 0
    d.o_shift_in = d.D
    d.o_bias_up = 2 * d.D
    d.o_gain_gate = d.o_bias_up + d.FF
    d.o_shift_gate = d.o_gain_gate + d.G
    d.o_bias_spatial = d.o_shift_gate + d.G
    d.o_bias_down = d.o_bias_spatial + d.S
    return d


class Comm:
    def __init__(self, send, recv):
        self.send, self.recv, self.next = send, recv, 0
        self.open = []

    def copy(self, src, dst, device):
        i = self.next
        self.next += 1
        made = pltpu.make_async_remote_copy(
            src_ref=src,
            dst_ref=dst,
            send_sem=self.send.at[i],
            recv_sem=self.recv.at[i],
            device_id=device,
            device_id_type=MESH,
        )
        return made

    def start(self, src, dst, device):
        made = self.copy(src, dst, device)
        made.start()
        self.open.append(made)
        return made

    def finish(self):
        for made in self.open:
            made.wait_send()
        self.open = []


def main_kernel(d, names, count, *refs):
    k = types.SimpleNamespace(**dict(zip(names, refs)))
    comm = Comm(k.send_sem, k.recv_sem)
    r, b = lax.axis_index("rows"), lax.axis_index("blk")
    zi, xi = r // d.minor, lax.rem(r, d.minor)
    y, c = b // 2, lax.rem(b, 2)
    S, H, T, D, G, FF = d.S, d.H, d.T, d.D, d.G, d.FF
    blk = d.block
    sibling = (r, 2 * y + 1 - c)
    across = (r, 2 * (1 - y) + c)

    def at_z(dz):
        return (lax.rem(zi + dz, d.major) * d.minor + xi, b)

    def at_x(dx):
        return (zi * d.minor + lax.rem(xi + dx, d.minor), b)

    barrier = pltpu.get_barrier_semaphore()
    for dr in range(1, d.R):
        pl.semaphore_signal(barrier, inc=1, device_id=(lax.rem(r + dr, d.R), b), device_id_type=MESH)
    for db in range(1, 4):
        pl.semaphore_signal(barrier, inc=1, device_id=(r, lax.rem(b + db, 4)), device_id_type=MESH)

    own = [
        pltpu.make_async_copy(k.small_w, k.small_stage, k.local_sem.at[0]),
        pltpu.make_async_copy(k.up_w, k.up_stage, k.local_sem.at[1]),
        pltpu.make_async_copy(k.sp_w, k.sp_stage, k.local_sem.at[2]),
        pltpu.make_async_copy(k.down_w, k.down_stage, k.local_sem.at[3]),
    ]
    for copy in own:
        copy.start()
    wire = f32 if d.wide else bf16
    groups = [
        ("up_gate", k.up_get, k.up_stage, d.su, G, G),
        ("up_content", k.up_get, k.up_stage, d.su, 0, G),
        ("spatial", k.sp_get, k.sp_stage, d.ss, 0, S),
        ("down", k.down_get, k.down_stage, d.sd, 0, D),
    ]

    own[0].wait()
    k.small_get[r] = jnp.zeros((8, LANES), f32)
    k.small_get[r, 0 : d.ks, :] = k.small_stage[...].astype(bf16).astype(f32)
    own[1].wait()
    if not d.wide:
        k.up_get[span(r * d.su, d.su), :] = k.up_stage[...].astype(bf16)
        own[2].wait()
        k.sp_get[span(r * d.ss, d.ss), :] = k.sp_stage[...].astype(bf16)
        own[3].wait()
        k.down_get[span(r * d.sd, d.sd), :] = k.down_stage[...].astype(bf16)
    else:
        own[2].wait()
        own[3].wait()
        copies = [
            pltpu.make_async_copy(k.up_stage, k.up_get.at[span(r * d.su, d.su), :], k.local_sem.at[1]),
            pltpu.make_async_copy(k.sp_stage, k.sp_get.at[span(r * d.ss, d.ss), :], k.local_sem.at[2]),
            pltpu.make_async_copy(k.down_stage, k.down_get.at[span(r * d.sd, d.sd), :], k.local_sem.at[3]),
        ]
        for copy in copies:
            copy.start()
        for copy in copies:
            copy.wait()

    pl.semaphore_wait(barrier, d.R - 1 + 3)

    def blk_of(g):
        return (r, g)

    tokens = []
    for number, (source, target) in enumerate(((k.x_in, k.X), (k.c_in, k.C))):
        for g in range(4):
            row = (g // 2) * 3 + g % 2
            tokens.append((source.at[row], target.at[span(b * blk, blk), :], g, number * 6 + g))
        for half in range(2):
            row = half * 3 + 2
            tokens.append(
                (source.at[row], target.at[span(S + c * blk, blk), :], 2 * half + y, number * 6 + 4 + half)
            )

    def i_recv(i):
        number, which = i // 6, i % 6
        if which < 4:
            return number * 6 + b
        return number * 6 + 4 + c

    def start_tokens(number):
        for entry in tokens[number * 6 : number * 6 + 6]:
            src, dst, g, i = entry
            slot = i_recv(i)

            @pl.when(g == b)
            def _():
                pltpu.make_async_copy(src, dst, k.token_recv.at[slot]).start()

            @pl.when(g != b)
            def _():
                pltpu.make_async_remote_copy(
                    src_ref=src,
                    dst_ref=dst,
                    send_sem=k.token_send.at[i],
                    recv_sem=k.token_recv.at[slot],
                    device_id=blk_of(g),
                    device_id_type=MESH,
                ).start()

    def wait_tokens(number):
        target = (k.X, k.C)[number]
        for g in range(4):
            pltpu.make_async_copy(
                k.x_in.at[0], target.at[g * blk : (g + 1) * blk, :], k.token_recv.at[number * 6 + g]
            ).wait()
        for j in range(2):
            pltpu.make_async_copy(
                k.x_in.at[0], target.at[S + j * blk : S + (j + 1) * blk, :], k.token_recv.at[number * 6 + 4 + j]
            ).wait()

    def finish_tokens():
        for src, dst, g, i in tokens:

            @pl.when(g != b)
            def _():
                pltpu.make_async_remote_copy(
                    src_ref=src,
                    dst_ref=dst,
                    send_sem=k.token_send.at[i],
                    recv_sem=k.token_recv.at[i],
                    device_id=blk_of(g),
                    device_id_type=MESH,
                ).wait_send()

    start_tokens(0)

    small_copies = []
    for dr in range(1, d.R):
        small_copies.append(
            comm.start(k.small_get.at[r], k.small_get.at[r], (lax.rem(r + dr, d.R), b))
        )

    def region(group, owner):
        name, ref, stage, s, first, width = group
        half = width // 2
        return ref.at[span(owner * s, s), pl.ds(pl.multiple_of(first + c * half, half), half)]

    def owner_of(dz, dx):
        return lax.rem(zi - dz + d.major, d.major) * d.minor + lax.rem(xi - dx + d.minor, d.minor)

    gather = {}
    for group in groups:
        state = types.SimpleNamespace(z={}, x={}, core={})
        gather[group[0]] = state
        mine = region(group, r)
        for dz in range(1, d.major):
            state.z[dz] = comm.start(mine, mine, at_z(dz))
    start_tokens(1)

    def forward_minor(group):
        state = gather[group[0]]
        for dz in range(d.major):
            piece = region(group, owner_of(dz, 0))
            if dz:
                state.z[dz].wait_recv()
            for dx in range(1, d.minor):
                state.x[dz, dx] = comm.start(piece, piece, at_x(dx))
            if dz:
                state.core[dz, 0] = comm.start(piece, piece, sibling)

    def forward_core(group):
        state = gather[group[0]]
        for dz in range(d.major):
            for dx in range(1, d.minor):
                state.x[dz, dx].wait_recv()
                piece = region(group, owner_of(dz, dx))
                state.core[dz, dx] = comm.start(piece, piece, sibling)

    def arrived(group):
        for copy in gather[group[0]].core.values():
            copy.wait_recv()

    def to_low(group):
        name, ref, stage, s, first, width = group
        low = {"up_gate": k.UP, "up_content": k.UP, "spatial": k.SP, "down": k.DOWN}[name]
        total = low.shape[0]
        step = 256

        def body(i):
            rows = span(i * step, step)
            part = k.F.at[0:step, 0:width]
            copy = pltpu.make_async_copy(ref.at[rows, first : first + width], part, k.local_sem.at[0])
            copy.start()
            copy.wait()
            low[rows, first : first + width] = part[...].astype(bf16)

        loop(total // step, body)

    for copy in small_copies:
        copy.wait_recv()
    for i in range(d.R):
        for j in range(d.ks):
            first = (i * d.ks + j) * LANES
            k.SM[:, first : first + LANES] = jnp.broadcast_to(k.small_get[i, j : j + 1, :], (8, LANES))

    def small(offset, width, rows):
        return rows_of(k.SM[:, offset : offset + width], rows)

    def ends_of(row):
        ends = [k.lengths[row, 0]]
        for n in range(1, k.lengths.shape[1]):
            ends.append(ends[-1] + k.lengths[row, n])
        return ends

    def label_of(places, ends, source):
        label = jnp.zeros(places.shape, f32)
        for end in ends:
            label = label + jnp.where(places >= end, 1.0, 0.0)
        if source:
            label = jnp.where(places < ends[-1], label, -1.0)
        return label

    def make_labels():
        for which, row in enumerate((3 * y + c, 3 * y + 2)):
            ends = ends_of(row)
            lane = lax.broadcasted_iota(jnp.int32, (8, S), 1)
            k.row_t[which] = label_of(lane, ends, False)
            k.row_s[which] = label_of(lane, ends, True)
            for first in range(0, S, 64):
                place = lax.broadcasted_iota(jnp.int32, (64, LANES), 0) + first
                k.col_t[which, first : first + 64, :] = label_of(place, ends, False)
                k.col_s[which, first : first + 64, :] = label_of(place, ends, True)

    def make_mixing():
        k.F[0:S, 0:S] = k.SP[...].astype(f32)
        k.F[0:S, S : 2 * S] = jnp.transpose(k.F[0:S, 0:S])

        def body(i):
            rows = span(i * 32, 32)
            keep = lanes_of(k.col_t[0, rows, :], S) == rows_of(k.row_s[0], 32)
            k.M[rows, :] = jnp.where(keep, k.F[rows, 0:S], 0.0).astype(bf16)
            keep = lanes_of(k.col_s[0, rows, :], S) == rows_of(k.row_t[0], 32)
            k.MT[rows, :] = jnp.where(keep, k.F[rows, S : 2 * S], 0.0).astype(bf16)

        loop(S // 32, body)

        def shared(i):
            rows = span(c * H + i * 32, 32)
            keep = lanes_of(k.col_t[1, rows, :], S) == rows_of(k.row_s[1], 32)
            k.M[span(S + i * 32, 32), :] = jnp.where(keep, k.F[rows, 0:S], 0.0).astype(bf16)

        loop(H // 32, shared)
        own_half = pl.ds(pl.multiple_of(c * H, H), H)
        own_lanes = pl.ds(pl.multiple_of(S + c * H, H), H)

        def turned(i):
            rows = span(i * 32, 32)
            keep = lanes_of(k.col_s[1, rows, :], H) == rows_of(k.row_t[1, :, own_half], 32)
            k.MTB[rows, :] = jnp.where(keep, k.F[rows, own_lanes], 0.0).astype(bf16)

        loop(S // 32, turned)
        bias = k.SM[:, d.o_bias_spatial : d.o_bias_spatial + S]
        k.BS[0:S, :] = jnp.transpose(rows_of(bias, LANES))
        k.BS[S:T, :] = k.BS[span(c * H, H), :]

    def input_norm():
        def body(i):
            rows = span(i * 32, 32)
            x = k.X[rows, :].astype(f32)
            centred = x - jnp.mean(x, axis=1, keepdims=True)
            spread = jnp.mean(centred * centred, axis=1, keepdims=True)
            normed = centred * lax.rsqrt(spread + 1e-05)
            normed = normed * small(d.o_gain_in, D, 32) + small(d.o_shift_in, D, 32)
            k.N[rows, :] = normed.astype(bf16)

        loop(T // 32, body)
        k.NT[...] = jnp.transpose(k.N[...].astype(f32)).astype(bf16)

    CH = 512

    def gelu_parts(before):
        cdf = 0.5 + 0.5 * lax.erf(before * 0.7071067811865476)
        bell = jnp.exp(before * before * -0.5)
        return before * cdf, cdf + before * bell * 0.3989422804014327

    def up_gate():
        def body(j):
            cols = span(j * CH, CH)
            k.F[:, cols] = dot_nn(k.N[...], k.UP[:, span(G + j * CH, CH)])
            bias = rows_of(k.SM[:, pl.ds(pl.multiple_of(d.o_bias_up + G + j * CH, LANES), CH)], 16)
            for first in range(0, T, 16):
                active, slope = gelu_parts(k.F[first : first + 16, cols] + bias)
                k.F[first : first + 16, cols] = active
                k.DG[first : first + 16, cols] = slope.astype(bf16)

        loop(G // CH, body)

    def gate_norm(first_row, count, place):
        def body(i):
            rows = span(first_row + i * 16, 16)
            active = k.F[rows, :]
            centred = active - jnp.mean(active, axis=1, keepdims=True)
            spread = jnp.mean(centred * centred, axis=1, keepdims=True)
            scale = lax.rsqrt(spread + 1e-05)
            xhat = centred * scale
            k.XH[rows, :] = xhat.astype(bf16)
            k.RG[rows, :] = jnp.broadcast_to(scale, (16, LANES))
            gate = xhat * small(d.o_gain_gate, G, 16) + small(d.o_shift_gate, G, 16)
            k.GATE[span(place + i * 16, 16), :] = gate.astype(bf16)

        loop(count // 16, body)

    def up_content():
        def body(j):
            cols = span(j * CH, CH)
            k.FA[...] = dot_nn(k.N[...], k.UP[:, cols])
            bias = rows_of(k.SM[:, pl.ds(pl.multiple_of(d.o_bias_up + j * CH, LANES), CH)], 16)
            for first in range(0, T, 16):
                active, slope = gelu_parts(k.FA[first : first + 16, :] + bias)
                k.CT[first : first + 16, cols] = active.astype(bf16)
                k.DC[first : first + 16, cols] = slope.astype(bf16)

        loop(G // CH, body)

    def mix():
        k.BSA[...] = jnp.zeros_like(k.BSA)

        def body(j):
            cols = span(j * CH, CH)
            k.FA[0:S, :] = dot_nn(k.M[0:S, :], k.GATE[0:S, cols])
            k.FA[S:T, :] = dot_nn(k.M[S:T, :], k.GATE[S : 2 * S, cols])
            k.FB[...] = dot_nt(k.C[...], k.DOWN[cols, :])
            total = jnp.zeros((8, CH), f32)
            for first in range(0, T, 16):
                rows = slice(first, first + 16)
                out = k.FA[rows, :] + lanes_of(k.BS[rows, :], CH)
                grad = k.FB[rows, :]
                content = k.CT[rows, cols].astype(f32)
                k.PR[rows, cols] = (content * out).astype(bf16)
                grad_spatial = (grad * content).astype(bf16)
                k.GS[rows, cols] = grad_spatial
                k.BSA[rows, :] = k.BSA[rows, :] + fold_lanes(grad_spatial.astype(f32))
                before = (grad * out * k.DC[rows, cols].astype(f32)).astype(bf16)
                k.GB[rows, cols] = before
                total = total + fold_rows(before.astype(f32))
            k.SG[:, pl.ds(pl.multiple_of(d.o_bias_up + j * CH, LANES), CH)] = total

        loop(G // CH, body)

    def project():
        def body(i):
            rows = span(i * 256, 256)
            k.FA[rows, :] = dot_nn(k.PR[rows, :], k.DOWN[...])
            for j in range(0, 256, 16):
                part = span(i * 256 + j, 16)
                value = k.FA[part, :] + small(d.o_bias_down, D, 16) + k.X[part, :].astype(f32)
                k.OT[part, :] = value.astype(bf16)

        loop(T // 256, body)

    def grad_down():
        def body(j):
            k.PD[span(j * 256, 256), :] = dot_tn(k.PR[:, span(j * 256, 256)], k.C[...]).astype(bf16)

        loop(G // 256, body)

    def grad_up(first):
        def body(j):
            cols = pl.ds(pl.multiple_of(first + j * CH, CH), CH)
            k.PU[:, cols] = dot_nn(k.NT[...], k.GB[:, cols]).astype(bf16)

        loop(G // CH, body)

    def grad_spatial_weight():
        k.FA[0:S, :] = dot_nt(k.GS[0:S, :], k.GATE[0:S, :])
        k.FB[0:H, :] = dot_nt(k.GS[S:T, :], k.GATE[S : 2 * S, :])

        def body(i):
            rows = span(i * 32, 32)
            keep = lanes_of(k.col_t[0, rows, :], S) == rows_of(k.row_s[0], 32)
            k.FA[rows, :] = jnp.where(keep, k.FA[rows, :], 0.0)

        loop(S // 32, body)

        def shared(i):
            rows = span(c * H + i * 32, 32)
            keep = lanes_of(k.col_t[1, rows, :], S) == rows_of(k.row_s[1], 32)
            k.FA[rows, :] = k.FA[rows, :] + jnp.where(keep, k.FB[span(i * 32, 32), :], 0.0)

        loop(H // 32, shared)
        k.PS[...] = k.FA[0:S, :].astype(bf16)

    def grad_gate_shared():
        other = span((1 - c) * H, H)
        mine = span(c * H, H)

        def body(j):
            cols = span(j * CH, CH)
            k.GX[:, cols] = dot_nn(k.MTB[other, :], k.GS[S:T, cols]).astype(bf16)

        loop(G // CH, body)
        copy = comm.start(k.GX, k.GY, sibling)

        def later(j):
            cols = span(j * CH, CH)
            k.F[S:T, cols] = dot_nn(k.MTB[mine, :], k.GS[S:T, cols])
            k.F[0:S, cols] = dot_nn(k.MT[...], k.GS[0:S, cols])

        loop(G // CH, later)
        return copy

    def gate_back(copy):
        for offset in (d.o_gain_gate, d.o_shift_gate, d.o_bias_up + G):
            k.SG[:, offset : offset + G] = jnp.zeros((8, G), f32)

        def rows_back(rows, grad):
            xhat = k.XH[rows, :].astype(f32)
            scaled = grad * small(d.o_gain_gate, G, 16)
            along = jnp.mean(scaled, axis=1, keepdims=True)
            across_ = jnp.mean(scaled * xhat, axis=1, keepdims=True)
            scale = lanes_of(k.RG[rows, :], G)
            back = scale * (scaled - along - xhat * across_)
            before = (back * k.DG[rows, :].astype(f32)).astype(bf16)
            k.GB[rows, G:FF] = before
            for offset, term in (
                (d.o_gain_gate, grad * xhat),
                (d.o_shift_gate, grad),
                (d.o_bias_up + G, before.astype(f32)),
            ):
                k.SG[:, offset : offset + G] = k.SG[:, offset : offset + G] + fold_rows(term)

        def body(i):
            rows = span(i * 16, 16)
            rows_back(rows, k.F[rows, :])

        loop(S // 16, body)
        copy.wait_recv()

        def shared(i):
            rows = span(S + i * 16, 16)
            rows_back(rows, k.F[rows, :] + k.GY[span(i * 16, 16), :].astype(f32))

        loop(H // 16, shared)

    def grad_input():
        for offset in (d.o_gain_in, d.o_shift_in, d.o_bias_down):
            k.SG[:, offset : offset + D] = jnp.zeros((8, D), f32)

        def product(i):
            rows = span(i * 256, 256)
            k.FA[rows, :] = dot_nt(k.GB[rows, :], k.UP[...])

        loop(T // 256, product)

        def body(i):
            rows = span(i * 32, 32)
            x = k.X[rows, :].astype(f32)
            centred = x - jnp.mean(x, axis=1, keepdims=True)
            spread = jnp.mean(centred * centred, axis=1, keepdims=True)
            scale = lax.rsqrt(spread + 1e-05)
            xhat = centred * scale
            grad = k.FA[rows, :]
            scaled = grad * small(d.o_gain_in, D, 32)
            along = jnp.mean(scaled, axis=1, keepdims=True)
            across_ = jnp.mean(scaled * xhat, axis=1, keepdims=True)
            cot = k.C[rows, :].astype(f32)
            back = scale * (scaled - along - xhat * across_) + cot
            k.IT[rows, :] = back.astype(bf16)
            for offset, term in ((d.o_gain_in, grad * xhat), (d.o_shift_in, grad), (d.o_bias_down, cot)):
                k.SG[:, offset : offset + D] = k.SG[:, offset : offset + D] + fold_rows(term)

        loop(T // 32, body)

    back = []
    for number, (source, target) in enumerate(((k.OT, k.out), (k.IT, k.ig))):
        for g in range(4):
            back.append((source.at[g * blk : (g + 1) * blk, :], target.at[3 * y + c], g, number * 6 + g))
        for half in range(2):
            back.append(
                (
                    source.at[S + half * blk : S + (half + 1) * blk, :],
                    target.at[3 * y + 2],
                    2 * c + half,
                    number * 6 + 4 + half,
                )
            )

    def back_slot(i):
        number, which = i // 6, i % 6
        return number * 6 + (b if which < 4 else 4 + y)

    def start_back(number):
        for src, dst, g, i in back[number * 6 : number * 6 + 6]:

            @pl.when(g == b)
            def _():
                pltpu.make_async_copy(src, dst, k.back_recv.at[back_slot(i)]).start()

            @pl.when(g != b)
            def _():
                pltpu.make_async_remote_copy(
                    src_ref=src,
                    dst_ref=dst,
                    send_sem=k.back_send.at[i],
                    recv_sem=k.back_recv.at[back_slot(i)],
                    device_id=blk_of(g),
                    device_id_type=MESH,
                ).start()

    def finish_back():
        for number, (source, target) in enumerate(((k.OT, k.out), (k.IT, k.ig))):
            for g in range(4):
                row = (g // 2) * 3 + g % 2
                pltpu.make_async_copy(
                    source.at[0:blk, :], target.at[row], k.back_recv.at[number * 6 + g]
                ).wait()
            for half in range(2):
                pltpu.make_async_copy(
                    source.at[0:blk, :], target.at[half * 3 + 2], k.back_recv.at[number * 6 + 4 + half]
                ).wait()
        for src, dst, g, i in back:

            @pl.when(g != b)
            def _():
                pltpu.make_async_remote_copy(
                    src_ref=src,
                    dst_ref=dst,
                    send_sem=k.back_send.at[i],
                    recv_sem=k.back_recv.at[i],
                    device_id=blk_of(g),
                    device_id_type=MESH,
                ).wait_send()

    class Reduce:
        def __init__(self, name, part, first, width, s):
            self.part, self.first, self.width, self.s = part, first, width, s
            self.half, self.quarter = width // 2, width // 4
            self.core, self.y = getattr(k, name + "_core"), getattr(k, name + "_y")
            self.x, self.z = getattr(k, name + "_x"), getattr(k, name + "_z")
            self.sum, self.low = getattr(k, name + "_sum"), getattr(k, name + "_low")
            self.total = part.shape[0]

        def cols(self, start, size):
            return pl.ds(pl.multiple_of(self.first + start, size), size)

        def start(self):
            half = self.half
            self.c1 = comm.start(self.part.at[:, self.cols((1 - c) * half, half)], self.core, sibling)

        def step_y(self):
            half, quarter = self.half, self.quarter
            self.c1.wait_recv()

            def body(i):
                rows = span(i * 64, 64)
                mine = self.part[rows, self.cols(c * half, half)]
                value = self.core[rows, :].astype(f32) + mine.astype(f32)
                self.core[rows, :] = value.astype(bf16)

            loop(self.total // 64, body)
            self.c2 = comm.start(
                self.core.at[:, pl.ds(pl.multiple_of((1 - y) * quarter, quarter), quarter)], self.y, across
            )

        def step_x(self):
            quarter, s = self.quarter, self.s
            self.c2.wait_recv()
            mine = pl.ds(pl.multiple_of(y * quarter, quarter), quarter)
            unit = math.lcm(s, 16)

            def body(i):
                rows = span(i * unit, unit)
                value = self.core[rows, mine].astype(f32) + self.y[rows, :].astype(f32)
                for j in range(unit // s):
                    owner = i * (unit // s) + j
                    part = value[j * s : (j + 1) * s]
                    self.x[owner // d.minor, lax.rem(owner, d.minor)] = part.astype(self.x.dtype)

            loop(self.total // unit, body)
            self.c3 = []
            for dx in range(1, d.minor):
                self.c3.append(
                    comm.start(self.x.at[:, lax.rem(xi + dx, d.minor)], self.z.at[dx - 1], at_x(dx))
                )

        def step_z(self):
            for copy in self.c3:
                copy.wait_recv()

            def body(i):
                value = self.x[i, xi].astype(f32)
                for dx in range(1, d.minor):
                    value = value + self.z[dx - 1, i].astype(f32)
                self.sum[i] = value.astype(self.sum.dtype)

            loop(d.major, body)
            self.c4 = []
            for dz in range(1, d.major):
                self.c4.append(
                    comm.start(
                        self.sum.at[lax.rem(zi + dz, d.major)], self.sum.at[d.major + dz - 1], at_z(dz)
                    )
                )

        def step_last(self):
            quarter, s = self.quarter, self.s
            for copy in self.c4:
                copy.wait_recv()
            value = self.sum[zi].astype(f32)
            for dz in range(1, d.major):
                value = value + self.sum[d.major + dz - 1].astype(f32)
            low = value.astype(self.low.dtype)
            self.low[b] = low
            self.c5 = comm.start(self.low.at[b], self.low.at[b], across)
            self.c6 = comm.start(self.low.at[b], self.low.at[b], sibling)
            kept = low.astype(f32)
            return jnp.sum(fold_lanes(fold_rows(kept * kept)))

        def step_share(self):
            self.c5.wait_recv()
            other = 2 * (1 - y) + c
            self.c7 = comm.start(self.low.at[other], self.low.at[other], sibling)

        def end(self):
            self.c6.wait_recv()
            self.c7.wait_recv()

    red = {
        "down": Reduce("down", k.PD, 0, D, d.sd),
        "up_content": Reduce("upc", k.PU, 0, G, d.su),
        "spatial": Reduce("sp", k.PS, 0, S, d.ss),
        "up_gate": Reduce("upg", k.PU, G, G, d.su),
    }
    rs = list(red.values())

    for group in groups:
        forward_minor(group)
        forward_core(group)
        arrived(group)
        if d.wide:
            to_low(group)
    wait_tokens(0)
    input_norm()
    make_labels()
    up_gate()
    gate_norm(S, H, S + c * H)
    mine = k.GATE.at[span(S + c * H, H), :]
    gate_copy = comm.start(mine, mine, sibling)
    gate_norm(0, S, 0)
    make_mixing()
    up_content()
    wait_tokens(1)
    gate_copy.wait_recv()
    mix()
    gate_gradient = grad_gate_shared()
    grad_down()
    red["down"].start()
    project()
    start_back(0)
    grad_up(0)
    red["up_content"].start()
    grad_spatial_weight()
    red["spatial"].start()
    gate_back(gate_gradient)
    grad_up(G)
    red["up_gate"].start()
    for one in rs:
        one.step_y()
    grad_input()
    start_back(1)

    def column_sums():
        bias = jnp.sum(jnp.transpose(k.BSA[...]), axis=0, keepdims=True)
        k.SG[:, d.o_bias_spatial : d.o_bias_spatial + S] = jnp.zeros((8, S), f32)
        k.SG[0:1, d.o_bias_spatial : d.o_bias_spatial + S] = bias[:, 0:S]
        place = pl.ds(pl.multiple_of(d.o_bias_spatial + c * H, H), H)
        k.SG[0:1, place] = k.SG[0:1, place] + bias[:, S:T]
        for i in range(d.nsmall // LANES):
            total = jnp.sum(k.SG[:, i * LANES : (i + 1) * LANES], axis=0, keepdims=True)
            k.small_part[i : i + 1, :] = total

    column_sums()
    quarter = d.nsmall // LANES // 4
    first = []
    for db in range(1, 4):
        other = lax.rem(b + db, 4)
        first.append(
            comm.start(k.small_part.at[span(other * quarter, quarter), :], k.small_one.at[db - 1], (r, other))
        )
    for one in rs:
        one.step_x()
    for copy in first:
        copy.wait_recv()
    value = k.small_part[span(b * quarter, quarter), :]
    for i in range(3):
        value = value + k.small_one[i]
    k.small_two[0] = value
    second = []
    for dr in range(1, d.R):
        second.append(comm.start(k.small_two.at[0], k.small_two.at[dr], (lax.rem(r + dr, d.R), b)))
    for one in rs:
        one.step_z()
    for copy in second:
        copy.wait_recv()
    value = k.small_two[0]
    for dr in range(1, d.R):
        value = value + k.small_two[dr]
    k.gsmall[span(b * quarter, quarter), :] = value
    squares = jnp.sum(fold_rows(value * value))
    third = []
    mine = k.gsmall.at[span(b * quarter, quarter), :]
    for db in range(1, 4):
        third.append(comm.start(mine, mine, (r, lax.rem(b + db, 4))))

    parts = [one.step_last() for one in rs]
    k.norm_rows[0] = jnp.full((8, LANES), parts[0] + parts[1] + parts[2] + parts[3], f32)
    norm_one = []
    for dr in range(1, d.R):
        norm_one.append(comm.start(k.norm_rows.at[0], k.norm_rows.at[dr], (lax.rem(r + dr, d.R), b)))
    for one in rs:
        one.step_share()
    for copy in norm_one:
        copy.wait_recv()
    value = jnp.full((8, LANES), squares, f32)
    for i in range(d.R):
        value = value + k.norm_rows[lax.rem(i - r + 2 * d.R, d.R)]
    k.norm_blk[b] = value
    norm_two = []
    for db in range(1, 4):
        norm_two.append(comm.start(k.norm_blk.at[b], k.norm_blk.at[b], (r, lax.rem(b + db, 4))))
    for one in rs:
        one.end()
    for copy in third + norm_two:
        copy.wait_recv()
    value = k.norm_blk[0]
    for i in range(1, 4):
        value = value + k.norm_blk[i]
    k.norm[...] = jnp.sqrt(value)
    finish_back()
    finish_tokens()
    comm.finish()
    if count is not None:
        count.append(comm.next)


def adam_kernel(d, *refs):
    norm, gsmall, gup_c, gup_g, gdown, gsp = refs[:6]
    up, down, sp, small = refs[6:9], refs[9:12], refs[12:15], refs[15:18]
    outs = refs[18:]
    r = lax.axis_index("rows")
    value = norm[...]
    factor = jnp.minimum(1.0, max_norm / (value + 1e-06))

    def step(ins, results, grad, rate, decay, place):
        weight, moment, square = (ref[place] for ref in ins)
        grad = grad * factor[0:1, 0:1]
        moment_next = beta_one * moment + (1.0 - beta_one) * grad
        square_next = beta_two * square + (1.0 - beta_two) * grad * grad
        moment_hat = moment_next / (1.0 - beta_one**STEP)
        square_hat = square_next / (1.0 - beta_two**STEP)
        update = moment_hat / (jnp.sqrt(square_hat) + 1e-08) + decay * weight
        for ref, result in zip(results, (weight - rate * update, moment_next, square_next)):
            ref[place] = result

    for q in range(4):
        y, c = q // 2, q % 2
        for s, low, first, ins, results in (
            (d.su, gup_c, 0, up, outs[0:3]),
            (d.su, gup_g, d.G, up, outs[0:3]),
            (d.sd, gdown, 0, down, outs[3:6]),
            (d.ss, gsp, 0, sp, outs[6:9]),
        ):
            width = low.shape[2]
            start = first + (2 * c + y) * width
            place = (slice(0, s), slice(start, start + width))
            step(ins, results, low[q].astype(f32), weight_rate, weight_decay, place)
    grad = gsmall[pl.ds(r * d.ks, d.ks), :]
    step(small, outs[9:12], grad, small_rate, 0.0, (slice(0, d.ks), slice(0, LANES)))


def body(mesh, *arrays):
    (
        inputs,
        cotangent,
        lengths,
        up_weight,
        up_moment,
        up_square,
        down_weight,
        down_moment,
        down_square,
        spatial_weight,
        spatial_moment,
        spatial_square,
        small_params,
        small_moment,
        small_square,
    ) = arrays
    d = plan_of(
        mesh,
        dict(
            inputs=inputs.shape,
            up=up_weight.shape,
            down=down_weight.shape,
            spatial=spatial_weight.shape,
            small=small_params.shape,
        ),
    )
    S, H, T, D, G, FF, R = d.S, d.H, d.T, d.D, d.G, d.FF, d.R
    wire = f32 if d.wide else bf16
    small_rows = d.nsmall // LANES
    quarter = small_rows // 4

    any_spec = pl.BlockSpec(memory_space=pl.ANY)
    vmem_spec = pl.BlockSpec(memory_space=VMEM)
    smem_spec = pl.BlockSpec(memory_space=pltpu.SMEM)

    ins = dict(
        x_in=(jnp.transpose(inputs, (1, 0, 2)), any_spec),
        c_in=(jnp.transpose(cotangent, (1, 0, 2)), any_spec),
        lengths=(lengths, smem_spec),
        up_w=(up_weight, any_spec),
        down_w=(down_weight, any_spec),
        sp_w=(spatial_weight, any_spec),
        small_w=(small_params.reshape(d.ks, LANES), any_spec),
    )
    outs = dict(
        out=((d.rows_here, d.block, D), bf16, any_spec),
        ig=((d.rows_here, d.block, D), bf16, any_spec),
        norm=((8, LANES), f32, vmem_spec),
        gsmall=((small_rows, LANES), f32, vmem_spec),
        upc_low=((4, d.su, G // 4), wire, vmem_spec),
        upg_low=((4, d.su, G // 4), wire, vmem_spec),
        down_low=((4, d.sd, D // 4), wire, vmem_spec),
        sp_low=((4, d.ss, S // 4), wire, vmem_spec),
    )
    if d.wide:
        outs["up_get"] = ((D, FF), f32, any_spec)
        outs["sp_get"] = ((S, S), f32, any_spec)
        outs["down_get"] = ((G, D), f32, any_spec)
    scratch = dict(
        up_stage=VMEM((d.su, FF), f32),
        down_stage=VMEM((d.sd, D), f32),
        sp_stage=VMEM((d.ss, S), f32),
        small_stage=VMEM((d.ks, LANES), f32),
        small_get=VMEM((R, 8, LANES), f32),
        SM=VMEM((8, d.nsmall), f32),
        SG=VMEM((8, d.nsmall), f32),
        UP=VMEM((D, FF), bf16),
        DOWN=VMEM((G, D), bf16),
        SP=VMEM((S, S), bf16),
        X=VMEM((T, D), bf16),
        C=VMEM((T, D), bf16),
        N=VMEM((T, D), bf16),
        NT=VMEM((D, T), bf16),
        F=VMEM((T, G), f32),
        FA=VMEM((T, 512), f32),
        FB=VMEM((T, 512), f32),
        DG=VMEM((T, G), bf16),
        XH=VMEM((T, G), bf16),
        RG=VMEM((T, LANES), f32),
        GATE=VMEM((2 * S, G), bf16),
        CT=VMEM((T, G), bf16),
        DC=VMEM((T, G), bf16),
        PR=VMEM((T, G), bf16),
        GS=VMEM((T, G), bf16),
        GB=VMEM((T, FF), bf16),
        GX=VMEM((H, G), bf16),
        GY=VMEM((H, G), bf16),
        BS=VMEM((T, LANES), f32),
        BSA=VMEM((T, LANES), f32),
        M=VMEM((T, S), bf16),
        MT=VMEM((S, S), bf16),
        MTB=VMEM((S, H), bf16),
        row_t=VMEM((2, 8, S), f32),
        row_s=VMEM((2, 8, S), f32),
        col_t=VMEM((2, S, LANES), f32),
        col_s=VMEM((2, S, LANES), f32),
        OT=VMEM((T, D), bf16),
        IT=VMEM((T, D), bf16),
        PU=VMEM((D, FF), bf16),
        PD=VMEM((G, D), bf16),
        PS=VMEM((S, S), bf16),
        small_part=VMEM((small_rows, LANES), f32),
        small_one=VMEM((3, quarter, LANES), f32),
        small_two=VMEM((R, quarter, LANES), f32),
        norm_rows=VMEM((R, 8, LANES), f32),
        norm_blk=VMEM((4, 8, LANES), f32),
    )
    for name, total, width, s in (
        ("down", G, D, d.sd),
        ("upc", D, G, d.su),
        ("upg", D, G, d.su),
        ("sp", S, S, d.ss),
    ):
        scratch[name + "_core"] = VMEM((total, width // 2), bf16)
        scratch[name + "_y"] = VMEM((total, width // 4), bf16)
        scratch[name + "_x"] = VMEM((d.major, d.minor, s, width // 4), wire)
        scratch[name + "_z"] = VMEM((max(d.minor - 1, 1), d.major, s, width // 4), wire)
        scratch[name + "_sum"] = VMEM((2 * d.major - 1, s, width // 4), wire)
    copies = (
        2 * (R - 1)
        + 4 * (d.major - 1 + d.major * (d.minor - 1) + R - 1)
        + 2
        + 4 * (1 + 1 + d.minor - 1 + d.major - 1 + 3)
        + 3
        + R
        - 1
        + 3
        + 3
    )
    scratch["send_sem"] = pltpu.SemaphoreType.DMA((copies,))
    scratch["recv_sem"] = pltpu.SemaphoreType.DMA((copies,))
    scratch["token_send"] = pltpu.SemaphoreType.DMA((12,))
    scratch["token_recv"] = pltpu.SemaphoreType.DMA((12,))
    scratch["back_send"] = pltpu.SemaphoreType.DMA((12,))
    scratch["back_recv"] = pltpu.SemaphoreType.DMA((12,))
    scratch["local_sem"] = pltpu.SemaphoreType.DMA((4,))

    names = list(ins) + list(outs) + list(scratch)

    def kernel(*refs):
        refs = list(refs)
        have = dict(zip(names, refs))
        if not d.wide:
            have["up_get"], have["sp_get"], have["down_get"] = have["UP"], have["SP"], have["DOWN"]
        main_kernel(d, list(have), None, *have.values())

    results = pl.pallas_call(
        kernel,
        out_shape=[jax.ShapeDtypeStruct(shape, dtype) for shape, dtype, _ in outs.values()],
        in_specs=[spec for _, spec in ins.values()],
        out_specs=[spec for _, _, spec in outs.values()],
        scratch_shapes=list(scratch.values()),
        compiler_params=pltpu.CompilerParams(
            collective_id=0, has_side_effects=True, vmem_limit_bytes=63 * 1024 * 1024
        ),
        name="block_step",
    )(*[array for array, _ in ins.values()])
    got = dict(zip(outs, results))

    params = [
        up_weight,
        up_moment,
        up_square,
        down_weight,
        down_moment,
        down_square,
        spatial_weight,
        spatial_moment,
        spatial_square,
        small_params.reshape(d.ks, LANES),
        small_moment.reshape(d.ks, LANES),
        small_square.reshape(d.ks, LANES),
    ]
    updated = pl.pallas_call(
        functools.partial(adam_kernel, d),
        out_shape=[jax.ShapeDtypeStruct(p.shape, f32) for p in params],
        in_specs=[vmem_spec] * (6 + len(params)),
        out_specs=[vmem_spec] * len(params),
        compiler_params=pltpu.CompilerParams(vmem_limit_bytes=32 * 1024 * 1024),
        name="adam_step",
    )(got["norm"], got["gsmall"], got["upc_low"], got["upg_low"], got["down_low"], got["sp_low"], *params)
    updated = list(updated[:9]) + [p.reshape(-1) for p in updated[9:]]
    return (
        jnp.transpose(got["out"], (1, 0, 2)),
        jnp.transpose(got["ig"], (1, 0, 2)),
        got["norm"][0, 0],
        *updated,
    )


def solution(mesh):
    rows = P("rows", None)
    flat = P("rows")
    tokens = P("blk", "rows", None)
    return jax.shard_map(
        functools.partial(body, mesh),
        mesh=mesh,
        in_specs=(tokens, tokens, rows) + (rows,) * 9 + (flat,) * 3,
        out_specs=(tokens, tokens, P()) + (rows,) * 9 + (flat,) * 3,
        check_vma=False,
    )
```

```python
import functools
import math
import types

import jax
import jax.numpy as jnp
from jax import lax
from jax.experimental import pallas as pl
from jax.experimental.pallas import tpu as pltpu
from jax.sharding import PartitionSpec as P

STEP = 10

beta_one = 0.9
beta_two = 0.999
max_norm = 1.0
weight_rate = 0.05
small_rate = 0.5
weight_decay = 0.01

MESH = pl.DeviceIdType.MESH
VMEM = pltpu.VMEM
bf16 = jnp.bfloat16
f32 = jnp.float32
LANES = 128


def loop(count, body):
    def step(i, carry):
        body(i)
        return carry

    lax.fori_loop(0, count, step, 0)


def span(start, size):
    return pl.ds(pl.multiple_of(start, size), size)


def rows_of(value, count):
    return jnp.concatenate([value] * (count // value.shape[0]), axis=0)


def lanes_of(value, count):
    return jnp.concatenate([value] * (count // value.shape[1]), axis=1)


def fold_rows(value):
    total = value[0:8]
    for first in range(8, value.shape[0], 8):
        total = total + value[first : first + 8]
    return total


def fold_lanes(value):
    total = value[:, 0:LANES]
    for first in range(LANES, value.shape[1], LANES):
        total = total + value[:, first : first + LANES]
    return total


def dot_nn(a, b):
    return lax.dot_general(a, b, (((1,), (0,)), ((), ())), preferred_element_type=f32)


def dot_nt(a, b):
    return lax.dot_general(a, b, (((1,), (1,)), ((), ())), preferred_element_type=f32)


def dot_tn(a, b):
    return lax.dot_general(a, b, (((0,), (0,)), ((), ())), preferred_element_type=f32)


def plan_of(mesh, shapes):
    d = types.SimpleNamespace()
    d.R = mesh.shape["rows"]
    d.minor = 1
    while d.minor * d.minor * 2 <= d.R:
        d.minor *= 2
    if d.minor * d.minor > d.R:
        d.minor //= 2
    d.major = d.R // d.minor
    d.block, d.rows_here, d.D = shapes["inputs"]
    d.S = d.block * mesh.shape["blk"]
    d.H = d.S // 2
    d.T = d.S + d.H
    d.FF = shapes["up"][1]
    d.G = d.FF // 2
    d.su, d.sd, d.ss = shapes["up"][0], shapes["down"][0], shapes["spatial"][0]
    d.ks = shapes["small"][0] // LANES
    d.nsmall = d.ks * d.R * LANES
    d.pair = 1
    while any(size * d.pair % 16 for size in (d.su, d.sd, d.ss)):
        d.pair *= 2
    d.minor = d.minor // d.pair
    d.pu, d.pd, d.ps = (size * d.pair for size in (d.su, d.sd, d.ss))
    d.CH = 512 if d.G % 512 == 0 else d.G
    d.chunks = d.G // d.CH
    d.split = d.R <= 16
    d.o_gain_in = 0
    d.o_shift_in = d.D
    d.o_bias_up = 2 * d.D
    d.o_gain_gate = d.o_bias_up + d.FF
    d.o_shift_gate = d.o_gain_gate + d.G
    d.o_bias_spatial = d.o_shift_gate + d.G
    d.o_bias_down = d.o_bias_spatial + d.S
    return d


class Comm:
    def __init__(self, send, recv):
        self.send, self.recv, self.next = send, recv, 0
        self.open = []

    def copy(self, src, dst, device):
        i = self.next
        self.next += 1
        made = pltpu.make_async_remote_copy(
            src_ref=src,
            dst_ref=dst,
            send_sem=self.send.at[i],
            recv_sem=self.recv.at[i],
            device_id=device,
            device_id_type=MESH,
        )
        return made

    def start(self, src, dst, device):
        made = self.copy(src, dst, device)
        made.start()
        self.open.append(made)
        return made

    def finish(self):
        for made in self.open:
            made.wait_send()
        self.open = []


class Gather:
    def __init__(self, net, ref, s, first, width, by_y, fill):
        self.net, self.ref, self.s, self.first = net, ref, s, first
        self.half, self.by_y, self.fill = width // 2, by_y, fill
        self.size = self.half // 2 if by_y else self.half
        self.z, self.x, self.y, self.core = {}, {}, {}, []

    def region(self, owner, of_y=None):
        start = self.first + self.net.c * self.half
        if self.by_y:
            start = start + (self.net.y if of_y is None else of_y) * self.size
        cols = pl.ds(pl.multiple_of(start, LANES), self.size)
        return self.ref.at[span(owner * self.s, self.s), cols]

    def owner(self, dz, dx):
        n = self.net
        return lax.rem(n.zi - dz + n.major, n.major) * n.minor + lax.rem(n.xi - dx + n.minor, n.minor)

    def begin(self):
        self.fill()
        mine = self.region(self.net.zi * self.net.minor + self.net.xi)
        for dz in range(1, self.net.major):
            self.z[dz] = self.net.comm.start(mine, mine, self.net.at_z(dz))

    def onward(self, piece, dz, dx):
        start = self.net.comm.start
        if self.by_y:
            self.y[dz, dx] = start(piece, piece, self.net.across)
        self.core.append(start(piece, piece, self.net.sibling))

    def minor(self):
        n = self.net
        for dz in range(n.major):
            piece = self.region(self.owner(dz, 0))
            if dz:
                self.z[dz].wait_recv()
            for dx in range(1, n.minor):
                self.x[dz, dx] = n.comm.start(piece, piece, n.at_x(dx))
            if dz:
                self.onward(piece, dz, 0)

    def last(self):
        n = self.net
        for dz in range(n.major):
            for dx in range(1, n.minor):
                self.x[dz, dx].wait_recv()
                self.onward(self.region(self.owner(dz, dx)), dz, dx)

    def swap(self):
        n = self.net
        for (dz, dx), copy in self.y.items():
            copy.wait_recv()
            piece = self.region(self.owner(dz, dx), 1 - n.y)
            self.core.append(n.comm.start(piece, piece, n.sibling))

    def end(self):
        for copy in self.core:
            copy.wait_recv()


class Reduce:
    def __init__(self, net, part, first, width, s, route, bufs, low):
        self.net, self.part, self.first, self.s, self.route = net, part, first, s, route
        self.half, self.quarter = width // 2, width // 4
        self.core, self.bufs, self.low = bufs[0], bufs[1:], low
        self.step = 0

    def cols(self, start, size):
        return pl.ds(pl.multiple_of(self.first + start, LANES), size)

    def start(self):
        n, half = self.net, self.half
        src = self.part.at[:, :, :, self.cols((1 - n.c) * half, half)]
        self.waits = [n.comm.start(src, self.core, n.sibling)]

    def advance(self):
        n = self.net
        for copy in self.waits:
            copy.wait_recv()
        if self.step == 0:
            mine = self.cols(n.c * self.half, self.half)
            self.zs, self.xs, self.width = n.major, n.minor, self.half

            def add(i, j):
                value = self.part[i, j, :, mine].astype(f32) + self.core[i, j].astype(f32)
                self.core[i, j] = value.astype(self.core.dtype)

            self.blocks(add)
            self.now = self.core
        else:
            kept, got = self.kept, self.got
            made = self.bufs[2 * self.step - 1]

            def add(i, j):
                value = kept(i, j).astype(f32)
                for ref in got:
                    value = value + ref[i, j].astype(f32)
                made[i, j] = value.astype(made.dtype)

            self.blocks(add)
            self.now = made
        if self.step == len(self.route):
            return self.share()
        axis = self.route[self.step]
        now, into = self.now, self.bufs[2 * self.step]
        self.step += 1
        if axis == "x":
            self.waits = [
                n.comm.start(now.at[:, pl.ds(lax.rem(n.xi + dx, n.minor), 1)], into.at[dx - 1], n.at_x(dx))
                for dx in range(1, n.minor)
            ]
            self.got = [into.at[dx - 1] for dx in range(1, n.minor)]
            self.kept = lambda i, j: now[i, n.xi]
            self.xs = 1
        elif axis == "z":
            self.waits = [
                n.comm.start(now.at[pl.ds(lax.rem(n.zi + dz, n.major), 1)], into.at[dz - 1], n.at_z(dz))
                for dz in range(1, n.major)
            ]
            self.got = [into.at[dz - 1] for dz in range(1, n.major)]
            self.kept = lambda i, j: now[n.zi, j]
            self.zs = 1
        elif axis == "p":
            self.waits = [n.comm.start(now, into.at[dp - 1], n.at_pair(dp)) for dp in range(1, n.pair)]
            self.got = [into.at[dp - 1] for dp in range(1, n.pair)]
            self.kept = lambda i, j: now[i, j]
        else:
            width = self.width // 2
            theirs = pl.ds(pl.multiple_of((1 - n.y) * width, LANES), width)
            mine = pl.ds(pl.multiple_of(n.y * width, LANES), width)
            self.waits = [n.comm.start(now.at[:, :, :, theirs], into.at[0], n.across)]
            self.got = [into.at[0]]
            self.kept = lambda i, j: now[i, j, :, mine]
            self.width = width

    def blocks(self, add):
        zs, xs = self.zs, self.xs
        if zs * xs == 1:
            add(0, 0)
        else:
            loop(zs * xs, lambda i: add(i // xs, lax.rem(i, xs)))

    def share(self):
        n, mine = self.net, self.now.at[0, 0]
        self.local = pltpu.make_async_copy(mine, self.low.at[n.b], n.local_sem())
        self.local.start()
        self.waits = [n.comm.start(mine, self.low.at[n.b], (n.r, lax.rem(n.b + db, 4))) for db in range(1, 4)]
        kept = self.now[0, 0].astype(f32)
        return jnp.sum(fold_lanes(fold_rows(kept * kept)))

    def end(self):
        self.local.wait()
        for copy in self.waits:
            copy.wait_recv()


def reduce_shapes(d, width, s, route):
    zs, xs, wide = d.major, d.minor, width // 2
    shapes = [(zs, xs, s, wide)]
    for axis in route:
        if axis == "x":
            count, xs = max(d.minor - 1, 1), 1
        elif axis == "z":
            count, zs = max(d.major - 1, 1), 1
        elif axis == "p":
            count = d.pair - 1
        else:
            count, wide = 1, wide // 2
        shapes.append((count, zs, xs, s, wide))
        shapes.append((zs, xs, s, wide))
    return shapes


def main_kernel(d, names, *refs):
    k = types.SimpleNamespace(**dict(zip(names, refs)))
    comm = Comm(k.send_sem, k.recv_sem)
    r, b = lax.axis_index("rows"), lax.axis_index("blk")
    line = d.minor * d.pair
    zi, xi, xp = r // line, lax.rem(r, line) // d.pair, lax.rem(r, d.pair)
    y, c = b // 2, lax.rem(b, 2)
    S, H, T, D, G, FF, CH = d.S, d.H, d.T, d.D, d.G, d.FF, d.CH
    blk = d.block
    sibling = (r, 2 * y + 1 - c)
    across = (r, 2 * (1 - y) + c)

    def at_z(dz):
        return (lax.rem(zi + dz, d.major) * line + xi * d.pair + xp, b)

    def at_x(dx):
        return (zi * line + lax.rem(xi + dx, d.minor) * d.pair + xp, b)

    def at_pair(dp):
        return (zi * line + xi * d.pair + lax.rem(xp + dp, d.pair), b)

    used = [0]

    def local_sem():
        used[0] += 1
        return k.local_sem.at[used[0] - 1]

    net = types.SimpleNamespace(
        comm=comm, r=r, b=b, zi=zi, xi=xi, y=y, c=c, major=d.major, minor=d.minor,
        sibling=sibling, across=across, at_z=at_z, at_x=at_x, at_pair=at_pair, pair=d.pair, local_sem=local_sem,
    )

    barrier = pltpu.get_barrier_semaphore()
    for dr in range(1, d.R):
        pl.semaphore_signal(barrier, inc=1, device_id=(lax.rem(r + dr, d.R), b), device_id_type=MESH)
    for db in range(1, 4):
        pl.semaphore_signal(barrier, inc=1, device_id=(r, lax.rem(b + db, 4)), device_id_type=MESH)

    own = {}
    for name, rows in (("small", d.ks), ("up", d.su), ("sp", d.ss), ("down", d.sd)):
        stage = getattr(k, name + "_stage")
        if name != "small":
            stage = stage.at[span(xp * rows, rows)]
        own[name] = pltpu.make_async_copy(getattr(k, name + "_w"), stage, local_sem())
        own[name].start()

    def staged(name):
        own[name].wait()

    def share_pair():
        made = []
        for name, rows in (("up", d.su), ("sp", d.ss), ("down", d.sd)):
            mine = getattr(k, name + "_stage").at[span(xp * rows, rows)]
            made += [comm.start(mine, mine, at_pair(dp)) for dp in range(1, d.pair)]
        for copy in made:
            copy.wait_recv()

    def gather(name, ref, s, first, width, by_y):
        stage = getattr(k, name + "_stage")

        def fill():
            cols = slice(first, first + width)
            ref[span((zi * d.minor + xi) * s, s), cols] = stage[:, cols].astype(bf16)

        return Gather(net, ref, s, first, width, by_y, fill)

    step = CH if d.split else G
    flow = [gather("up", k.UP, d.pu, G + j, step, False) for j in range(0, G, step)]
    flow += [gather("up", k.UP, d.pu, j, step, False) for j in range(0, G, step)]
    flow += [gather("sp", k.SP, d.ps, 0, S, False), gather("down", k.DOWN, d.pd, 0, D, True)]
    per = G // step

    def blk_of(g):
        return (r, g)

    tokens = []
    for number, (source, target) in enumerate(((k.x_in, k.X), (k.c_in, k.C))):
        for g in range(4):
            row = (g // 2) * 3 + g % 2
            tokens.append((source.at[row], target.at[span(b * blk, blk), :], g, number * 6 + g, number * 6 + b))
        for half in range(2):
            row, i = half * 3 + 2, number * 6 + 4
            tokens.append((source.at[row], target.at[span(S + c * blk, blk), :], 2 * half + y, i + half, i + c))

    def token_copy(src, dst, g, i, slot):
        return pltpu.make_async_remote_copy(
            src_ref=src,
            dst_ref=dst,
            send_sem=k.token_send.at[i],
            recv_sem=k.token_recv.at[slot],
            device_id=blk_of(g),
            device_id_type=MESH,
        )

    def start_tokens(number):
        for src, dst, g, i, slot in tokens[number * 6 : number * 6 + 6]:

            @pl.when(g == b)
            def _():
                pltpu.make_async_copy(src, dst, k.token_recv.at[slot]).start()

            @pl.when(g != b)
            def _():
                token_copy(src, dst, g, i, slot).start()

    def wait_tokens(number):
        target = (k.X, k.C)[number]
        for g in range(4):
            here = target.at[g * blk : (g + 1) * blk, :]
            pltpu.make_async_copy(k.x_in.at[0], here, k.token_recv.at[number * 6 + g]).wait()
        for j in range(2):
            here = target.at[S + j * blk : S + (j + 1) * blk, :]
            pltpu.make_async_copy(k.x_in.at[0], here, k.token_recv.at[number * 6 + 4 + j]).wait()

    def finish_tokens():
        for src, dst, g, i, slot in tokens:

            @pl.when(g != b)
            def _():
                token_copy(src, dst, g, i, slot).wait_send()

    small_copies = []

    def send_small():
        k.small_get[r] = jnp.zeros((8, LANES), f32)
        k.small_get[r, 0 : d.ks, :] = k.small_stage[...].astype(bf16).astype(f32)
        for dr in range(1, d.R):
            mine = k.small_get.at[r]
            small_copies.append(comm.start(mine, mine, (lax.rem(r + dr, d.R), b)))

    def take_small():
        for copy in small_copies:
            copy.wait_recv()
        for i in range(d.R):
            for j in range(d.ks):
                first = (i * d.ks + j) * LANES
                k.SM[:, first : first + LANES] = jnp.broadcast_to(k.small_get[i, j : j + 1, :], (8, LANES))

    def small(offset, width, rows):
        return rows_of(k.SM[:, offset : offset + width], rows)

    def label_of(places, ends, source):
        label = jnp.zeros(places.shape, f32)
        for end in ends:
            label = label + jnp.where(places >= end, 1.0, 0.0)
        if source:
            label = jnp.where(places < ends[-1], label, -1.0)
        return label

    def make_labels():
        for which, row in enumerate((3 * y + c, 3 * y + 2)):
            ends = [k.lengths[0, row]]
            for n in range(1, k.lengths.shape[0]):
                ends.append(ends[-1] + k.lengths[n, row])
            lane = lax.broadcasted_iota(jnp.int32, (8, S), 1)
            k.row_t[which] = label_of(lane, ends, False)
            k.row_s[which] = label_of(lane, ends, True)
            for first in range(0, S, 64):
                place = lax.broadcasted_iota(jnp.int32, (64, LANES), 0) + first
                k.col_t[which, first : first + 64, :] = label_of(place, ends, False)
                k.col_s[which, first : first + 64, :] = label_of(place, ends, True)

    def make_mixing():
        k.FA[0:S, :] = k.SP[...].astype(f32)
        k.FB[0:S, :] = jnp.transpose(k.FA[0:S, :])

        def body(i):
            rows = span(i * 32, 32)
            keep = lanes_of(k.col_t[0, rows, :], S) == rows_of(k.row_s[0], 32)
            k.M[rows, :] = jnp.where(keep, k.FA[rows, :], 0.0).astype(bf16)
            keep = lanes_of(k.col_s[0, rows, :], S) == rows_of(k.row_t[0], 32)
            k.MT[rows, :] = jnp.where(keep, k.FB[rows, :], 0.0).astype(bf16)

        loop(S // 32, body)

        def shared(i):
            rows = span(c * H + i * 32, 32)
            keep = lanes_of(k.col_t[1, rows, :], S) == rows_of(k.row_s[1], 32)
            k.M[span(S + i * 32, 32), :] = jnp.where(keep, k.FA[rows, :], 0.0).astype(bf16)

        loop(H // 32, shared)
        own_half = pl.ds(pl.multiple_of(c * H, H), H)

        def turned(i):
            rows = span(i * 32, 32)
            keep = lanes_of(k.col_s[1, rows, :], H) == rows_of(k.row_t[1, :, own_half], 32)
            k.MTB[rows, :] = jnp.where(keep, k.FB[rows, own_half], 0.0).astype(bf16)

        loop(S // 32, turned)
        bias = k.SM[:, d.o_bias_spatial : d.o_bias_spatial + S]
        k.BS[0:S, :] = jnp.transpose(rows_of(bias, LANES))
        k.BS[S:T, :] = k.BS[span(c * H, H), :]

    def row_mean(ref, first, count, width, finish):
        def body(i):
            rows = span(first + i * 128, 128)
            total = jnp.sum(ref[rows, :], axis=1, keepdims=True) * (1.0 / width)
            ref[rows, :] = jnp.broadcast_to(finish(total), (128, LANES))

        loop(count // 128, body)

    def scale_of(spread):
        return lax.rsqrt(spread + 1e-05)

    def input_norm():
        def sums(i):
            rows = span(i * 32, 32)
            k.MU[rows, :] = fold_lanes(k.X[rows, :].astype(f32))

        loop(T // 32, sums)
        row_mean(k.MU, 0, T, D, lambda v: v)

        def spreads(i):
            rows = span(i * 32, 32)
            centred = k.X[rows, :].astype(f32) - lanes_of(k.MU[rows, :], D)
            k.RX[rows, :] = fold_lanes(centred * centred)

        loop(T // 32, spreads)
        row_mean(k.RX, 0, T, D, scale_of)

        def body(i):
            rows = span(i * 32, 32)
            centred = k.X[rows, :].astype(f32) - lanes_of(k.MU[rows, :], D)
            normed = centred * lanes_of(k.RX[rows, :], D)
            normed = normed * small(d.o_gain_in, D, 32) + small(d.o_shift_in, D, 32)
            k.N[rows, :] = normed.astype(bf16)

        loop(T // 32, body)

    def turn_normed():
        k.NT[...] = jnp.transpose(k.N[...].astype(f32)).astype(bf16)

    def gelu_parts(before):
        cdf = 0.5 + 0.5 * lax.erf(before * 0.7071067811865476)
        bell = jnp.exp(before * before * -0.5)
        return before * cdf, cdf + before * bell * 0.3989422804014327

    def up_gate(j):
        cols = slice(j * CH, (j + 1) * CH)
        at = G + j * CH
        k.F[:, cols] = dot_nn(k.N[...], k.UP[:, at : at + CH])
        bias = small(d.o_bias_up + at, CH, 16)
        for first in range(0, T, 16):
            rows = slice(first, first + 16)
            active, slope = gelu_parts(k.F[rows, cols] + bias)
            k.F[rows, cols] = active
            k.DG[rows, cols] = slope.astype(bf16)
            total = fold_lanes(active)
            k.S1[rows, :] = total if j == 0 else k.S1[rows, :] + total

    def gate_norm(first_row, count, place):
        row_mean(k.S1, first_row, count, G, lambda v: v)

        def spreads(i):
            rows = span(first_row + i * 16, 16)
            centred = k.F[rows, :] - lanes_of(k.S1[rows, :], G)
            k.RG[rows, :] = fold_lanes(centred * centred)

        loop(count // 16, spreads)
        row_mean(k.RG, first_row, count, G, scale_of)

        def body(i):
            rows = span(first_row + i * 16, 16)
            xhat = (k.F[rows, :] - lanes_of(k.S1[rows, :], G)) * lanes_of(k.RG[rows, :], G)
            k.XH[rows, :] = xhat.astype(bf16)
            gate = xhat * small(d.o_gain_gate, G, 16) + small(d.o_shift_gate, G, 16)
            k.GATE[span(place + i * 16, 16), :] = gate.astype(bf16)

        loop(count // 16, body)

    def up_content(j):
        cols = slice(j * CH, (j + 1) * CH)
        k.FA[...] = dot_nn(k.N[...], k.UP[:, cols])
        bias = small(d.o_bias_up + j * CH, CH, 16)
        for first in range(0, T, 16):
            rows = slice(first, first + 16)
            active, slope = gelu_parts(k.FA[rows, :] + bias)
            k.CT[rows, cols] = active.astype(bf16)
            k.DC[rows, cols] = slope.astype(bf16)

    def mix(j):
        cols = slice(j * CH, (j + 1) * CH)
        k.FA[0:S, :] = dot_nn(k.M[0:S, :], k.GATE[0:S, cols])
        k.FA[S:T, :] = dot_nn(k.M[S:T, :], k.GATE[S : 2 * S, cols])
        k.FB[...] = dot_nt(k.C[...], k.DOWN[cols, :])
        total = jnp.zeros((8, CH), f32)
        for first in range(0, T, 16):
            rows = slice(first, first + 16)
            out = k.FA[rows, :] + lanes_of(k.BS[rows, :], CH)
            grad = k.FB[rows, :]
            content = k.CT[rows, cols].astype(f32)
            k.PR[rows, cols] = (content * out).astype(bf16)
            grad_spatial = (grad * content).astype(bf16)
            k.GS[rows, cols] = grad_spatial
            along = fold_lanes(grad_spatial.astype(f32))
            k.BSA[rows, :] = along if j == 0 else k.BSA[rows, :] + along
            before = (grad * out * k.DC[rows, cols].astype(f32)).astype(bf16)
            k.GB[rows, cols] = before
            total = total + fold_rows(before.astype(f32))
        k.SG[:, d.o_bias_up + j * CH : d.o_bias_up + (j + 1) * CH] = total

    def project():
        def body(i):
            rows = span(i * 256, 256)
            k.FA[rows, 0:D] = dot_nn(k.PR[rows, :], k.DOWN[...])
            for j in range(0, 256, 16):
                part = span(i * 256 + j, 16)
                value = k.FA[part, 0:D] + small(d.o_bias_down, D, 16) + k.X[part, :].astype(f32)
                k.OT[part, :] = value.astype(bf16)

        loop(T // 256, body)

    def grad_down():
        step = d.pd * max(1, 384 // d.pd)
        for first in range(0, G, step):
            size = min(step, G - first)
            value = dot_tn(k.PR[:, first : first + size], k.C[...])
            for owner in range(first // d.pd, (first + size) // d.pd):
                at = owner * d.pd - first
                k.PD[owner // d.minor, owner % d.minor] = value[at : at + d.pd].astype(k.PD.dtype)

    def grad_up(first):
        cols = slice(first, first + CH)
        value = dot_nn(k.NT[...], k.GB[:, cols])
        k.PU[:, :, :, cols] = value.reshape(d.major, d.minor, d.pu, CH).astype(k.PU.dtype)

    def grad_spatial_weight():
        k.FA[0:S, 0:S] = dot_nt(k.GS[0:S, :], k.GATE[0:S, :])
        k.FB[0:H, 0:S] = dot_nt(k.GS[S:T, :], k.GATE[S : 2 * S, :])

        def body(i):
            rows = span(i * 32, 32)
            keep = lanes_of(k.col_t[0, rows, :], S) == rows_of(k.row_s[0], 32)
            k.FA[rows, 0:S] = jnp.where(keep, k.FA[rows, 0:S], 0.0)

        loop(S // 32, body)

        def shared(i):
            rows = span(c * H + i * 32, 32)
            keep = lanes_of(k.col_t[1, rows, :], S) == rows_of(k.row_s[1], 32)
            k.FA[rows, 0:S] = k.FA[rows, 0:S] + jnp.where(keep, k.FB[span(i * 32, 32), 0:S], 0.0)

        loop(H // 32, shared)
        k.PS[...] = k.FA[0:S, 0:S].reshape(d.major, d.minor, d.ps, S).astype(k.PS.dtype)

    def grad_gate_shared():
        other = span((1 - c) * H, H)
        for j in range(d.chunks):
            cols = slice(j * CH, (j + 1) * CH)
            k.GX[:, cols] = dot_nn(k.MTB[other, :], k.GS[S:T, cols]).astype(bf16)
        return comm.start(k.GX, k.GY, sibling)

    def gate_terms(rows, cols, grad, j, sums):
        xhat = k.XH[rows, cols].astype(f32)
        product = grad * xhat
        gain = small(d.o_gain_gate + j * CH, CH, 16)
        one, two = fold_lanes(grad * gain), fold_lanes(product * gain)
        k.S1[rows, :] = one if j == 0 else k.S1[rows, :] + one
        k.S2[rows, :] = two if j == 0 else k.S2[rows, :] + two
        return sums[0] + fold_rows(product), sums[1] + fold_rows(grad)

    def grad_gate(j):
        cols = slice(j * CH, (j + 1) * CH)
        mine = span(c * H, H)
        k.F[S:T, cols] = dot_nn(k.MTB[mine, :], k.GS[S:T, cols])
        k.F[0:S, cols] = dot_nn(k.MT[...], k.GS[0:S, cols])
        sums = (jnp.zeros((8, CH), f32), jnp.zeros((8, CH), f32))
        for first in range(0, S, 16):
            rows = slice(first, first + 16)
            sums = gate_terms(rows, cols, k.F[rows, cols], j, sums)
        for offset, total in zip((d.o_gain_gate, d.o_shift_gate), sums):
            k.SG[:, offset + j * CH : offset + (j + 1) * CH] = total

    def grad_gate_other(j):
        cols = slice(j * CH, (j + 1) * CH)
        sums = (jnp.zeros((8, CH), f32), jnp.zeros((8, CH), f32))
        for first in range(S, T, 16):
            rows = slice(first, first + 16)
            grad = k.F[rows, cols] + k.GY[first - S : first - S + 16, cols].astype(f32)
            k.F[rows, cols] = grad
            sums = gate_terms(rows, cols, grad, j, sums)
        for offset, total in zip((d.o_gain_gate, d.o_shift_gate), sums):
            at = slice(offset + j * CH, offset + (j + 1) * CH)
            k.SG[:, at] = k.SG[:, at] + total

    def gate_back(j):
        cols = slice(j * CH, (j + 1) * CH)
        gain = small(d.o_gain_gate + j * CH, CH, 16)
        total = jnp.zeros((8, CH), f32)
        for first in range(0, T, 16):
            rows = slice(first, first + 16)
            scaled = k.F[rows, cols] * gain - lanes_of(k.S1[rows, :], CH)
            back = scaled - k.XH[rows, cols].astype(f32) * lanes_of(k.S2[rows, :], CH)
            back = back * lanes_of(k.RG[rows, :], CH)
            before = (back * k.DG[rows, cols].astype(f32)).astype(bf16)
            k.GB[rows, G + j * CH : G + (j + 1) * CH] = before
            total = total + fold_rows(before.astype(f32))
        k.SG[:, d.o_bias_up + G + j * CH : d.o_bias_up + G + (j + 1) * CH] = total

    def grad_normed(i):
        rows = slice(i * 256, (i + 1) * 256)
        k.FA[rows, 0:D] = dot_nt(k.GB[rows, :], k.UP[...])

    def input_back():
        def parts(rows):
            xhat = (k.X[rows, :].astype(f32) - lanes_of(k.MU[rows, :], D)) * lanes_of(k.RX[rows, :], D)
            grad = k.FA[rows, 0:D]
            return xhat, grad, grad * small(d.o_gain_in, D, 32)

        def sums(i):
            rows = span(i * 32, 32)
            xhat, grad, scaled = parts(rows)
            k.S1[rows, :] = fold_lanes(scaled)
            k.S2[rows, :] = fold_lanes(scaled * xhat)

        loop(T // 32, sums)
        row_mean(k.S1, 0, T, D, lambda v: v)
        row_mean(k.S2, 0, T, D, lambda v: v)
        for offset in (d.o_gain_in, d.o_shift_in, d.o_bias_down):
            k.SG[:, offset : offset + D] = jnp.zeros((8, D), f32)

        def body(i):
            rows = span(i * 32, 32)
            xhat, grad, scaled = parts(rows)
            cot = k.C[rows, :].astype(f32)
            back = scaled - lanes_of(k.S1[rows, :], D) - xhat * lanes_of(k.S2[rows, :], D)
            k.IT[rows, :] = (back * lanes_of(k.RX[rows, :], D) + cot).astype(bf16)
            for offset, term in ((d.o_gain_in, grad * xhat), (d.o_shift_in, grad), (d.o_bias_down, cot)):
                k.SG[:, offset : offset + D] = k.SG[:, offset : offset + D] + fold_rows(term)

        loop(T // 32, body)

    back = []
    for number, (source, target) in enumerate(((k.OT, k.out), (k.IT, k.ig))):
        for g in range(4):
            here = source.at[g * blk : (g + 1) * blk, :]
            back.append((here, target.at[3 * y + c], g, number * 6 + g, number * 6 + b))
        for half in range(2):
            here, i = source.at[S + half * blk : S + (half + 1) * blk, :], number * 6 + 4
            back.append((here, target.at[3 * y + 2], 2 * c + half, i + half, i + y))

    def back_copy(src, dst, g, i, slot):
        return pltpu.make_async_remote_copy(
            src_ref=src,
            dst_ref=dst,
            send_sem=k.back_send.at[i],
            recv_sem=k.back_recv.at[slot],
            device_id=blk_of(g),
            device_id_type=MESH,
        )

    def start_back(number):
        for src, dst, g, i, slot in back[number * 6 : number * 6 + 6]:

            @pl.when(g == b)
            def _():
                pltpu.make_async_copy(src, dst, k.back_recv.at[slot]).start()

            @pl.when(g != b)
            def _():
                back_copy(src, dst, g, i, slot).start()

    def finish_back():
        for number, (source, target) in enumerate(((k.OT, k.out), (k.IT, k.ig))):
            here = source.at[0:blk, :]
            for g in range(4):
                row = (g // 2) * 3 + g % 2
                pltpu.make_async_copy(here, target.at[row], k.back_recv.at[number * 6 + g]).wait()
            for half in range(2):
                slot = number * 6 + 4 + half
                pltpu.make_async_copy(here, target.at[half * 3 + 2], k.back_recv.at[slot]).wait()
        for src, dst, g, i, slot in back:

            @pl.when(g != b)
            def _():
                back_copy(src, dst, g, i, slot).wait_send()

    def reduce(name, part, first, width, s, low):
        route = d.routes[name]
        bufs = [getattr(k, "%s_%d" % (name, i)) for i in range(1 + 2 * len(route))]
        return Reduce(net, part, first, width, s, route, bufs, low)

    red = {}
    for j in range(d.chunks):
        red["uc%d" % j] = reduce("uc%d" % j, k.PU, j * CH, CH, d.pu, k.up_low.at[j])
        red["ug%d" % j] = reduce("ug%d" % j, k.PU, G + j * CH, CH, d.pu, k.up_low.at[d.chunks + j])
    red["dn"] = reduce("dn", k.PD, 0, D, d.pd, k.down_low)
    red["sp"] = reduce("sp", k.PS, 0, S, d.ps, k.sp_low)

    def column_sums():
        bias = jnp.sum(jnp.transpose(k.BSA[...]), axis=0, keepdims=True)
        k.SG[:, d.o_bias_spatial : d.o_bias_spatial + S] = jnp.zeros((8, S), f32)
        k.SG[0:1, d.o_bias_spatial : d.o_bias_spatial + S] = bias[:, 0:S]
        place = pl.ds(pl.multiple_of(d.o_bias_spatial + c * H, H), H)
        k.SG[0:1, place] = k.SG[0:1, place] + bias[:, S:T]
        for i in range(d.nsmall // LANES):
            total = jnp.sum(k.SG[:, i * LANES : (i + 1) * LANES], axis=0, keepdims=True)
            k.small_part[i : i + 1, :] = total

    quarter = d.nsmall // LANES // 4

    def small_blk():
        made = []
        for db in range(1, 4):
            other = lax.rem(b + db, 4)
            part = k.small_part.at[span(other * quarter, quarter), :]
            made.append(comm.start(part, k.small_one.at[db - 1], (r, other)))
        return made

    def small_rows(before):
        for copy in before:
            copy.wait_recv()
        value = k.small_part[span(b * quarter, quarter), :]
        for i in range(3):
            value = value + k.small_one[i]
        k.small_two[0] = value
        return [
            comm.start(k.small_two.at[0], k.small_two.at[dr], (lax.rem(r + dr, d.R), b)) for dr in range(1, d.R)
        ]

    def small_share(before):
        for copy in before:
            copy.wait_recv()
        value = k.small_two[0]
        for dr in range(1, d.R):
            value = value + k.small_two[dr]
        k.small_sum[...] = value
        mine = k.gsmall.at[span(b * quarter, quarter), :]
        local = pltpu.make_async_copy(k.small_sum, mine, local_sem())
        local.start()
        made = [comm.start(k.small_sum, mine, (r, lax.rem(b + db, 4))) for db in range(1, 4)]
        return local, made, jnp.sum(fold_rows(value * value))

    schedule(d, types.SimpleNamespace(**locals()))


def schedule(d, p):
    k, comm, flow, red = p.k, p.comm, p.flow, p.red
    chunks, per, r, b, G, CH = d.chunks, p.per, p.r, p.b, d.G, d.CH

    def done(i):
        flow[i].end()

    for name in ("small", "up", "sp", "down"):
        p.staged(name)
    pl.semaphore_wait(p.barrier, d.R - 1 + 3)
    p.start_tokens(0)
    p.share_pair()
    p.send_small()
    flow[0].begin()
    flow[1].begin()
    p.make_labels()

    def minor(i):
        flow[i].minor()
        if i + 2 < len(flow):
            flow[i + 2].begin()

    last = len(flow) - 1
    if per > 1:
        minor(0)
        p.take_small()
        minor(1)
        flow[0].last()
        p.wait_tokens(0)
        p.input_norm()
        p.start_tokens(1)
        for j in range(chunks):
            minor(j + 2)
            flow[j + 1].last()
            done(j)
            p.up_gate(j)
            if j == 0:
                p.turn_normed()
    else:
        p.take_small()
        p.wait_tokens(0)
        p.input_norm()
        p.turn_normed()
        p.start_tokens(1)
        for i in range(len(flow)):
            minor(i)
            flow[i].last()
            if i == last:
                flow[i].swap()
            done(i)
        for j in range(chunks):
            p.up_gate(j)
    p.gate_norm(d.S, d.H, d.S + p.c * d.H)
    mine = k.GATE.at[span(d.S + p.c * d.H, d.H), :]
    gate_copy = comm.start(mine, mine, p.sibling)
    if per > 1:
        minor(5)
        flow[4].last()
        done(3)
        p.gate_norm(0, d.S, 0)
        minor(6)
        flow[5].last()
        done(4)
        p.up_content(0)
        minor(7)
        flow[6].last()
        done(5)
        p.up_content(1)
        flow[7].last()
        done(6)
        p.make_mixing()
        p.up_content(2)
        flow[7].swap()
        done(7)
    else:
        p.gate_norm(0, d.S, 0)
        p.make_mixing()
        for j in range(chunks):
            p.up_content(j)
    p.wait_tokens(1)
    gate_copy.wait_recv()

    uc = [red["uc%d" % j] for j in range(chunks)]
    ug = [red["ug%d" % j] for j in range(chunks)]
    dn, sp = red["dn"], red["sp"]
    squares = []

    def final(one):
        if d.pair > 1:
            one.advance()
        squares.append(one.advance())

    for j in range(chunks):
        p.mix(j)
        p.grad_up(j * CH)
        uc[j].start()
        if j:
            uc[j - 1].advance()
    gate_gradient = p.grad_gate_shared()
    p.grad_down()
    dn.start()
    uc[-1].advance()
    for j in range(chunks):
        p.grad_gate(j)
        uc[j].advance()
        if j == 0:
            dn.advance()
    gate_gradient.wait_recv()
    for j in range(chunks):
        p.grad_gate_other(j)
    p.row_mean(k.S1, 0, d.T, G, lambda v: v)
    p.row_mean(k.S2, 0, d.T, G, lambda v: v)
    for j in range(chunks):
        p.gate_back(j)
        p.grad_up(G + j * CH)
        ug[j].start()
        if j:
            ug[j - 1].advance()
        uc[j].advance()
    p.grad_spatial_weight()
    sp.start()
    ug[-1].advance()
    dn.advance()
    p.project()
    p.start_back(0)
    sp.advance()
    for j in range(chunks):
        final(uc[j])
    for j in range(chunks):
        p.grad_normed(j)
        ug[j].advance()
    dn.advance()
    sp.advance()
    p.input_back()
    p.start_back(1)
    p.column_sums()
    small = p.small_blk()
    for one in ug:
        one.advance()
    small = p.small_rows(small)
    final(dn)
    sp.advance()
    for one in ug:
        final(one)
    final(sp)
    total = squares[0]
    for value in squares[1:]:
        total = total + value
    k.norm_rows[0] = jnp.full((8, LANES), total, f32)
    norm_one = [
        comm.start(k.norm_rows.at[0], k.norm_rows.at[dr], (lax.rem(r + dr, d.R), b)) for dr in range(1, d.R)
    ]
    local, shared, extra = p.small_share(small)
    for copy in norm_one:
        copy.wait_recv()
    value = jnp.full((8, LANES), extra, f32)
    for i in range(d.R):
        value = value + k.norm_rows[lax.rem(i - r + 2 * d.R, d.R)]
    k.norm_blk[b] = value
    norm_two = [
        comm.start(k.norm_blk.at[b], k.norm_blk.at[b], (r, lax.rem(b + db, 4))) for db in range(1, 4)
    ]
    for one in red.values():
        one.end()
    local.wait()
    for copy in shared + norm_two:
        copy.wait_recv()
    value = k.norm_blk[0]
    for i in range(1, 4):
        value = value + k.norm_blk[i]
    k.norm[...] = jnp.sqrt(value)
    p.finish_back()
    p.finish_tokens()
    comm.finish()

def adam_kernel(d, count, *refs):
    norm, out_in, ig_in = refs[:3]
    given = refs[3 : 3 + count]
    norm_out, out, ig = refs[3 + count : 6 + count]
    results = refs[6 + count : 18 + count]
    held = refs[18 + count : 18 + 2 * count]
    sems, turned = refs[18 + 2 * count :]
    r = lax.axis_index("rows")
    through = [
        pltpu.make_async_copy(out_in, out, sems.at[0]),
        pltpu.make_async_copy(ig_in, ig, sems.at[1]),
    ]
    loads = [pltpu.make_async_copy(src, dst, sems.at[2 + i]) for i, (src, dst) in enumerate(zip(given, held))]
    for copy in loads + through:
        copy.start()
    value = norm[...]
    norm_out[0, 0] = norm[0, 0]
    factor = jnp.minimum(1.0, max_norm / (value + 1e-06))
    low_up, low_down, low_sp, gsmall = held[:4]
    params = held[4:]
    stores = []

    def step(ins, grad, rate, decay, place):
        weight, moment, square = (ref[place] for ref in ins)
        grad = grad * factor[0:1, :]
        moment_next = beta_one * moment + (1.0 - beta_one) * grad
        square_next = beta_two * square + (1.0 - beta_two) * grad * grad
        moment_hat = moment_next / (1.0 - beta_one**STEP)
        square_hat = square_next / (1.0 - beta_two**STEP)
        update = moment_hat / (jnp.sqrt(square_hat) + 1e-08) + decay * weight
        for ref, result in zip(ins, (weight - rate * update, moment_next, square_next)):
            ref[place] = result

    def store(i):
        for j in range(3):
            n = 3 * i + j
            copy = pltpu.make_async_copy(params[n], results[n], sems.at[2 + count + n])
            copy.start()
            stores.append(copy)

    def part(low, q, first, s, width):
        start = first + (2 * (q % 2) + q // 2) * (width // 4)
        for at in range(0, width // 4, LANES):
            grad = low[q, :, at : at + LANES].astype(f32)
            if d.pair > 1:
                turned[0 : d.pair * s, :] = grad
                grad = turned[pl.ds(pl.multiple_of(lax.rem(r, d.pair) * s, s), s), :]
            yield grad, (slice(0, s), slice(start + at, start + at + LANES))

    for i in (3, 13, 14, 15):
        loads[i].wait()
    grad = gsmall[pl.ds(r * d.ks, d.ks), :]
    step(params[9:12], grad, small_rate, 0.0, (slice(0, d.ks), slice(0, LANES)))
    store(3)
    for i in (1, 7, 8, 9):
        loads[i].wait()
    for q in range(4):
        for grad, place in part(low_down, q, 0, d.sd, d.D):
            step(params[3:6], grad, weight_rate, weight_decay, place)
    store(1)
    for i in (2, 10, 11, 12):
        loads[i].wait()
    for q in range(4):
        for grad, place in part(low_sp, q, 0, d.ss, d.S):
            step(params[6:9], grad, weight_rate, weight_decay, place)
    store(2)
    for i in (0, 4, 5, 6):
        loads[i].wait()
    for j in range(2 * d.chunks):
        for q in range(4):
            for grad, place in part(low_up.at[j], q, j * d.CH, d.su, d.CH):
                step(params[0:3], grad, weight_rate, weight_decay, place)
    store(0)
    for copy in through + stores:
        copy.wait()


def body(mesh, *arrays):
    (
        inputs,
        cotangent,
        lengths,
        up_weight,
        up_moment,
        up_square,
        down_weight,
        down_moment,
        down_square,
        spatial_weight,
        spatial_moment,
        spatial_square,
        small_params,
        small_moment,
        small_square,
    ) = arrays
    d = plan_of(
        mesh,
        dict(
            inputs=inputs.shape,
            up=up_weight.shape,
            down=down_weight.shape,
            spatial=spatial_weight.shape,
            small=small_params.shape,
        ),
    )
    S, H, T, D, G, FF, R = d.S, d.H, d.T, d.D, d.G, d.FF, d.R
    wire = bf16
    small_rows = d.nsmall // LANES
    quarter = small_rows // 4

    any_spec = pl.BlockSpec(memory_space=pl.ANY)
    vmem_spec = pl.BlockSpec(memory_space=VMEM)
    smem_spec = pl.BlockSpec(memory_space=pltpu.SMEM)

    ins = dict(
        x_in=(jnp.transpose(inputs, (1, 0, 2)), any_spec),
        c_in=(jnp.transpose(cotangent, (1, 0, 2)), any_spec),
        lengths=(lengths.T, smem_spec),
        up_w=(up_weight, any_spec),
        down_w=(down_weight, any_spec),
        sp_w=(spatial_weight, any_spec),
        small_w=(small_params.reshape(d.ks, LANES), any_spec),
    )
    outs = dict(
        out=((d.rows_here, d.block, D), bf16, any_spec),
        ig=((d.rows_here, d.block, D), bf16, any_spec),
        norm=((8, LANES), f32, vmem_spec),
        gsmall=((small_rows, LANES), f32, any_spec),
        up_low=((2 * d.chunks, 4, d.pu, d.CH // 4), wire, any_spec),
        down_low=((4, d.pd, D // 4), wire, any_spec),
        sp_low=((4, d.ps, S // 4), wire, any_spec),
    )
    scratch = dict(
        up_stage=VMEM((d.pu, FF), f32),
        down_stage=VMEM((d.pd, D), f32),
        sp_stage=VMEM((d.ps, S), f32),
        small_stage=VMEM((d.ks, LANES), f32),
        small_get=VMEM((R, 8, LANES), f32),
        SM=VMEM((8, d.nsmall), f32),
        SG=VMEM((8, d.nsmall), f32),
        UP=VMEM((D, FF), bf16),
        DOWN=VMEM((G, D), bf16),
        SP=VMEM((S, S), bf16),
        X=VMEM((T, D), bf16),
        C=VMEM((T, D), bf16),
        N=VMEM((T, D), bf16),
        NT=VMEM((D, T), bf16),
        F=VMEM((T, G), f32),
        FA=VMEM((T, 512), f32),
        FB=VMEM((T, 512), f32),
        DG=VMEM((T, G), bf16),
        XH=VMEM((T, G), bf16),
        RG=VMEM((T, LANES), f32),
        GATE=VMEM((2 * S, G), bf16),
        CT=VMEM((T, G), bf16),
        DC=VMEM((T, G), bf16),
        PR=VMEM((T, G), bf16),
        GS=VMEM((T, G), bf16),
        GB=VMEM((T, FF), bf16),
        GX=VMEM((H, G), bf16),
        GY=VMEM((H, G), bf16),
        BS=VMEM((T, LANES), f32),
        BSA=VMEM((T, LANES), f32),
        M=VMEM((T, S), bf16),
        MT=VMEM((S, S), bf16),
        MTB=VMEM((S, H), bf16),
        row_t=VMEM((2, 8, S), f32),
        row_s=VMEM((2, 8, S), f32),
        col_t=VMEM((2, S, LANES), f32),
        col_s=VMEM((2, S, LANES), f32),
        OT=VMEM((T, D), bf16),
        IT=VMEM((T, D), bf16),
        PU=VMEM((d.major, d.minor, d.pu, FF), wire),
        PD=VMEM((d.major, d.minor, d.pd, D), wire),
        PS=VMEM((d.major, d.minor, d.ps, S), wire),
        MU=VMEM((T, LANES), f32),
        RX=VMEM((T, LANES), f32),
        S1=VMEM((T, LANES), f32),
        S2=VMEM((T, LANES), f32),
        small_sum=VMEM((quarter, LANES), f32),
        small_part=VMEM((small_rows, LANES), f32),
        small_one=VMEM((3, quarter, LANES), f32),
        small_two=VMEM((R, quarter, LANES), f32),
        norm_rows=VMEM((R, 8, LANES), f32),
        norm_blk=VMEM((4, 8, LANES), f32),
    )
    sizes = {"dn": (D, d.pd), "sp": (S, d.ps)}
    d.routes = {"dn": "xzy", "sp": "yxz"}
    for j in range(d.chunks):
        sizes["uc%d" % j] = sizes["ug%d" % j] = (d.CH, d.pu)
        d.routes["uc%d" % j] = "xzy"
        d.routes["ug%d" % j] = ("xyz", "yxz", "xzy")[j % 3]
    if d.pair > 1:
        d.routes = {name: route + "p" for name, route in d.routes.items()}
    for name, (width, s) in sizes.items():
        for i, shape in enumerate(reduce_shapes(d, width, s, d.routes[name])):
            scratch["%s_%d" % (name, i)] = VMEM(shape, wire)
    owners = d.major * d.minor
    pieces = d.major - 1 + d.major * (d.minor - 1) + owners - 1
    flows = 2 * (d.chunks if d.split else 1) + 2
    copies = flows * pieces + 2 * (owners - 1) + len(sizes) * (1 + 1 + d.minor - 1 + d.major - 1 + d.pair - 1 + 3)
    copies += 3 * (d.pair - 1) + 2 + 3 * (R - 1) + 3 * 3
    scratch["send_sem"] = pltpu.SemaphoreType.DMA((copies,))
    scratch["recv_sem"] = pltpu.SemaphoreType.DMA((copies,))
    scratch["token_send"] = pltpu.SemaphoreType.DMA((12,))
    scratch["token_recv"] = pltpu.SemaphoreType.DMA((12,))
    scratch["back_send"] = pltpu.SemaphoreType.DMA((12,))
    scratch["back_recv"] = pltpu.SemaphoreType.DMA((12,))
    scratch["local_sem"] = pltpu.SemaphoreType.DMA((64,))

    names = list(ins) + list(outs) + list(scratch)

    def kernel(*refs):
        refs = list(refs)
        have = dict(zip(names, refs))
        main_kernel(d, list(have), *have.values())

    results = pl.pallas_call(
        kernel,
        out_shape=[jax.ShapeDtypeStruct(shape, dtype) for shape, dtype, _ in outs.values()],
        in_specs=[spec for _, spec in ins.values()],
        out_specs=[spec for _, _, spec in outs.values()],
        scratch_shapes=list(scratch.values()),
        compiler_params=pltpu.CompilerParams(
            collective_id=0, has_side_effects=True, vmem_limit_bytes=63 * 1024 * 1024
        ),
        name="block_step",
    )(*[array for array, _ in ins.values()])
    got = dict(zip(outs, results))

    params = [
        up_weight,
        up_moment,
        up_square,
        down_weight,
        down_moment,
        down_square,
        spatial_weight,
        spatial_moment,
        spatial_square,
        small_params.reshape(d.ks, LANES),
        small_moment.reshape(d.ks, LANES),
        small_square.reshape(d.ks, LANES),
    ]
    passed = [got["up_low"], got["down_low"], got["sp_low"], got["gsmall"], *params]
    count = len(passed)
    updated = pl.pallas_call(
        functools.partial(adam_kernel, d, count),
        out_shape=[jax.ShapeDtypeStruct((1, 1), f32)]
        + [jax.ShapeDtypeStruct(got[name].shape, bf16) for name in ("out", "ig")]
        + [jax.ShapeDtypeStruct(p.shape, f32) for p in params],
        in_specs=[vmem_spec] + [any_spec] * (2 + count),
        out_specs=[smem_spec] + [any_spec] * (2 + len(params)),
        scratch_shapes=[VMEM(p.shape, p.dtype) for p in passed]
        + [pltpu.SemaphoreType.DMA((2 + count + 12,)), VMEM((max(d.pu, d.pd, d.ps), LANES), f32)],
        compiler_params=pltpu.CompilerParams(vmem_limit_bytes=63 * 1024 * 1024),
        name="adam_step",
    )(got["norm"], got["out"], got["ig"], *passed)
    norm, out, ig = updated[:3]
    updated = list(updated[3:12]) + [p.reshape(-1) for p in updated[12:]]
    return (
        jnp.transpose(out, (1, 0, 2)),
        jnp.transpose(ig, (1, 0, 2)),
        norm.reshape(()),
        *updated,
    )


def solution(mesh):
    rows = P("rows", None)
    flat = P("rows")
    tokens = P("blk", "rows", None)
    return jax.shard_map(
        functools.partial(body, mesh),
        mesh=mesh,
        in_specs=(tokens, tokens, rows) + (rows,) * 9 + (flat,) * 3,
        out_specs=(tokens, tokens, P()) + (rows,) * 9 + (flat,) * 3,
        check_vma=False,
    )
```

```python
import functools
import math
import types

import jax
import jax.numpy as jnp
from jax import lax
from jax.experimental import pallas as pl
from jax.experimental.pallas import tpu as pltpu
from jax.sharding import PartitionSpec as P

STEP = 10

beta_one = 0.9
beta_two = 0.999
max_norm = 1.0
weight_rate = 0.05
small_rate = 0.5
weight_decay = 0.01

MESH = pl.DeviceIdType.MESH
VMEM = pltpu.VMEM
bf16 = jnp.bfloat16
f32 = jnp.float32
LANES = 128


def loop(count, body):
    def step(i, carry):
        body(i)
        return carry

    lax.fori_loop(0, count, step, 0)


def span(start, size):
    return pl.ds(pl.multiple_of(start, size), size)


def rows_of(value, count):
    return jnp.concatenate([value] * (count // value.shape[0]), axis=0)


def lanes_of(value, count):
    return jnp.concatenate([value] * (count // value.shape[1]), axis=1)


def fold_rows(value):
    total = value[0:8]
    for first in range(8, value.shape[0], 8):
        total = total + value[first : first + 8]
    return total


def fold_lanes(value):
    total = value[:, 0:LANES]
    for first in range(LANES, value.shape[1], LANES):
        total = total + value[:, first : first + LANES]
    return total


def dot_nn(a, b):
    return lax.dot_general(a, b, (((1,), (0,)), ((), ())), preferred_element_type=f32)


def dot_nt(a, b):
    return lax.dot_general(a, b, (((1,), (1,)), ((), ())), preferred_element_type=f32)


def dot_tn(a, b):
    return lax.dot_general(a, b, (((0,), (0,)), ((), ())), preferred_element_type=f32)


def plan_of(mesh, shapes):
    d = types.SimpleNamespace()
    d.R = mesh.shape["rows"]
    d.minor = 1
    while d.minor * d.minor * 2 <= d.R:
        d.minor *= 2
    if d.minor * d.minor > d.R:
        d.minor //= 2
    d.major = d.R // d.minor
    d.block, d.rows_here, d.D = shapes["inputs"]
    d.S = d.block * mesh.shape["blk"]
    d.H = d.S // 2
    d.T = d.S + d.H
    d.FF = shapes["up"][1]
    d.G = d.FF // 2
    d.su, d.sd, d.ss = shapes["up"][0], shapes["down"][0], shapes["spatial"][0]
    d.ks = shapes["small"][0] // LANES
    d.nsmall = d.ks * d.R * LANES
    d.pair = 1
    while any(size * d.pair % 16 for size in (d.su, d.sd, d.ss)):
        d.pair *= 2
    d.minor = d.minor // d.pair
    d.pu, d.pd, d.ps = (size * d.pair for size in (d.su, d.sd, d.ss))
    d.CH = 512 if d.G % 512 == 0 else d.G
    d.chunks = d.G // d.CH
    d.split = d.R <= 16
    d.o_gain_in = 0
    d.o_shift_in = d.D
    d.o_bias_up = 2 * d.D
    d.o_gain_gate = d.o_bias_up + d.FF
    d.o_shift_gate = d.o_gain_gate + d.G
    d.o_bias_spatial = d.o_shift_gate + d.G
    d.o_bias_down = d.o_bias_spatial + d.S
    return d


class Comm:
    def __init__(self, send, recv, space):
        self.send, self.recv, self.space = send, recv, space
        self.sends, self.recvs, self.open = 0, 0, []

    def outgoing(self):
        made = Outgoing(self, self.send.at[self.sends])
        self.sends += 1
        self.open.append(made)
        return made

    def group(self, out=None):
        made = Group(self, out or self.outgoing(), self.recv.at[self.recvs])
        self.recvs += 1
        return made

    def wait(self, sem, size):
        cols = LANES
        while size // cols > self.space.shape[0]:
            cols += LANES
            while size % (cols * 16):
                cols += LANES
        ref = self.space.at[0 : size // cols, 0:cols]
        pltpu.make_async_copy(ref, ref, sem).wait()

    def finish(self):
        for made in self.open:
            self.wait(made.sem, made.size)


class Outgoing:
    def __init__(self, comm, sem):
        self.comm, self.sem, self.size = comm, sem, 0


class Group:
    def __init__(self, comm, out, sem):
        self.comm, self.out, self.sem, self.size = comm, out, sem, 0

    def start(self, src, dst, device):
        size = math.prod(src.shape) * (2 if src.dtype == f32 else 1)
        self.size += size
        self.out.size += size
        pltpu.make_async_remote_copy(
            src_ref=src,
            dst_ref=dst,
            send_sem=self.out.sem,
            recv_sem=self.sem,
            device_id=device,
            device_id_type=MESH,
        ).start()
        return self

    def wait(self):
        self.comm.wait(self.sem, self.size)


class Gather:
    def __init__(self, net, ref, s, first, width, by_y, fill):
        self.net, self.ref, self.s, self.first = net, ref, s, first
        self.half, self.by_y, self.fill = width // 2, by_y, fill
        self.size = self.half // 2 if by_y else self.half
        self.out = net.comm.outgoing()
        self.z, self.x, self.core = (net.comm.group(self.out) for _ in range(3))
        if by_y:
            self.y = net.comm.group(self.out)

    def region(self, owner, of_y=None):
        start = self.first + self.net.c * self.half
        if self.by_y:
            start = start + (self.net.y if of_y is None else of_y) * self.size
        cols = pl.ds(pl.multiple_of(start, LANES), self.size)
        return self.ref.at[span(owner * self.s, self.s), cols]

    def owner(self, dz, dx):
        n = self.net
        return lax.rem(n.zi - dz + n.major, n.major) * n.minor + lax.rem(n.xi - dx + n.minor, n.minor)

    def begin(self):
        n = self.net
        self.fill()
        mine = self.region(n.zi * n.minor + n.xi)
        for dz in range(1, n.major):
            self.z.start(mine, mine, n.at_z(dz))
        for dx in range(1, n.minor):
            self.x.start(mine, mine, n.at_x(dx))

    def onward(self, piece):
        if self.by_y:
            self.y.start(piece, piece, self.net.across)
        self.core.start(piece, piece, self.net.sibling)

    def minor(self):
        n = self.net
        self.z.wait()
        pieces = [self.region(self.owner(dz, 0)) for dz in range(1, n.major)]
        for piece in pieces:
            for dx in range(1, n.minor):
                self.x.start(piece, piece, n.at_x(dx))
        for piece in pieces:
            self.onward(piece)

    def last(self):
        n = self.net
        self.x.wait()
        for dz in range(n.major):
            for dx in range(1, n.minor):
                self.onward(self.region(self.owner(dz, dx)))

    def swap(self):
        n = self.net
        if self.by_y:
            self.y.wait()
            for dz in range(n.major):
                for dx in range(n.minor):
                    if dz or dx:
                        piece = self.region(self.owner(dz, dx), 1 - n.y)
                        self.core.start(piece, piece, n.sibling)

    def end(self):
        self.core.wait()


class Reduce:
    def __init__(self, net, part, first, width, s, route, bufs, low):
        self.net, self.part, self.first, self.s, self.route = net, part, first, s, route
        self.half, self.quarter = width // 2, width // 4
        self.core, self.bufs, self.low = bufs[0], bufs[1:], low
        self.step, self.out = 0, net.comm.outgoing()

    def send(self, copies):
        self.waits = self.net.comm.group(self.out)
        for copy in copies:
            self.waits.start(*copy)

    def cols(self, start, size):
        return pl.ds(pl.multiple_of(self.first + start, LANES), size)

    def start(self):
        n, half = self.net, self.half
        src = self.part.at[:, :, :, self.cols((1 - n.c) * half, half)]
        self.send([(src, self.core, n.sibling)])

    def advance(self):
        n = self.net
        self.waits.wait()
        if self.step == 0:
            mine = self.cols(n.c * self.half, self.half)
            self.zs, self.xs, self.width = n.major, n.minor, self.half

            def add(i, j):
                value = self.part[i, j, :, mine].astype(f32) + self.core[i, j].astype(f32)
                self.core[i, j] = value.astype(self.core.dtype)

            self.blocks(add)
            self.now = self.core
        else:
            kept, got = self.kept, self.got
            made = self.bufs[2 * self.step - 1]

            def add(i, j):
                value = kept(i, j).astype(f32)
                for ref in got:
                    value = value + ref[i, j].astype(f32)
                made[i, j] = value.astype(made.dtype)

            self.blocks(add)
            self.now = made
        if self.step == len(self.route):
            return self.share()
        axis = self.route[self.step]
        now, into = self.now, self.bufs[2 * self.step]
        self.step += 1
        if axis == "x":
            self.send(
                (now.at[:, pl.ds(lax.rem(n.xi + dx, n.minor), 1)], into.at[dx - 1], n.at_x(dx))
                for dx in range(1, n.minor)
            )
            self.got = [into.at[dx - 1] for dx in range(1, n.minor)]
            self.kept = lambda i, j: now[i, n.xi]
            self.xs = 1
        elif axis == "z":
            self.send(
                (now.at[pl.ds(lax.rem(n.zi + dz, n.major), 1)], into.at[dz - 1], n.at_z(dz))
                for dz in range(1, n.major)
            )
            self.got = [into.at[dz - 1] for dz in range(1, n.major)]
            self.kept = lambda i, j: now[n.zi, j]
            self.zs = 1
        elif axis == "p":
            self.send((now, into.at[dp - 1], n.at_pair(dp)) for dp in range(1, n.pair))
            self.got = [into.at[dp - 1] for dp in range(1, n.pair)]
            self.kept = lambda i, j: now[i, j]
        else:
            width = self.width // 2
            theirs = pl.ds(pl.multiple_of((1 - n.y) * width, LANES), width)
            mine = pl.ds(pl.multiple_of(n.y * width, LANES), width)
            self.send([(now.at[:, :, :, theirs], into.at[0], n.across)])
            self.got = [into.at[0]]
            self.kept = lambda i, j: now[i, j, :, mine]
            self.width = width

    def blocks(self, add):
        zs, xs = self.zs, self.xs
        if zs * xs == 1:
            add(0, 0)
        else:
            loop(zs * xs, lambda i: add(i // xs, lax.rem(i, xs)))

    def share(self):
        n, mine = self.net, self.now.at[0, 0]
        self.local = pltpu.make_async_copy(mine, self.low.at[n.b], n.local_sem())
        self.local.start()
        self.send((mine, self.low.at[n.b], (n.r, lax.rem(n.b + db, 4))) for db in range(1, 4))
        kept = self.now[0, 0].astype(f32)
        return jnp.sum(fold_lanes(fold_rows(kept * kept)))

    def end(self):
        self.local.wait()
        self.waits.wait()


def reduce_shapes(d, width, s, route):
    zs, xs, wide = d.major, d.minor, width // 2
    shapes = [(zs, xs, s, wide)]
    for axis in route:
        if axis == "x":
            count, xs = max(d.minor - 1, 1), 1
        elif axis == "z":
            count, zs = max(d.major - 1, 1), 1
        elif axis == "p":
            count = d.pair - 1
        else:
            count, wide = 1, wide // 2
        shapes.append((count, zs, xs, s, wide))
        shapes.append((zs, xs, s, wide))
    return shapes


def main_kernel(d, names, *refs):
    k = types.SimpleNamespace(**dict(zip(names, refs)))
    comm = Comm(k.send_sem, k.recv_sem, k.GATE)
    r, b = lax.axis_index("rows"), lax.axis_index("blk")
    line = d.minor * d.pair
    zi, xi, xp = r // line, lax.rem(r, line) // d.pair, lax.rem(r, d.pair)
    y, c = b // 2, lax.rem(b, 2)
    S, H, T, D, G, FF, CH = d.S, d.H, d.T, d.D, d.G, d.FF, d.CH
    blk = d.block
    sibling = (r, 2 * y + 1 - c)
    across = (r, 2 * (1 - y) + c)

    def at_z(dz):
        return (lax.rem(zi + dz, d.major) * line + xi * d.pair + xp, b)

    def at_x(dx):
        return (zi * line + lax.rem(xi + dx, d.minor) * d.pair + xp, b)

    def at_pair(dp):
        return (zi * line + xi * d.pair + lax.rem(xp + dp, d.pair), b)

    used = [0]

    def local_sem():
        used[0] += 1
        return k.local_sem.at[used[0] - 1]

    net = types.SimpleNamespace(
        comm=comm, r=r, b=b, zi=zi, xi=xi, y=y, c=c, major=d.major, minor=d.minor,
        sibling=sibling, across=across, at_z=at_z, at_x=at_x, at_pair=at_pair, pair=d.pair, local_sem=local_sem,
    )

    barrier = pltpu.get_barrier_semaphore()
    for dr in range(1, d.R):
        pl.semaphore_signal(barrier, inc=1, device_id=(lax.rem(r + dr, d.R), b), device_id_type=MESH)
    for db in range(1, 4):
        pl.semaphore_signal(barrier, inc=1, device_id=(r, lax.rem(b + db, 4)), device_id_type=MESH)

    own = {}
    for name, rows in (("small", d.ks), ("up", d.su), ("sp", d.ss), ("down", d.sd)):
        stage = getattr(k, name + "_stage")
        if name != "small":
            stage = stage.at[span(xp * rows, rows)]
        own[name] = pltpu.make_async_copy(getattr(k, name + "_w"), stage, local_sem())
        own[name].start()

    def staged(name):
        own[name].wait()

    def share_pair():
        if d.pair == 1:
            return
        made = comm.group()
        for name, rows in (("up", d.su), ("sp", d.ss), ("down", d.sd)):
            mine = getattr(k, name + "_stage").at[span(xp * rows, rows)]
            for dp in range(1, d.pair):
                made.start(mine, mine, at_pair(dp))
        made.wait()

    def gather(name, ref, s, first, width, by_y):
        stage = getattr(k, name + "_stage")

        def fill():
            cols = slice(first, first + width)
            ref[span((zi * d.minor + xi) * s, s), cols] = stage[:, cols].astype(bf16)

        return Gather(net, ref, s, first, width, by_y, fill)

    step = CH if d.split else G
    flow = [gather("up", k.UP, d.pu, G + j, step, False) for j in range(0, G, step)]
    flow += [gather("up", k.UP, d.pu, j, step, True) for j in range(0, G, step)]
    flow += [gather("sp", k.SP, d.ps, 0, S, True)]
    step = D // 2 if d.split else D
    flow += [gather("down", k.DOWN, d.pd, j, step, False) for j in range(0, D, step)]

    tokens = []
    for source, target in ((k.x_in, k.X), (k.c_in, k.C)):
        moves = []
        for g in range(4):
            moves.append((source.at[(g // 2) * 3 + g % 2], target.at[span(b * blk, blk), :], g))
        for half in range(2):
            moves.append((source.at[half * 3 + 2], target.at[span(S + c * blk, blk), :], 2 * half + y))
        tokens.append((moves, target))

    def send_blocks(moves, send, recv):
        for src, dst, g in moves:

            @pl.when(g == b)
            def _():
                pltpu.make_async_copy(src, dst, recv).start()

            @pl.when(g != b)
            def _():
                pltpu.make_async_remote_copy(
                    src_ref=src, dst_ref=dst, send_sem=send, recv_sem=recv, device_id=(r, g), device_id_type=MESH
                ).start()

    def sent_blocks(send):
        for here, count in ((y == c, 4), (y != c, 5)):

            @pl.when(here)
            def _():
                space = k.X.at[0 : count * blk, :]
                pltpu.make_async_copy(space, space, send).wait()

    def start_tokens(number):
        send_blocks(tokens[number][0], k.token_sem.at[number], k.token_sem.at[2 + number])

    def wait_tokens(number):
        target = tokens[number][1]
        pltpu.make_async_copy(target, target, k.token_sem.at[2 + number]).wait()

    def finish_tokens():
        for number in range(2):
            sent_blocks(k.token_sem.at[number])

    small_in = comm.group()

    def send_small():
        k.small_get[r] = jnp.zeros((8, LANES), f32)
        k.small_get[r, 0 : d.ks, :] = k.small_stage[...].astype(bf16).astype(f32)
        for dr in range(1, d.R):
            mine = k.small_get.at[r]
            small_in.start(mine, mine, (lax.rem(r + dr, d.R), b))

    def take_small():
        small_in.wait()
        for i in range(d.R):
            for j in range(d.ks):
                first = (i * d.ks + j) * LANES
                k.SM[:, first : first + LANES] = jnp.broadcast_to(k.small_get[i, j : j + 1, :], (8, LANES))

    def small(offset, width, rows):
        return rows_of(k.SM[:, offset : offset + width], rows)

    def label_of(places, ends, source):
        label = jnp.zeros(places.shape, f32)
        for end in ends:
            label = label + jnp.where(places >= end, 1.0, 0.0)
        if source:
            label = jnp.where(places < ends[-1], label, -1.0)
        return label

    lengths_copy = pltpu.make_async_copy(k.lengths_in, k.lengths, local_sem())
    lengths_copy.start()

    def make_labels():
        lengths_copy.wait()
        for which, row in enumerate((3 * y + c, 3 * y + 2)):
            ends = [k.lengths[0, row]]
            for n in range(1, k.lengths.shape[0]):
                ends.append(ends[-1] + k.lengths[n, row])
            lane = lax.broadcasted_iota(jnp.int32, (8, S), 1)
            k.row_t[which] = label_of(lane, ends, False)
            k.row_s[which] = label_of(lane, ends, True)
            for first in range(0, S, 64):
                place = lax.broadcasted_iota(jnp.int32, (64, LANES), 0) + first
                k.col_t[which, first : first + 64, :] = label_of(place, ends, False)
                k.col_s[which, first : first + 64, :] = label_of(place, ends, True)

    def make_mixing():
        k.FA[0:S, :] = k.SP[...].astype(f32)
        k.FB[0:S, :] = jnp.transpose(k.FA[0:S, :])

        def body(i):
            rows = span(i * 32, 32)
            keep = lanes_of(k.col_t[0, rows, :], S) == rows_of(k.row_s[0], 32)
            k.M[rows, :] = jnp.where(keep, k.FA[rows, :], 0.0).astype(bf16)
            keep = lanes_of(k.col_s[0, rows, :], S) == rows_of(k.row_t[0], 32)
            k.MT[rows, :] = jnp.where(keep, k.FB[rows, :], 0.0).astype(bf16)

        loop(S // 32, body)

        def shared(i):
            rows = span(c * H + i * 32, 32)
            keep = lanes_of(k.col_t[1, rows, :], S) == rows_of(k.row_s[1], 32)
            k.M[span(S + i * 32, 32), :] = jnp.where(keep, k.FA[rows, :], 0.0).astype(bf16)

        loop(H // 32, shared)
        own_half = pl.ds(pl.multiple_of(c * H, H), H)

        def turned(i):
            rows = span(i * 32, 32)
            keep = lanes_of(k.col_s[1, rows, :], H) == rows_of(k.row_t[1, :, own_half], 32)
            k.MTB[rows, :] = jnp.where(keep, k.FB[rows, own_half], 0.0).astype(bf16)

        loop(S // 32, turned)
        bias = k.SM[:, d.o_bias_spatial : d.o_bias_spatial + S]
        k.BS[0:S, :] = jnp.transpose(rows_of(bias, LANES))
        k.BS[S:T, :] = k.BS[span(c * H, H), :]

    def row_mean(ref, first, count, width, finish):
        def body(i):
            rows = span(first + i * 128, 128)
            total = jnp.sum(ref[rows, :], axis=1, keepdims=True) * (1.0 / width)
            ref[rows, :] = jnp.broadcast_to(finish(total), (128, LANES))

        loop(count // 128, body)

    def scale_of(spread):
        return lax.rsqrt(spread + 1e-05)

    def input_norm(at, count):
        def sums(i):
            rows = span(at + i * 32, 32)
            k.MU[rows, :] = fold_lanes(k.X[rows, :].astype(f32))

        loop(count // 32, sums)
        row_mean(k.MU, at, count, D, lambda v: v)

        def spreads(i):
            rows = span(at + i * 32, 32)
            centred = k.X[rows, :].astype(f32) - lanes_of(k.MU[rows, :], D)
            k.RX[rows, :] = fold_lanes(centred * centred)

        loop(count // 32, spreads)
        row_mean(k.RX, at, count, D, scale_of)

        def body(i):
            rows = span(at + i * 32, 32)
            centred = k.X[rows, :].astype(f32) - lanes_of(k.MU[rows, :], D)
            normed = centred * lanes_of(k.RX[rows, :], D)
            normed = normed * small(d.o_gain_in, D, 32) + small(d.o_shift_in, D, 32)
            k.N[rows, :] = normed.astype(bf16)

        loop(count // 32, body)

    def turn_normed():
        k.NT[...] = jnp.transpose(k.N[...].astype(f32)).astype(bf16)

    def gelu_parts(before):
        cdf = 0.5 + 0.5 * lax.erf(before * 0.7071067811865476)
        bell = jnp.exp(before * before * -0.5)
        return before * cdf, cdf + before * bell * 0.3989422804014327

    def up_gate(j):
        cols = slice(j * CH, (j + 1) * CH)
        at = G + j * CH
        k.F[:, cols] = dot_nn(k.N[...], k.UP[:, at : at + CH])
        bias = small(d.o_bias_up + at, CH, 16)
        for first in range(0, T, 16):
            rows = slice(first, first + 16)
            active, slope = gelu_parts(k.F[rows, cols] + bias)
            k.F[rows, cols] = active
            k.DG[rows, cols] = slope.astype(bf16)
            total = fold_lanes(active)
            k.S1[rows, :] = total if j == 0 else k.S1[rows, :] + total

    def gate_norm(first_row, count, place):
        row_mean(k.S1, first_row, count, G, lambda v: v)

        def spreads(i):
            rows = span(first_row + i * 16, 16)
            centred = k.F[rows, :] - lanes_of(k.S1[rows, :], G)
            k.RG[rows, :] = fold_lanes(centred * centred)

        loop(count // 16, spreads)
        row_mean(k.RG, first_row, count, G, scale_of)

        def body(i):
            rows = span(first_row + i * 16, 16)
            xhat = (k.F[rows, :] - lanes_of(k.S1[rows, :], G)) * lanes_of(k.RG[rows, :], G)
            k.XH[rows, :] = xhat.astype(bf16)
            gate = xhat * small(d.o_gain_gate, G, 16) + small(d.o_shift_gate, G, 16)
            k.GATE[span(place + i * 16, 16), :] = gate.astype(bf16)

        loop(count // 16, body)

    def up_content(j):
        cols = slice(j * CH, (j + 1) * CH)
        k.FA[...] = dot_nn(k.N[...], k.UP[:, cols])
        bias = small(d.o_bias_up + j * CH, CH, 16)
        for first in range(0, T, 16):
            rows = slice(first, first + 16)
            active, slope = gelu_parts(k.FA[rows, :] + bias)
            k.CT[rows, cols] = active.astype(bf16)
            k.DC[rows, cols] = slope.astype(bf16)

    def mix(j):
        cols = slice(j * CH, (j + 1) * CH)
        k.FA[0:S, :] = dot_nn(k.M[0:S, :], k.GATE[0:S, cols])
        k.FA[S:T, :] = dot_nn(k.M[S:T, :], k.GATE[S : 2 * S, cols])
        k.FB[...] = dot_nt(k.C[...], k.DOWN[cols, :])
        total = jnp.zeros((8, CH), f32)
        for first in range(0, T, 16):
            rows = slice(first, first + 16)
            out = k.FA[rows, :] + lanes_of(k.BS[rows, :], CH)
            grad = k.FB[rows, :]
            content = k.CT[rows, cols].astype(f32)
            k.PR[rows, cols] = (content * out).astype(bf16)
            grad_spatial = (grad * content).astype(bf16)
            k.GS[rows, cols] = grad_spatial
            along = fold_lanes(grad_spatial.astype(f32))
            k.BSA[rows, :] = along if j == 0 else k.BSA[rows, :] + along
            before = (grad * out * k.DC[rows, cols].astype(f32)).astype(bf16)
            k.GB[rows, cols] = before
            total = total + fold_rows(before.astype(f32))
        k.SG[:, d.o_bias_up + j * CH : d.o_bias_up + (j + 1) * CH] = total

    def project():
        def body(i):
            rows = span(i * 256, 256)
            k.FA[rows, 0:D] = dot_nn(k.PR[rows, :], k.DOWN[...])
            for j in range(0, 256, 16):
                part = span(i * 256 + j, 16)
                value = k.FA[part, 0:D] + small(d.o_bias_down, D, 16) + k.X[part, :].astype(f32)
                k.OT[part, :] = value.astype(bf16)

        loop(T // 256, body)

    def grad_down():
        step = d.pd * max(1, 384 // d.pd)
        for first in range(0, G, step):
            size = min(step, G - first)
            value = dot_tn(k.PR[:, first : first + size], k.C[...])
            for owner in range(first // d.pd, (first + size) // d.pd):
                at = owner * d.pd - first
                k.PD[owner // d.minor, owner % d.minor] = value[at : at + d.pd].astype(k.PD.dtype)

    def grad_up(first):
        cols = slice(first, first + CH)
        value = dot_nn(k.NT[...], k.GB[:, cols])
        k.PU[:, :, :, cols] = value.reshape(d.major, d.minor, d.pu, CH).astype(k.PU.dtype)

    def grad_spatial_weight():
        k.FA[0:S, 0:S] = dot_nt(k.GS[0:S, :], k.GATE[0:S, :])
        k.FB[0:H, 0:S] = dot_nt(k.GS[S:T, :], k.GATE[S : 2 * S, :])

        def body(i):
            rows = span(i * 32, 32)
            keep = lanes_of(k.col_t[0, rows, :], S) == rows_of(k.row_s[0], 32)
            k.FA[rows, 0:S] = jnp.where(keep, k.FA[rows, 0:S], 0.0)

        loop(S // 32, body)

        def shared(i):
            rows = span(c * H + i * 32, 32)
            keep = lanes_of(k.col_t[1, rows, :], S) == rows_of(k.row_s[1], 32)
            k.FA[rows, 0:S] = k.FA[rows, 0:S] + jnp.where(keep, k.FB[span(i * 32, 32), 0:S], 0.0)

        loop(H // 32, shared)
        k.PS[...] = k.FA[0:S, 0:S].reshape(d.major, d.minor, d.ps, S).astype(k.PS.dtype)

    def grad_gate_shared():
        other = span((1 - c) * H, H)
        for j in range(d.chunks):
            cols = slice(j * CH, (j + 1) * CH)
            k.GX[:, cols] = dot_nn(k.MTB[other, :], k.GS[S:T, cols]).astype(bf16)
        return comm.group().start(k.GX, k.GY, sibling)

    def gate_terms(rows, cols, grad, j, sums):
        xhat = k.XH[rows, cols].astype(f32)
        product = grad * xhat
        gain = small(d.o_gain_gate + j * CH, CH, 16)
        one, two = fold_lanes(grad * gain), fold_lanes(product * gain)
        k.S1[rows, :] = one if j == 0 else k.S1[rows, :] + one
        k.S2[rows, :] = two if j == 0 else k.S2[rows, :] + two
        return sums[0] + fold_rows(product), sums[1] + fold_rows(grad)

    def grad_gate(j):
        cols = slice(j * CH, (j + 1) * CH)
        mine = span(c * H, H)
        k.F[S:T, cols] = dot_nn(k.MTB[mine, :], k.GS[S:T, cols])
        k.F[0:S, cols] = dot_nn(k.MT[...], k.GS[0:S, cols])
        sums = (jnp.zeros((8, CH), f32), jnp.zeros((8, CH), f32))
        for first in range(0, S, 16):
            rows = slice(first, first + 16)
            sums = gate_terms(rows, cols, k.F[rows, cols], j, sums)
        for offset, total in zip((d.o_gain_gate, d.o_shift_gate), sums):
            k.SG[:, offset + j * CH : offset + (j + 1) * CH] = total

    def grad_gate_other(j):
        cols = slice(j * CH, (j + 1) * CH)
        sums = (jnp.zeros((8, CH), f32), jnp.zeros((8, CH), f32))
        for first in range(S, T, 16):
            rows = slice(first, first + 16)
            grad = k.F[rows, cols] + k.GY[first - S : first - S + 16, cols].astype(f32)
            k.F[rows, cols] = grad
            sums = gate_terms(rows, cols, grad, j, sums)
        for offset, total in zip((d.o_gain_gate, d.o_shift_gate), sums):
            at = slice(offset + j * CH, offset + (j + 1) * CH)
            k.SG[:, at] = k.SG[:, at] + total

    def gate_back(j):
        cols = slice(j * CH, (j + 1) * CH)
        gain = small(d.o_gain_gate + j * CH, CH, 16)
        total = jnp.zeros((8, CH), f32)
        for first in range(0, T, 16):
            rows = slice(first, first + 16)
            scaled = k.F[rows, cols] * gain - lanes_of(k.S1[rows, :], CH)
            back = scaled - k.XH[rows, cols].astype(f32) * lanes_of(k.S2[rows, :], CH)
            back = back * lanes_of(k.RG[rows, :], CH)
            before = (back * k.DG[rows, cols].astype(f32)).astype(bf16)
            k.GB[rows, G + j * CH : G + (j + 1) * CH] = before
            total = total + fold_rows(before.astype(f32))
        k.SG[:, d.o_bias_up + G + j * CH : d.o_bias_up + G + (j + 1) * CH] = total

    def grad_normed(i):
        rows = slice(i * 256, (i + 1) * 256)
        k.FA[rows, 0:D] = dot_nt(k.GB[rows, :], k.UP[...])

    def input_back():
        def parts(rows):
            xhat = (k.X[rows, :].astype(f32) - lanes_of(k.MU[rows, :], D)) * lanes_of(k.RX[rows, :], D)
            grad = k.FA[rows, 0:D]
            return xhat, grad, grad * small(d.o_gain_in, D, 32)

        def sums(i):
            rows = span(i * 32, 32)
            xhat, grad, scaled = parts(rows)
            k.S1[rows, :] = fold_lanes(scaled)
            k.S2[rows, :] = fold_lanes(scaled * xhat)

        loop(T // 32, sums)
        row_mean(k.S1, 0, T, D, lambda v: v)
        row_mean(k.S2, 0, T, D, lambda v: v)
        for offset in (d.o_gain_in, d.o_shift_in, d.o_bias_down):
            k.SG[:, offset : offset + D] = jnp.zeros((8, D), f32)

        def body(i):
            rows = span(i * 32, 32)
            xhat, grad, scaled = parts(rows)
            cot = k.C[rows, :].astype(f32)
            back = scaled - lanes_of(k.S1[rows, :], D) - xhat * lanes_of(k.S2[rows, :], D)
            k.IT[rows, :] = (back * lanes_of(k.RX[rows, :], D) + cot).astype(bf16)
            for offset, term in ((d.o_gain_in, grad * xhat), (d.o_shift_in, grad), (d.o_bias_down, cot)):
                k.SG[:, offset : offset + D] = k.SG[:, offset : offset + D] + fold_rows(term)

        loop(T // 32, body)

    back = []
    for source, target in ((k.OT, k.out), (k.IT, k.ig)):
        moves = []
        for g in range(4):
            moves.append((source.at[g * blk : (g + 1) * blk, :], target.at[3 * y + c], g))
        for half in range(2):
            here = source.at[S + half * blk : S + (half + 1) * blk, :]
            moves.append((here, target.at[3 * y + 2], 2 * c + half))
        back.append((moves, target))

    def start_back(number):
        send_blocks(back[number][0], k.token_sem.at[4 + number], k.token_sem.at[6 + number])

    def finish_back():
        for number in range(2):
            target = back[number][1]
            pltpu.make_async_copy(target, target, k.token_sem.at[6 + number]).wait()
            sent_blocks(k.token_sem.at[4 + number])

    def reduce(name, part, first, width, s, low):
        route = d.routes[name]
        bufs = [getattr(k, "%s_%d" % (name, i)) for i in range(1 + 2 * len(route))]
        return Reduce(net, part, first, width, s, route, bufs, low)

    red = {}
    for j in range(d.chunks):
        red["uc%d" % j] = reduce("uc%d" % j, k.PU, j * CH, CH, d.pu, k.up_low.at[j])
        red["ug%d" % j] = reduce("ug%d" % j, k.PU, G + j * CH, CH, d.pu, k.up_low.at[d.chunks + j])
    red["dn"] = reduce("dn", k.PD, 0, D, d.pd, k.down_low)
    red["sp"] = reduce("sp", k.PS, 0, S, d.ps, k.sp_low)

    def column_sums():
        bias = jnp.sum(jnp.transpose(k.BSA[...]), axis=0, keepdims=True)
        k.SG[:, d.o_bias_spatial : d.o_bias_spatial + S] = jnp.zeros((8, S), f32)
        k.SG[0:1, d.o_bias_spatial : d.o_bias_spatial + S] = bias[:, 0:S]
        place = pl.ds(pl.multiple_of(d.o_bias_spatial + c * H, H), H)
        k.SG[0:1, place] = k.SG[0:1, place] + bias[:, S:T]
        for i in range(d.nsmall // LANES):
            total = jnp.sum(k.SG[:, i * LANES : (i + 1) * LANES], axis=0, keepdims=True)
            k.small_part[i : i + 1, :] = total

    quarter = d.nsmall // LANES // 4

    def small_blk():
        made = comm.group()
        for db in range(1, 4):
            other = lax.rem(b + db, 4)
            part = k.small_part.at[span(other * quarter, quarter), :]
            made.start(part, k.small_one.at[db - 1], (r, other))
        return made

    def to_rows(ref):
        made = comm.group()
        for dr in range(1, d.R):
            made.start(ref.at[0], ref.at[dr], (lax.rem(r + dr, d.R), b))
        return made

    def to_blk(src, dst):
        made = comm.group()
        for db in range(1, 4):
            made.start(src, dst, (r, lax.rem(b + db, 4)))
        return made

    def small_rows(before):
        before.wait()
        value = k.small_part[span(b * quarter, quarter), :]
        for i in range(3):
            value = value + k.small_one[i]
        k.small_two[0] = value
        return to_rows(k.small_two)

    def small_share(before):
        before.wait()
        value = k.small_two[0]
        for dr in range(1, d.R):
            value = value + k.small_two[dr]
        k.small_sum[...] = value
        mine = k.gsmall.at[span(b * quarter, quarter), :]
        local = pltpu.make_async_copy(k.small_sum, mine, local_sem())
        local.start()
        return local, to_blk(k.small_sum, mine), jnp.sum(fold_rows(value * value))

    schedule(d, types.SimpleNamespace(**locals()))


def schedule(d, p):
    k, comm, flow, red = p.k, p.comm, p.flow, p.red
    chunks, r, b, G, CH = d.chunks, p.r, p.b, d.G, d.CH
    flow = list(flow)
    begun = [0]

    def begin(count):
        for _ in range(count):
            if begun[0] < len(flow):
                flow[begun[0]].begin()
                begun[0] += 1

    def minor(i, more=1):
        flow[i].minor()
        begin(more)

    def last(*these):
        for i in these:
            flow[i].last()

    def swap(*these):
        for i in these:
            flow[i].swap()

    def end(*these):
        for i in these:
            flow[i].end()

    def send_gate():
        mine = k.GATE.at[span(d.S + p.c * d.H, d.H), :]
        return comm.group().start(mine, mine, p.sibling)

    def gate_shared():
        p.gate_norm(d.S, d.H, d.S + p.c * d.H)
        return send_gate()

    for name in ("small", "up", "sp", "down"):
        p.staged(name)
    pl.semaphore_wait(p.barrier, d.R - 1 + 3)
    p.start_tokens(0)
    p.share_pair()
    p.send_small()
    begin(2)
    p.make_labels()
    if d.split:
        p.take_small()
        minor(0)
        minor(1)
        last(0)
        minor(2, 2)
        last(1)
        p.wait_tokens(0)
        p.input_norm(0, 256)
        minor(3)
        last(2)
        p.input_norm(256, 256)
        minor(4)
        p.input_norm(512, 256)
        end(0)
        p.up_gate(0)
        minor(5)
        last(3)
        end(1)
        p.up_gate(1)
        minor(6)
        last(4)
        end(2)
        p.up_gate(2)
        last(5)
        swap(3)
        gate_copy = gate_shared()
        last(6)
        swap(4)
        p.start_tokens(1)
        p.gate_norm(0, d.S, 0)
        minor(7)
        end(3)
        p.up_content(0)
        swap(5)
        end(4)
        p.up_content(1)
        swap(6)
        last(7)
        end(5)
        p.up_content(2)
        minor(8)
        p.turn_normed()
        end(6)
        p.make_mixing()
        last(8)
        end(7, 8)
    else:
        p.take_small()
        p.wait_tokens(0)
        p.input_norm(0, d.T)
        p.turn_normed()
        p.start_tokens(1)
        for i in range(len(flow)):
            minor(i)
            last(i)
            swap(i)
            end(i)
        for j in range(chunks):
            p.up_gate(j)
        gate_copy = gate_shared()
        p.gate_norm(0, d.S, 0)
        p.make_mixing()
        for j in range(chunks):
            p.up_content(j)
    p.wait_tokens(1)
    gate_copy.wait()

    uc = [red["uc%d" % j] for j in range(chunks)]
    ug = [red["ug%d" % j] for j in range(chunks)]
    dn, sp = red["dn"], red["sp"]
    squares = []

    def final(one):
        if d.pair > 1:
            one.advance()
        squares.append(one.advance())

    for j in range(chunks):
        p.mix(j)
        p.grad_up(j * CH)
        uc[j].start()
        if j:
            uc[j - 1].advance()
    gate_gradient = p.grad_gate_shared()
    p.grad_down()
    dn.start()
    uc[-1].advance()
    for j in range(chunks):
        p.grad_gate(j)
        uc[j].advance()
        if j == 0:
            dn.advance()
    gate_gradient.wait()
    for j in range(chunks):
        p.grad_gate_other(j)
    p.row_mean(k.S1, 0, d.T, G, lambda v: v)
    p.row_mean(k.S2, 0, d.T, G, lambda v: v)
    for j in range(chunks):
        p.gate_back(j)
        p.grad_up(G + j * CH)
        ug[j].start()
        if j:
            ug[j - 1].advance()
        uc[j].advance()
    p.grad_spatial_weight()
    sp.start()
    ug[-1].advance()
    dn.advance()
    p.project()
    p.start_back(0)
    sp.advance()
    for j in range(chunks):
        final(uc[j])
    for j in range(chunks):
        p.grad_normed(j)
        ug[j].advance()
    dn.advance()
    sp.advance()
    p.input_back()
    p.start_back(1)
    p.column_sums()
    small = p.small_blk()
    for one in ug:
        one.advance()
    small = p.small_rows(small)
    final(dn)
    sp.advance()
    for one in ug:
        final(one)
    final(sp)
    total = squares[0]
    for value in squares[1:]:
        total = total + value
    k.norm_rows[0] = jnp.full((8, LANES), total, f32)
    norm_one = p.to_rows(k.norm_rows)
    local, shared, extra = p.small_share(small)
    norm_one.wait()
    value = jnp.full((8, LANES), extra, f32)
    for i in range(d.R):
        value = value + k.norm_rows[lax.rem(i - r + 2 * d.R, d.R)]
    k.norm_blk[b] = value
    norm_two = p.to_blk(k.norm_blk.at[b], k.norm_blk.at[b])
    for one in red.values():
        one.end()
    local.wait()
    shared.wait()
    norm_two.wait()
    value = k.norm_blk[0]
    for i in range(1, 4):
        value = value + k.norm_blk[i]
    k.norm[...] = jnp.sqrt(value)
    p.finish_back()
    p.finish_tokens()
    comm.finish()

def adam_kernel(d, count, *refs):
    norm, out_in, ig_in = refs[:3]
    given = refs[3 : 3 + count]
    norm_out, out, ig = refs[3 + count : 6 + count]
    results = refs[6 + count : 18 + count]
    held = refs[18 + count : 18 + 2 * count]
    sems, turned, held_out, held_ig = refs[18 + 2 * count :]
    r = lax.axis_index("rows")
    through = [
        (pltpu.make_async_copy(src, held, sems.at[i]), pltpu.make_async_copy(held, dst, sems.at[i]))
        for i, (src, held, dst) in enumerate(((out_in, held_out, out), (ig_in, held_ig, ig)))
    ]
    loads = [pltpu.make_async_copy(src, dst, sems.at[2 + i]) for i, (src, dst) in enumerate(zip(given, held))]
    for copy in loads + [first for first, _ in through]:
        copy.start()
    value = norm[...]
    norm_out[0, 0] = norm[0, 0]
    factor = jnp.minimum(1.0, max_norm / (value + 1e-06))
    low_up, low_down, low_sp, gsmall = held[:4]
    params = held[4:]
    stores = []

    def step(ins, grad, rate, decay, place):
        weight, moment, square = (ref[place] for ref in ins)
        grad = grad * factor[0:1, :]
        moment_next = beta_one * moment + (1.0 - beta_one) * grad
        square_next = beta_two * square + (1.0 - beta_two) * grad * grad
        moment_hat = moment_next / (1.0 - beta_one**STEP)
        square_hat = square_next / (1.0 - beta_two**STEP)
        update = moment_hat / (jnp.sqrt(square_hat) + 1e-08) + decay * weight
        for ref, result in zip(ins, (weight - rate * update, moment_next, square_next)):
            ref[place] = result

    def store(i):
        for j in range(3):
            n = 3 * i + j
            copy = pltpu.make_async_copy(params[n], results[n], sems.at[2 + count + n])
            copy.start()
            stores.append(copy)

    def part(low, q, first, s, width):
        start = first + (2 * (q % 2) + q // 2) * (width // 4)
        for at in range(0, width // 4, LANES):
            grad = low[q, :, at : at + LANES].astype(f32)
            if d.pair > 1:
                turned[0 : d.pair * s, :] = grad
                grad = turned[pl.ds(pl.multiple_of(lax.rem(r, d.pair) * s, s), s), :]
            yield grad, (slice(0, s), slice(start + at, start + at + LANES))

    for i in (3, 13, 14, 15):
        loads[i].wait()
    grad = gsmall[pl.ds(r * d.ks, d.ks), :]
    step(params[9:12], grad, small_rate, 0.0, (slice(0, d.ks), slice(0, LANES)))
    store(3)
    for i in (1, 7, 8, 9):
        loads[i].wait()
    for q in range(4):
        for grad, place in part(low_down, q, 0, d.sd, d.D):
            step(params[3:6], grad, weight_rate, weight_decay, place)
    store(1)
    for i in (2, 10, 11, 12):
        loads[i].wait()
    for q in range(4):
        for grad, place in part(low_sp, q, 0, d.ss, d.S):
            step(params[6:9], grad, weight_rate, weight_decay, place)
    store(2)
    for first, second in through:
        first.wait()
        second.start()
        stores.append(second)
    for i in (0, 4, 5, 6):
        loads[i].wait()
    for j in range(2 * d.chunks):
        for q in range(4):
            for grad, place in part(low_up.at[j], q, j * d.CH, d.su, d.CH):
                step(params[0:3], grad, weight_rate, weight_decay, place)
    store(0)
    for copy in stores:
        copy.wait()


def body(mesh, *arrays):
    (
        inputs,
        cotangent,
        lengths,
        up_weight,
        up_moment,
        up_square,
        down_weight,
        down_moment,
        down_square,
        spatial_weight,
        spatial_moment,
        spatial_square,
        small_params,
        small_moment,
        small_square,
    ) = arrays
    d = plan_of(
        mesh,
        dict(
            inputs=inputs.shape,
            up=up_weight.shape,
            down=down_weight.shape,
            spatial=spatial_weight.shape,
            small=small_params.shape,
        ),
    )
    S, H, T, D, G, FF, R = d.S, d.H, d.T, d.D, d.G, d.FF, d.R
    wire = bf16
    small_rows = d.nsmall // LANES
    quarter = small_rows // 4

    any_spec = pl.BlockSpec(memory_space=pl.ANY)
    vmem_spec = pl.BlockSpec(memory_space=VMEM)
    smem_spec = pl.BlockSpec(memory_space=pltpu.SMEM)

    ins = dict(
        x_in=(jnp.transpose(inputs, (1, 0, 2)), any_spec),
        c_in=(jnp.transpose(cotangent, (1, 0, 2)), any_spec),
        lengths_in=(lengths.T, any_spec),
        up_w=(up_weight, any_spec),
        down_w=(down_weight, any_spec),
        sp_w=(spatial_weight, any_spec),
        small_w=(small_params.reshape(d.ks, LANES), any_spec),
    )
    outs = dict(
        out=((d.rows_here, d.block, D), bf16, any_spec),
        ig=((d.rows_here, d.block, D), bf16, any_spec),
        norm=((8, LANES), f32, vmem_spec),
        gsmall=((small_rows, LANES), f32, any_spec),
        up_low=((2 * d.chunks, 4, d.pu, d.CH // 4), wire, any_spec),
        down_low=((4, d.pd, D // 4), wire, any_spec),
        sp_low=((4, d.ps, S // 4), wire, any_spec),
    )
    scratch = dict(
        lengths=pltpu.SMEM(lengths.T.shape, jnp.int32),
        up_stage=VMEM((d.pu, FF), f32),
        down_stage=VMEM((d.pd, D), f32),
        sp_stage=VMEM((d.ps, S), f32),
        small_stage=VMEM((d.ks, LANES), f32),
        small_get=VMEM((R, 8, LANES), f32),
        SM=VMEM((8, d.nsmall), f32),
        SG=VMEM((8, d.nsmall), f32),
        UP=VMEM((D, FF), bf16),
        DOWN=VMEM((G, D), bf16),
        SP=VMEM((S, S), bf16),
        X=VMEM((T, D), bf16),
        C=VMEM((T, D), bf16),
        N=VMEM((T, D), bf16),
        NT=VMEM((D, T), bf16),
        F=VMEM((T, G), f32),
        FA=VMEM((T, 512), f32),
        FB=VMEM((T, 512), f32),
        DG=VMEM((T, G), bf16),
        XH=VMEM((T, G), bf16),
        RG=VMEM((T, LANES), f32),
        GATE=VMEM((2 * S, G), bf16),
        CT=VMEM((T, G), bf16),
        DC=VMEM((T, G), bf16),
        PR=VMEM((T, G), bf16),
        GS=VMEM((T, G), bf16),
        GB=VMEM((T, FF), bf16),
        GX=VMEM((H, G), bf16),
        GY=VMEM((H, G), bf16),
        BS=VMEM((T, LANES), f32),
        BSA=VMEM((T, LANES), f32),
        M=VMEM((T, S), bf16),
        MT=VMEM((S, S), bf16),
        MTB=VMEM((S, H), bf16),
        row_t=VMEM((2, 8, S), f32),
        row_s=VMEM((2, 8, S), f32),
        col_t=VMEM((2, S, LANES), f32),
        col_s=VMEM((2, S, LANES), f32),
        OT=VMEM((T, D), bf16),
        IT=VMEM((T, D), bf16),
        PU=VMEM((d.major, d.minor, d.pu, FF), wire),
        PD=VMEM((d.major, d.minor, d.pd, D), wire),
        PS=VMEM((d.major, d.minor, d.ps, S), wire),
        MU=VMEM((T, LANES), f32),
        RX=VMEM((T, LANES), f32),
        S1=VMEM((T, LANES), f32),
        S2=VMEM((T, LANES), f32),
        small_sum=VMEM((quarter, LANES), f32),
        small_part=VMEM((small_rows, LANES), f32),
        small_one=VMEM((3, quarter, LANES), f32),
        small_two=VMEM((R, quarter, LANES), f32),
        norm_rows=VMEM((R, 8, LANES), f32),
        norm_blk=VMEM((4, 8, LANES), f32),
    )
    sizes = {"dn": (D, d.pd), "sp": (S, d.ps)}
    d.routes = {"dn": "xzy", "sp": "yxz"}
    for j in range(d.chunks):
        sizes["uc%d" % j] = sizes["ug%d" % j] = (d.CH, d.pu)
        d.routes["uc%d" % j] = "xzy"
        d.routes["ug%d" % j] = ("xyz", "yxz", "xzy")[j % 3]
    if d.pair > 1:
        d.routes = {name: route + "p" for name, route in d.routes.items()}
    for name, (width, s) in sizes.items():
        for i, shape in enumerate(reduce_shapes(d, width, s, d.routes[name])):
            scratch["%s_%d" % (name, i)] = VMEM(shape, wire)
    flows = 2 * d.chunks + 3 if d.split else 4
    sends = flows + len(sizes) + 9
    recvs = 4 * flows + len(sizes) * (2 + len(d.routes["dn"])) + 9
    scratch["send_sem"] = pltpu.SemaphoreType.DMA((sends,))
    scratch["recv_sem"] = pltpu.SemaphoreType.DMA((recvs,))
    scratch["token_sem"] = pltpu.SemaphoreType.DMA((8,))
    scratch["local_sem"] = pltpu.SemaphoreType.DMA((6 + len(sizes),))

    names = list(ins) + list(outs) + list(scratch)

    def kernel(*refs):
        refs = list(refs)
        have = dict(zip(names, refs))
        main_kernel(d, list(have), *have.values())

    results = pl.pallas_call(
        kernel,
        out_shape=[jax.ShapeDtypeStruct(shape, dtype) for shape, dtype, _ in outs.values()],
        in_specs=[spec for _, spec in ins.values()],
        out_specs=[spec for _, _, spec in outs.values()],
        scratch_shapes=list(scratch.values()),
        compiler_params=pltpu.CompilerParams(
            collective_id=0, has_side_effects=True, vmem_limit_bytes=63 * 1024 * 1024
        ),
        name="block_step",
    )(*[array for array, _ in ins.values()])
    got = dict(zip(outs, results))

    params = [
        up_weight,
        up_moment,
        up_square,
        down_weight,
        down_moment,
        down_square,
        spatial_weight,
        spatial_moment,
        spatial_square,
        small_params.reshape(d.ks, LANES),
        small_moment.reshape(d.ks, LANES),
        small_square.reshape(d.ks, LANES),
    ]
    passed = [got["up_low"], got["down_low"], got["sp_low"], got["gsmall"], *params]
    count = len(passed)
    updated = pl.pallas_call(
        functools.partial(adam_kernel, d, count),
        out_shape=[jax.ShapeDtypeStruct((1, 1), f32)]
        + [jax.ShapeDtypeStruct(got[name].shape, bf16) for name in ("out", "ig")]
        + [jax.ShapeDtypeStruct(p.shape, f32) for p in params],
        in_specs=[vmem_spec] + [any_spec] * (2 + count),
        out_specs=[smem_spec] + [any_spec] * (2 + len(params)),
        scratch_shapes=[VMEM(p.shape, p.dtype) for p in passed]
        + [pltpu.SemaphoreType.DMA((2 + count + 12,)), VMEM((max(d.pu, d.pd, d.ps), LANES), f32)]
        + [VMEM(got[name].shape, bf16) for name in ("out", "ig")],
        compiler_params=pltpu.CompilerParams(vmem_limit_bytes=63 * 1024 * 1024),
        name="adam_step",
    )(got["norm"], got["out"], got["ig"], *passed)
    norm, out, ig = updated[:3]
    updated = list(updated[3:12]) + [p.reshape(-1) for p in updated[12:]]
    return (
        jnp.transpose(out, (1, 0, 2)),
        jnp.transpose(ig, (1, 0, 2)),
        norm.reshape(()),
        *updated,
    )


def solution(mesh):
    rows = P("rows", None)
    flat = P("rows")
    tokens = P("blk", "rows", None)
    return jax.shard_map(
        functools.partial(body, mesh),
        mesh=mesh,
        in_specs=(tokens, tokens, rows) + (rows,) * 9 + (flat,) * 3,
        out_specs=(tokens, tokens, P()) + (rows,) * 9 + (flat,) * 3,
        check_vma=False,
    )
```

```python
import functools
import math
import types

import jax
import jax.numpy as jnp
from jax import lax
from jax.experimental import pallas as pl
from jax.experimental.pallas import tpu as pltpu
from jax.sharding import PartitionSpec as P

STEP = 10

beta_one = 0.9
beta_two = 0.999
max_norm = 1.0
weight_rate = 0.05
small_rate = 0.5
weight_decay = 0.01

MESH = pl.DeviceIdType.MESH
VMEM = pltpu.VMEM
bf16 = jnp.bfloat16
f32 = jnp.float32
LANES = 128


def loop(count, body):
    def step(i, carry):
        body(i)
        return carry

    lax.fori_loop(0, count, step, 0)


def span(start, size):
    return pl.ds(pl.multiple_of(start, size), size)


def rows_of(value, count):
    return jnp.concatenate([value] * (count // value.shape[0]), axis=0)


def lanes_of(value, count):
    return jnp.concatenate([value] * (count // value.shape[1]), axis=1)


def fold_rows(value):
    total = value[0:8]
    for first in range(8, value.shape[0], 8):
        total = total + value[first : first + 8]
    return total


def fold_lanes(value):
    total = value[:, 0:LANES]
    for first in range(LANES, value.shape[1], LANES):
        total = total + value[:, first : first + LANES]
    return total


def dot_nn(a, b):
    return lax.dot_general(a, b, (((1,), (0,)), ((), ())), preferred_element_type=f32)


def dot_nt(a, b):
    return lax.dot_general(a, b, (((1,), (1,)), ((), ())), preferred_element_type=f32)


def dot_tn(a, b):
    return lax.dot_general(a, b, (((0,), (0,)), ((), ())), preferred_element_type=f32)


def plan_of(mesh, shapes):
    d = types.SimpleNamespace()
    d.R = mesh.shape["rows"]
    d.minor = 1
    while d.minor * d.minor * 2 <= d.R:
        d.minor *= 2
    if d.minor * d.minor > d.R:
        d.minor //= 2
    d.major = d.R // d.minor
    d.block, d.rows_here, d.D = shapes["inputs"]
    d.S = d.block * mesh.shape["blk"]
    d.H = d.S // 2
    d.T = d.S + d.H
    d.FF = shapes["up"][1]
    d.G = d.FF // 2
    d.su, d.sd, d.ss = shapes["up"][0], shapes["down"][0], shapes["spatial"][0]
    d.ks = shapes["small"][0] // LANES
    d.nsmall = d.ks * d.R * LANES
    d.pair = 1
    while any(size * d.pair % 16 for size in (d.su, d.sd, d.ss)):
        d.pair *= 2
    d.minor = d.minor // d.pair
    d.pu, d.pd, d.ps = (size * d.pair for size in (d.su, d.sd, d.ss))
    d.CH = 512 if d.G % 512 == 0 else d.G
    d.chunks = d.G // d.CH
    d.split = d.R <= 16
    d.down_parts = 3 if d.pd % 48 == 0 else 1
    d.o_gain_in = 0
    d.o_shift_in = d.D
    d.o_bias_up = 2 * d.D
    d.o_gain_gate = d.o_bias_up + d.FF
    d.o_shift_gate = d.o_gain_gate + d.G
    d.o_bias_spatial = d.o_shift_gate + d.G
    d.o_bias_down = d.o_bias_spatial + d.S
    return d


class Comm:
    def __init__(self, send, recv, space):
        self.send, self.recv, self.space = send, recv, space
        self.sends, self.recvs, self.open = 0, 0, []

    def outgoing(self):
        made = Outgoing(self, self.send.at[self.sends])
        self.sends += 1
        self.open.append(made)
        return made

    def group(self, out=None):
        made = Group(self, out or self.outgoing(), self.recv.at[self.recvs])
        self.recvs += 1
        return made

    def wait(self, sem, size):
        cols = LANES
        while size // cols > self.space.shape[0]:
            cols += LANES
            while size % (cols * 16):
                cols += LANES
        ref = self.space.at[0 : size // cols, 0:cols]
        pltpu.make_async_copy(ref, ref, sem).wait()

    def finish(self):
        for made in self.open:
            self.wait(made.sem, made.size)


class Outgoing:
    def __init__(self, comm, sem):
        self.comm, self.sem, self.size = comm, sem, 0


class Group:
    def __init__(self, comm, out, sem):
        self.comm, self.out, self.sem, self.size = comm, out, sem, 0

    def start(self, src, dst, device):
        size = math.prod(src.shape) * (2 if src.dtype == f32 else 1)
        self.size += size
        self.out.size += size
        pltpu.make_async_remote_copy(
            src_ref=src,
            dst_ref=dst,
            send_sem=self.out.sem,
            recv_sem=self.sem,
            device_id=device,
            device_id_type=MESH,
        ).start()
        return self

    def wait(self):
        self.comm.wait(self.sem, self.size)


class Gather:
    def __init__(self, net, ref, s, first, width, by_y, fill):
        self.net, self.ref, self.s, self.first = net, ref, s, first
        self.half, self.by_y, self.fill = width // 2, by_y, fill
        self.size = self.half // 2 if by_y else self.half
        self.out = net.comm.outgoing()
        self.z, self.x, self.core = (net.comm.group(self.out) for _ in range(3))
        if by_y:
            self.y = net.comm.group(self.out)

    def region(self, owner, of_y=None):
        start = self.first + self.net.c * self.half
        if self.by_y:
            start = start + (self.net.y if of_y is None else of_y) * self.size
        cols = pl.ds(pl.multiple_of(start, LANES), self.size)
        return self.ref.at[span(owner * self.s, self.s), cols]

    def owner(self, dz, dx):
        n = self.net
        return lax.rem(n.zi - dz + n.major, n.major) * n.minor + lax.rem(n.xi - dx + n.minor, n.minor)

    def begin(self):
        n = self.net
        self.fill()
        mine = self.region(n.zi * n.minor + n.xi)
        for dz in range(1, n.major):
            self.z.start(mine, mine, n.at_z(dz))
        for dx in range(1, n.minor):
            self.x.start(mine, mine, n.at_x(dx))

    def onward(self, piece):
        if self.by_y:
            self.y.start(piece, piece, self.net.across)
        self.core.start(piece, piece, self.net.sibling)

    def minor(self):
        n = self.net
        self.z.wait()
        pieces = [self.region(self.owner(dz, 0)) for dz in range(1, n.major)]
        for piece in pieces:
            for dx in range(1, n.minor):
                self.x.start(piece, piece, n.at_x(dx))
        for piece in pieces:
            self.onward(piece)

    def last(self):
        n = self.net
        self.x.wait()
        for dz in range(n.major):
            for dx in range(1, n.minor):
                self.onward(self.region(self.owner(dz, dx)))

    def swap(self):
        n = self.net
        if self.by_y:
            self.y.wait()
            for dz in range(n.major):
                for dx in range(n.minor):
                    if dz or dx:
                        piece = self.region(self.owner(dz, dx), 1 - n.y)
                        self.core.start(piece, piece, n.sibling)

    def end(self):
        self.core.wait()


class Reduce:
    def __init__(self, net, part, rows, first, width, route, bufs, low):
        self.net, self.part, self.rows, self.first, self.route = net, part, rows, first, route
        self.half, self.quarter = width // 2, width // 4
        self.core, self.bufs, self.low = bufs[0], bufs[1:], low
        self.step, self.out = 0, net.comm.outgoing()

    def send(self, copies):
        self.waits = self.net.comm.group(self.out)
        for copy in copies:
            self.waits.start(*copy)

    def cols(self, start, size):
        return pl.ds(pl.multiple_of(self.first + start, LANES), size)

    def start(self):
        n, half = self.net, self.half
        src = self.part.at[:, :, self.rows, self.cols((1 - n.c) * half, half)]
        self.send([(src, self.core, n.sibling)])

    def advance(self):
        n = self.net
        self.waits.wait()
        if self.step == 0:
            mine = self.cols(n.c * self.half, self.half)
            self.zs, self.xs, self.width = n.major, n.minor, self.half

            def add(i, j):
                self.core[i, j] = self.part[i, j, self.rows, mine] + self.core[i, j]

            self.blocks(add)
            self.now = self.core
        else:
            kept, got = self.kept, self.got
            made = self.bufs[2 * self.step - 1]

            def add(i, j):
                if len(got) == 1:
                    made[i, j] = kept(i, j) + got[0][i, j]
                    return
                value = kept(i, j).astype(f32)
                for ref in got:
                    value = value + ref[i, j].astype(f32)
                made[i, j] = value.astype(made.dtype)

            self.blocks(add)
            self.now = made
        if self.step == len(self.route):
            return self.share()
        axis = self.route[self.step]
        now, into = self.now, self.bufs[2 * self.step]
        self.step += 1
        if axis == "x":
            self.send(
                (now.at[:, pl.ds(lax.rem(n.xi + dx, n.minor), 1)], into.at[dx - 1], n.at_x(dx))
                for dx in range(1, n.minor)
            )
            self.got = [into.at[dx - 1] for dx in range(1, n.minor)]
            self.kept = lambda i, j: now[i, n.xi]
            self.xs = 1
        elif axis == "z":
            self.send(
                (now.at[pl.ds(lax.rem(n.zi + dz, n.major), 1)], into.at[dz - 1], n.at_z(dz))
                for dz in range(1, n.major)
            )
            self.got = [into.at[dz - 1] for dz in range(1, n.major)]
            self.kept = lambda i, j: now[n.zi, j]
            self.zs = 1
        elif axis == "p":
            self.send((now, into.at[dp - 1], n.at_pair(dp)) for dp in range(1, n.pair))
            self.got = [into.at[dp - 1] for dp in range(1, n.pair)]
            self.kept = lambda i, j: now[i, j]
        else:
            width = self.width // 2
            theirs = pl.ds(pl.multiple_of((1 - n.y) * width, LANES), width)
            mine = pl.ds(pl.multiple_of(n.y * width, LANES), width)
            self.send([(now.at[:, :, :, theirs], into.at[0], n.across)])
            self.got = [into.at[0]]
            self.kept = lambda i, j: now[i, j, :, mine]
            self.width = width

    def blocks(self, add):
        zs, xs = self.zs, self.xs
        if zs * xs == 1:
            add(0, 0)
        else:
            loop(zs * xs, lambda i: add(i // xs, lax.rem(i, xs)))

    def share(self):
        n, mine = self.net, self.now.at[0, 0]
        self.local = pltpu.make_async_copy(mine, self.low.at[n.b], n.local_sem())
        self.local.start()
        self.send((mine, self.low.at[n.b], (n.r, lax.rem(n.b + db, 4))) for db in range(1, 4))
        kept = self.now[0, 0].astype(f32)
        return fold_lanes(fold_rows(kept * kept))

    def end(self):
        self.local.wait()
        self.waits.wait()


def reduce_shapes(d, width, s, route):
    zs, xs, wide = d.major, d.minor, width // 2
    shapes = [(zs, xs, s, wide)]
    for axis in route:
        if axis == "x":
            count, xs = max(d.minor - 1, 1), 1
        elif axis == "z":
            count, zs = max(d.major - 1, 1), 1
        elif axis == "p":
            count = d.pair - 1
        else:
            count, wide = 1, wide // 2
        shapes.append((count, zs, xs, s, wide))
        shapes.append((zs, xs, s, wide))
    return shapes


def main_kernel(d, names, *refs):
    k = types.SimpleNamespace(**dict(zip(names, refs)))
    comm = Comm(k.send_sem, k.recv_sem, k.GATE)
    r, b = lax.axis_index("rows"), lax.axis_index("blk")
    line = d.minor * d.pair
    zi, xi, xp = r // line, lax.rem(r, line) // d.pair, lax.rem(r, d.pair)
    y, c = b // 2, lax.rem(b, 2)
    S, H, T, D, G, FF, CH = d.S, d.H, d.T, d.D, d.G, d.FF, d.CH
    blk = d.block
    sibling = (r, 2 * y + 1 - c)
    across = (r, 2 * (1 - y) + c)

    def at_z(dz):
        return (lax.rem(zi + dz, d.major) * line + xi * d.pair + xp, b)

    def at_x(dx):
        return (zi * line + lax.rem(xi + dx, d.minor) * d.pair + xp, b)

    def at_pair(dp):
        return (zi * line + xi * d.pair + lax.rem(xp + dp, d.pair), b)

    used = [0]

    def local_sem():
        used[0] += 1
        return k.local_sem.at[used[0] - 1]

    net = types.SimpleNamespace(
        comm=comm, r=r, b=b, zi=zi, xi=xi, y=y, c=c, major=d.major, minor=d.minor,
        sibling=sibling, across=across, at_z=at_z, at_x=at_x, at_pair=at_pair, pair=d.pair, local_sem=local_sem,
    )

    barrier = pltpu.get_barrier_semaphore()
    for dr in range(1, d.R):
        pl.semaphore_signal(barrier, inc=1, device_id=(lax.rem(r + dr, d.R), b), device_id_type=MESH)
    for db in range(1, 4):
        pl.semaphore_signal(barrier, inc=1, device_id=(r, lax.rem(b + db, 4)), device_id_type=MESH)

    own = {}
    for name, rows in (("small", d.ks), ("up", d.su), ("sp", d.ss), ("down", d.sd)):
        stage = getattr(k, name + "_stage")
        if name != "small":
            stage = stage.at[span(xp * rows, rows)]
        own[name] = pltpu.make_async_copy(getattr(k, name + "_w"), stage, local_sem())
        own[name].start()

    def staged(name):
        own[name].wait()

    def share_pair():
        if d.pair == 1:
            return
        made = comm.group()
        for name, rows in (("up", d.su), ("sp", d.ss), ("down", d.sd)):
            mine = getattr(k, name + "_stage").at[span(xp * rows, rows)]
            for dp in range(1, d.pair):
                made.start(mine, mine, at_pair(dp))
        made.wait()

    def gather(name, ref, s, first, width, by_y):
        stage = getattr(k, name + "_stage")

        def fill():
            cols = slice(first, first + width)
            ref[span((zi * d.minor + xi) * s, s), cols] = stage[:, cols].astype(bf16)

        return Gather(net, ref, s, first, width, by_y, fill)

    def flow_of(name, i, by_y):
        if name == "ug" or name == "uc":
            step = CH if d.split else G
            return gather("up", k.UP, d.pu, (G if name == "ug" else 0) + i * step, step, by_y)
        if name == "sp":
            return gather("sp", k.SP, d.ps, 0, S, by_y)
        step = D // 2 if d.split else D
        return gather("down", k.DOWN, d.pd, i * step, step, by_y)

    flow = [flow_of(*one) for one in (FLOW if d.split else WHOLE_FLOW)]

    tokens = []
    for source, target in ((k.x_in, k.X), (k.c_in, k.C)):
        moves = []
        for g in range(4):
            moves.append((source.at[(g // 2) * 3 + g % 2], target.at[span(b * blk, blk), :], g))
        for half in range(2):
            moves.append((source.at[half * 3 + 2], target.at[span(S + c * blk, blk), :], 2 * half + y))
        tokens.append((moves, target))

    def send_blocks(moves, send, recv):
        for src, dst, g in moves:

            @pl.when(g == b)
            def _():
                pltpu.make_async_copy(src, dst, recv).start()

            @pl.when(g != b)
            def _():
                pltpu.make_async_remote_copy(
                    src_ref=src, dst_ref=dst, send_sem=send, recv_sem=recv, device_id=(r, g), device_id_type=MESH
                ).start()

    def sent_blocks(send):
        for here, count in ((y == c, 4), (y != c, 5)):

            @pl.when(here)
            def _():
                space = k.X.at[0 : count * blk, :]
                pltpu.make_async_copy(space, space, send).wait()

    def start_tokens(number):
        send_blocks(tokens[number][0], k.token_sem.at[number], k.token_sem.at[2 + number])

    def wait_tokens(number):
        target = tokens[number][1]
        pltpu.make_async_copy(target, target, k.token_sem.at[2 + number]).wait()

    def finish_tokens():
        for number in range(2):
            sent_blocks(k.token_sem.at[number])

    small_in = comm.group()

    def send_small():
        k.small_get[r] = jnp.zeros((8, LANES), f32)
        k.small_get[r, 0 : d.ks, :] = k.small_stage[...].astype(bf16).astype(f32)
        for dr in range(1, d.R):
            mine = k.small_get.at[r]
            small_in.start(mine, mine, (lax.rem(r + dr, d.R), b))

    def take_small():
        small_in.wait()
        for i in range(d.R):
            for j in range(d.ks):
                first = (i * d.ks + j) * LANES
                k.SM[:, first : first + LANES] = jnp.broadcast_to(k.small_get[i, j : j + 1, :], (8, LANES))

    def small(offset, width, rows):
        return rows_of(k.SM[:, offset : offset + width], rows)

    def label_of(places, ends, source):
        label = jnp.zeros(places.shape, f32)
        for end in ends:
            label = label + jnp.where(places >= end, 1.0, 0.0)
        if source:
            label = jnp.where(places < ends[-1], label, -1.0)
        return label

    lengths_copy = pltpu.make_async_copy(k.lengths_in, k.lengths, local_sem())
    lengths_copy.start()

    def make_labels():
        lengths_copy.wait()
        for which, row in enumerate((3 * y + c, 3 * y + 2)):
            ends = [k.lengths[0, row]]
            for n in range(1, k.lengths.shape[0]):
                ends.append(ends[-1] + k.lengths[n, row])
            lane = lax.broadcasted_iota(jnp.int32, (8, S), 1)
            k.row_t[which] = label_of(lane, ends, False)
            k.row_s[which] = label_of(lane, ends, True)
            for first in range(0, S, 64):
                place = lax.broadcasted_iota(jnp.int32, (64, LANES), 0) + first
                k.col_t[which, first : first + 64, :] = label_of(place, ends, False)
                k.col_s[which, first : first + 64, :] = label_of(place, ends, True)

    def make_mixing():
        k.FA[0:S, :] = k.SP[...].astype(f32)
        k.FB[0:S, :] = jnp.transpose(k.FA[0:S, :])

        def body(i):
            rows = span(i * 32, 32)
            keep = lanes_of(k.col_t[0, rows, :], S) == rows_of(k.row_s[0], 32)
            k.M[rows, :] = jnp.where(keep, k.FA[rows, :], 0.0).astype(bf16)
            keep = lanes_of(k.col_s[0, rows, :], S) == rows_of(k.row_t[0], 32)
            k.MT[rows, :] = jnp.where(keep, k.FB[rows, :], 0.0).astype(bf16)

        loop(S // 32, body)

        def shared(i):
            rows = span(c * H + i * 32, 32)
            keep = lanes_of(k.col_t[1, rows, :], S) == rows_of(k.row_s[1], 32)
            k.M[span(S + i * 32, 32), :] = jnp.where(keep, k.FA[rows, :], 0.0).astype(bf16)

        loop(H // 32, shared)
        own_half = pl.ds(pl.multiple_of(c * H, H), H)

        def turned(i):
            rows = span(i * 32, 32)
            keep = lanes_of(k.col_s[1, rows, :], H) == rows_of(k.row_t[1, :, own_half], 32)
            k.MTB[rows, :] = jnp.where(keep, k.FB[rows, own_half], 0.0).astype(bf16)

        loop(S // 32, turned)
        bias = k.SM[:, d.o_bias_spatial : d.o_bias_spatial + S]
        k.BS[0:S, :] = jnp.transpose(rows_of(bias, LANES))
        k.BS[S:T, :] = k.BS[span(c * H, H), :]

    def row_mean(ref, first, count, width, finish):
        def body(i):
            rows = span(first + i * 128, 128)
            total = jnp.sum(ref[rows, :], axis=1, keepdims=True) * (1.0 / width)
            ref[rows, :] = jnp.broadcast_to(finish(total), (128, LANES))

        loop(count // 128, body)

    def scale_of(spread):
        return lax.rsqrt(spread + 1e-05)

    def input_norm(at, count):
        def sums(i):
            rows = span(at + i * 64, 64)
            k.MU[rows, :] = fold_lanes(k.X[rows, :].astype(f32))

        loop(count // 64, sums)
        row_mean(k.MU, at, count, D, lambda v: v)

        def spreads(i):
            rows = span(at + i * 64, 64)
            centred = k.X[rows, :].astype(f32) - lanes_of(k.MU[rows, :], D)
            k.RX[rows, :] = fold_lanes(centred * centred)

        loop(count // 64, spreads)
        row_mean(k.RX, at, count, D, scale_of)

        def body(i):
            rows = span(at + i * 64, 64)
            centred = k.X[rows, :].astype(f32) - lanes_of(k.MU[rows, :], D)
            normed = centred * lanes_of(k.RX[rows, :], D)
            normed = normed * small(d.o_gain_in, D, 64) + small(d.o_shift_in, D, 64)
            k.N[rows, :] = normed.astype(bf16)

        loop(count // 64, body)

    def turn_normed():
        k.NT[...] = jnp.transpose(k.N[...].astype(f32)).astype(bf16)

    def gelu_parts(before):
        cdf = 0.5 + 0.5 * lax.erf(before * 0.7071067811865476)
        bell = jnp.exp(before * before * -0.5)
        return before * cdf, cdf + before * bell * 0.3989422804014327

    def up_gate(j):
        cols = slice(j * CH, (j + 1) * CH)
        at = G + j * CH
        k.F[:, cols] = dot_nn(k.N[...], k.UP[:, at : at + CH])
        bias = small(d.o_bias_up + at, CH, 16)
        for first in range(0, T, 16):
            rows = slice(first, first + 16)
            active, slope = gelu_parts(k.F[rows, cols] + bias)
            k.F[rows, cols] = active
            k.DG[rows, cols] = slope.astype(bf16)
            total = fold_lanes(active)
            k.S1[rows, :] = total if j == 0 else k.S1[rows, :] + total

    def gate_norm(first_row, count, place):
        row_mean(k.S1, first_row, count, G, lambda v: v)

        def spreads(i):
            rows = span(first_row + i * 32, 32)
            centred = k.F[rows, :] - lanes_of(k.S1[rows, :], G)
            k.RG[rows, :] = fold_lanes(centred * centred)

        loop(count // 32, spreads)
        row_mean(k.RG, first_row, count, G, scale_of)

        def body(i):
            rows = span(first_row + i * 32, 32)
            xhat = (k.F[rows, :] - lanes_of(k.S1[rows, :], G)) * lanes_of(k.RG[rows, :], G)
            k.XH[rows, :] = xhat.astype(bf16)
            gate = xhat * small(d.o_gain_gate, G, 32) + small(d.o_shift_gate, G, 32)
            k.GATE[span(place + i * 32, 32), :] = gate.astype(bf16)

        loop(count // 32, body)

    def up_content(j):
        cols = slice(j * CH, (j + 1) * CH)
        k.FA[...] = dot_nn(k.N[...], k.UP[:, cols])
        bias = small(d.o_bias_up + j * CH, CH, 16)
        for first in range(0, T, 16):
            rows = slice(first, first + 16)
            active, slope = gelu_parts(k.FA[rows, :] + bias)
            k.CT[rows, cols] = active.astype(bf16)
            k.DC[rows, cols] = slope.astype(bf16)

    def mix(j):
        cols = slice(j * CH, (j + 1) * CH)
        k.FA[0:S, :] = dot_nn(k.M[0:S, :], k.GATE[0:S, cols])
        k.FA[S:T, :] = dot_nn(k.M[S:T, :], k.GATE[S : 2 * S, cols])
        k.FB[...] = dot_nt(k.C[...], k.DOWN[cols, :])
        total = jnp.zeros((8, CH), f32)
        for first in range(0, T, 16):
            rows = slice(first, first + 16)
            out = k.FA[rows, :] + lanes_of(k.BS[rows, :], CH)
            grad = k.FB[rows, :]
            content = k.CT[rows, cols].astype(f32)
            k.PR[rows, cols] = (content * out).astype(bf16)
            grad_spatial = (grad * content).astype(bf16)
            k.GS[rows, cols] = grad_spatial
            along = fold_lanes(grad_spatial.astype(f32))
            k.BSA[rows, :] = along if j == 0 else k.BSA[rows, :] + along
            before = (grad * out * k.DC[rows, cols].astype(f32)).astype(bf16)
            k.GB[rows, cols] = before
            total = total + fold_rows(before.astype(f32))
        k.SG[:, d.o_bias_up + j * CH : d.o_bias_up + (j + 1) * CH] = total

    def project(i):
        rows = slice(i * 2 * blk, (i + 1) * 2 * blk)
        k.FA[rows, 0:D] = dot_nn(k.PR[rows, :], k.DOWN[...])
        for first in range(i * 2 * blk, (i + 1) * 2 * blk, 16):
            part = slice(first, first + 16)
            value = k.FA[part, 0:D] + small(d.o_bias_down, D, 16) + k.X[part, :].astype(f32)
            k.OT[part, :] = value.astype(bf16)

    def grad_down():
        step = d.pd * max(1, 384 // d.pd)
        for first in range(0, G, step):
            size = min(step, G - first)
            value = dot_tn(k.PR[:, first : first + size], k.C[...])
            for owner in range(first // d.pd, (first + size) // d.pd):
                at = owner * d.pd - first
                k.PD[owner // d.minor, owner % d.minor] = value[at : at + d.pd].astype(k.PD.dtype)

    def grad_up(first):
        cols = slice(first, first + CH)
        value = dot_nn(k.NT[...], k.GB[:, cols])
        k.PU[:, :, :, cols] = value.reshape(d.major, d.minor, d.pu, CH).astype(k.PU.dtype)

    def grad_spatial_weight():
        k.FA[0:S, 0:S] = dot_nt(k.GS[0:S, :], k.GATE[0:S, :])
        k.FB[0:H, 0:S] = dot_nt(k.GS[S:T, :], k.GATE[S : 2 * S, :])

        def body(i):
            rows = span(i * 32, 32)
            keep = lanes_of(k.col_t[0, rows, :], S) == rows_of(k.row_s[0], 32)
            k.FA[rows, 0:S] = jnp.where(keep, k.FA[rows, 0:S], 0.0)

        loop(S // 32, body)

        def shared(i):
            rows = span(c * H + i * 32, 32)
            keep = lanes_of(k.col_t[1, rows, :], S) == rows_of(k.row_s[1], 32)
            k.FA[rows, 0:S] = k.FA[rows, 0:S] + jnp.where(keep, k.FB[span(i * 32, 32), 0:S], 0.0)

        loop(H // 32, shared)
        k.PS[...] = k.FA[0:S, 0:S].reshape(d.major, d.minor, d.ps, S).astype(k.PS.dtype)

    def grad_gate_shared():
        other = span((1 - c) * H, H)
        for j in range(d.chunks):
            cols = slice(j * CH, (j + 1) * CH)
            k.GX[:, cols] = dot_nn(k.MTB[other, :], k.GS[S:T, cols]).astype(bf16)
        return comm.group().start(k.GX, k.GY, sibling)

    def gate_terms(rows, cols, grad, j, sums):
        xhat = k.XH[rows, cols].astype(f32)
        product = grad * xhat
        gain = small(d.o_gain_gate + j * CH, CH, 16)
        one, two = fold_lanes(grad * gain), fold_lanes(product * gain)
        k.S1[rows, :] = one if j == 0 else k.S1[rows, :] + one
        k.S2[rows, :] = two if j == 0 else k.S2[rows, :] + two
        return sums[0] + fold_rows(product), sums[1] + fold_rows(grad)

    def grad_gate(j):
        cols = slice(j * CH, (j + 1) * CH)
        mine = span(c * H, H)
        k.F[S:T, cols] = dot_nn(k.MTB[mine, :], k.GS[S:T, cols])
        k.F[0:S, cols] = dot_nn(k.MT[...], k.GS[0:S, cols])
        sums = (jnp.zeros((8, CH), f32), jnp.zeros((8, CH), f32))
        for first in range(0, S, 16):
            rows = slice(first, first + 16)
            sums = gate_terms(rows, cols, k.F[rows, cols], j, sums)
        for offset, total in zip((d.o_gain_gate, d.o_shift_gate), sums):
            k.SG[:, offset + j * CH : offset + (j + 1) * CH] = total

    def grad_gate_other(j):
        cols = slice(j * CH, (j + 1) * CH)
        sums = (jnp.zeros((8, CH), f32), jnp.zeros((8, CH), f32))
        for first in range(S, T, 16):
            rows = slice(first, first + 16)
            grad = k.F[rows, cols] + k.GY[first - S : first - S + 16, cols].astype(f32)
            k.F[rows, cols] = grad
            sums = gate_terms(rows, cols, grad, j, sums)
        for offset, total in zip((d.o_gain_gate, d.o_shift_gate), sums):
            at = slice(offset + j * CH, offset + (j + 1) * CH)
            k.SG[:, at] = k.SG[:, at] + total

    def gate_back(j):
        cols = slice(j * CH, (j + 1) * CH)
        gain = small(d.o_gain_gate + j * CH, CH, 16)
        total = jnp.zeros((8, CH), f32)
        for first in range(0, T, 16):
            rows = slice(first, first + 16)
            scaled = k.F[rows, cols] * gain - lanes_of(k.S1[rows, :], CH)
            back = scaled - k.XH[rows, cols].astype(f32) * lanes_of(k.S2[rows, :], CH)
            back = back * lanes_of(k.RG[rows, :], CH)
            before = (back * k.DG[rows, cols].astype(f32)).astype(bf16)
            k.GB[rows, G + j * CH : G + (j + 1) * CH] = before
            total = total + fold_rows(before.astype(f32))
        k.SG[:, d.o_bias_up + G + j * CH : d.o_bias_up + G + (j + 1) * CH] = total

    def grad_normed(i):
        rows = slice(i * 2 * blk, (i + 1) * 2 * blk)
        k.FB[rows, 0:D] = dot_nt(k.GB[rows, :], k.UP[...])

    def input_back(which):
        at = which * 2 * blk

        def parts(rows):
            xhat = (k.X[rows, :].astype(f32) - lanes_of(k.MU[rows, :], D)) * lanes_of(k.RX[rows, :], D)
            grad = k.FB[rows, 0:D]
            return xhat, grad, grad * small(d.o_gain_in, D, 64)

        def sums(i):
            rows = span(at + i * 64, 64)
            xhat, grad, scaled = parts(rows)
            k.S1[rows, :] = fold_lanes(scaled)
            k.S2[rows, :] = fold_lanes(scaled * xhat)

        loop(2 * blk // 64, sums)
        row_mean(k.S1, at, 2 * blk, D, lambda v: v)
        row_mean(k.S2, at, 2 * blk, D, lambda v: v)
        if which == 0:
            for offset in (d.o_gain_in, d.o_shift_in, d.o_bias_down):
                k.SG[:, offset : offset + D] = jnp.zeros((8, D), f32)

        def body(i):
            rows = span(at + i * 64, 64)
            xhat, grad, scaled = parts(rows)
            cot = k.C[rows, :].astype(f32)
            back = scaled - lanes_of(k.S1[rows, :], D) - xhat * lanes_of(k.S2[rows, :], D)
            k.IT[rows, :] = (back * lanes_of(k.RX[rows, :], D) + cot).astype(bf16)
            for offset, term in ((d.o_gain_in, grad * xhat), (d.o_shift_in, grad), (d.o_bias_down, cot)):
                k.SG[:, offset : offset + D] = k.SG[:, offset : offset + D] + fold_rows(term)

        loop(2 * blk // 64, body)

    back = []
    for source, target in ((k.OT, k.out), (k.IT, k.ig)):
        moves = []
        for g in range(4):
            moves.append((source.at[g * blk : (g + 1) * blk, :], target.at[3 * y + c], g))
        for half in range(2):
            here = source.at[S + half * blk : S + (half + 1) * blk, :]
            moves.append((here, target.at[3 * y + 2], 2 * c + half))
        back.append((moves, target))

    def start_back(number, part):
        moves = back[number][0][2 * part : 2 * part + 2]
        send_blocks(moves, k.token_sem.at[4 + number], k.token_sem.at[6 + number])

    def finish_back():
        for number in range(2):
            target = back[number][1]
            pltpu.make_async_copy(target, target, k.token_sem.at[6 + number]).wait()
            sent_blocks(k.token_sem.at[4 + number])

    def reduce(name, part, rows, first, width, low):
        route = d.routes[name]
        bufs = [getattr(k, "%s_%d" % (name, i)) for i in range(1 + 2 * len(route))]
        return Reduce(net, part, rows, first, width, route, bufs, low)

    red = {}
    for j in range(d.chunks):
        rows = slice(0, d.pu)
        red["uc%d" % j] = reduce("uc%d" % j, k.PU, rows, j * CH, CH, k.up_low.at[j])
        red["ug%d" % j] = reduce("ug%d" % j, k.PU, rows, G + j * CH, CH, k.up_low.at[d.chunks + j])
    size = d.pd // d.down_parts
    for j in range(d.down_parts):
        rows = slice(j * size, (j + 1) * size)
        red["dn%d" % j] = reduce("dn%d" % j, k.PD, rows, 0, D, k.down_low.at[j])
    red["sp"] = reduce("sp", k.PS, slice(0, d.ps), 0, S, k.sp_low)

    def column_sums():
        bias = jnp.sum(jnp.transpose(k.BSA[...]), axis=0, keepdims=True)
        k.SG[:, d.o_bias_spatial : d.o_bias_spatial + S] = jnp.zeros((8, S), f32)
        k.SG[0:1, d.o_bias_spatial : d.o_bias_spatial + S] = bias[:, 0:S]
        place = pl.ds(pl.multiple_of(d.o_bias_spatial + c * H, H), H)
        k.SG[0:1, place] = k.SG[0:1, place] + bias[:, S:T]
        for i in range(d.nsmall // LANES):
            total = jnp.sum(k.SG[:, i * LANES : (i + 1) * LANES], axis=0, keepdims=True)
            k.small_part[i : i + 1, :] = total

    quarter = d.nsmall // LANES // 4

    def small_blk():
        made = comm.group()
        for db in range(1, 4):
            other = lax.rem(b + db, 4)
            part = k.small_part.at[span(other * quarter, quarter), :]
            made.start(part, k.small_one.at[db - 1], (r, other))
        return made

    def to_rows(ref):
        made = comm.group()
        for dr in range(1, d.R):
            made.start(ref.at[0], ref.at[dr], (lax.rem(r + dr, d.R), b))
        return made

    def to_blk(src, dst):
        made = comm.group()
        for db in range(1, 4):
            made.start(src, dst, (r, lax.rem(b + db, 4)))
        return made

    def small_rows(before):
        before.wait()
        value = k.small_part[span(b * quarter, quarter), :]
        for i in range(3):
            value = value + k.small_one[i]
        k.small_two[0] = value
        return to_rows(k.small_two)

    def small_share(before):
        before.wait()
        value = k.small_two[0]
        for dr in range(1, d.R):
            value = value + k.small_two[dr]
        k.small_sum[...] = value
        mine = k.gsmall.at[span(b * quarter, quarter), :]
        local = pltpu.make_async_copy(k.small_sum, mine, local_sem())
        local.start()
        return local, to_blk(k.small_sum, mine), fold_rows(value * value)

    schedule(d, types.SimpleNamespace(**locals()))


ORDER = (
    "b0", "b1", "sm", "b2", "m0", "b3", "m1", "b4", "b5", "T0", "t1", "n0", "b6", "l0", "n1", "b7", "m2", "n2",
    "l1", "m3", "e0", "G0", "m4", "e1", "G1", "b8", "m5", "tn", "m6", "l2", "l3", "l4", "e2", "G2", "gs", "l5",
    "m7", "T1", "ga", "l6", "gw", "m8", "w3", "l7", "w4", "e3", "c0", "e7", "w5", "e4", "c1", "w6", "e5", "c2",
    "l8", "e6", "mx", "e8", "x0", "u0", "x1", "uc0", "u1", "x2", "uc1", "u2", "gx", "gd", "uc0", "uc2", "uc1",
    "ow", "q0", "dn0", "dn1", "p0", "dn2", "p1", "q1", "uc2", "uc0", "q2", "ot", "dn1", "dn0", "uc1", "k0",
    "v0", "k1", "dn2", "uc2", "uc0", "v1", "ug0", "dn1", "uc1", "k2", "dn0", "ug1", "dn2", "v2", "uc2", "S",
    "ug2", "ug0", "dn1", "dn0", "dn2", "p2", "ug1", "sp", "r0", "r1", "ug2", "ug0", "r2", "sp", "i0", "ug1",
    "i1", "ug2", "ug0", "i2", "cs", "ug1", "sp", "ug2", "sr", "sp",
)


ROUTES = dict(dn0="xzy", dn1="yxz", dn2="xyz", sp="xyz", uc0="yzx", uc1="yzx", uc2="xzy", ug0="xzy", ug1="yzx", ug2="xyz")
FLOW = (("ug", 0, False), ("ug", 1, False), ("ug", 2, False), ("uc", 0, True), ("uc", 1, True), ("uc", 2, True), ("sp", 0, True), ("dn", 0, False), ("dn", 1, False))
WHOLE_FLOW = (("ug", 0, False), ("sp", 0, False), ("dn", 0, False), ("uc", 0, False))


def plain_order(d, groups):
    order = ["b0", "b1", "sm", "T0", "n0", "n1", "n2", "tn", "t1"]
    for i in range(groups):
        order += ["m%d" % i, "l%d" % i, "w%d" % i, "e%d" % i]
        if i + 2 < groups:
            order.append("b%d" % (i + 2))
    each = range(d.chunks)
    order += ["G%d" % j for j in each] + ["gs", "ga", "mx", "T1", "gw"]
    for j in each:
        order += ["c%d" % j, "x%d" % j, "u%d" % j]
    order += ["p0", "p1", "p2", "gx", "gd"] + ["q%d" % j for j in each] + ["ow", "ot"]
    for j in each:
        order += ["k%d" % j, "v%d" % j]
    order += ["S", "r0", "i0", "r1", "i1", "r2", "i2", "cs", "sr"]
    sums = [n + str(j) for n in ("uc", "ug") for j in each] + ["dn%d" % j for j in range(d.down_parts)] + ["sp"]
    return order + sums * (4 + (d.pair > 1))


def schedule(d, p):
    k, comm, flow, red = p.k, p.comm, p.flow, p.red
    chunks, r, b, G, CH = d.chunks, p.r, p.b, d.G, d.CH
    kept = {}
    squares = []
    steps = {}

    def step(name):
        def add(function):
            steps[name] = function

        return add

    for i, one in enumerate(flow):
        for letter, function in zip("bmlwe", (one.begin, one.minor, one.last, one.swap, one.end)):
            steps[letter + str(i)] = function
    for i in range(2):
        steps["t%d" % i] = functools.partial(p.start_tokens, i)
        steps["T%d" % i] = functools.partial(p.wait_tokens, i)
    steps["sm"] = p.take_small
    for i in range(3):
        steps["n%d" % i] = functools.partial(p.input_norm, 2 * d.block * i, 2 * d.block)
    for j in range(chunks):
        steps["G%d" % j] = functools.partial(p.up_gate, j)
        steps["c%d" % j] = functools.partial(p.up_content, j)
        steps["x%d" % j] = functools.partial(p.mix, j)
        steps["q%d" % j] = functools.partial(p.grad_gate, j)
        steps["k%d" % j] = functools.partial(p.gate_back, j)

    @step("gs")
    def _():
        p.gate_norm(d.S, d.H, d.S + p.c * d.H)
        mine = k.GATE.at[span(d.S + p.c * d.H, d.H), :]
        kept["gate"] = comm.group().start(mine, mine, p.sibling)

    steps["ga"] = functools.partial(p.gate_norm, 0, d.S, 0)
    steps["gw"] = lambda: kept["gate"].wait()
    steps["tn"] = p.turn_normed
    steps["mx"] = p.make_mixing

    def grad_up(j, name, first):
        p.grad_up(first + j * CH)
        red[name + str(j)].start()

    for j in range(chunks):
        steps["u%d" % j] = functools.partial(grad_up, j, "uc", 0)
        steps["v%d" % j] = functools.partial(grad_up, j, "ug", G)

    def project(i):
        p.project(i)
        p.start_back(0, i)

    def input_back(i):
        p.input_back(i)
        p.start_back(1, i)

    for i in range(3):
        steps["p%d" % i] = functools.partial(project, i)
        steps["r%d" % i] = functools.partial(p.grad_normed, i)
        steps["i%d" % i] = functools.partial(input_back, i)

    @step("gx")
    def _():
        kept["gradient"] = p.grad_gate_shared()

    @step("gd")
    def _():
        p.grad_down()
        for j in range(d.down_parts):
            red["dn%d" % j].start()

    steps["ow"] = lambda: kept["gradient"].wait()

    @step("ot")
    def _():
        for j in range(chunks):
            p.grad_gate_other(j)
        p.row_mean(k.S1, 0, d.T, G, lambda v: v)
        p.row_mean(k.S2, 0, d.T, G, lambda v: v)

    @step("S")
    def _():
        p.grad_spatial_weight()
        red["sp"].start()

    @step("cs")
    def _():
        p.column_sums()
        kept["small"] = p.small_blk()

    @step("sr")
    def _():
        kept["small"] = p.small_rows(kept["small"])

    def advance(one):
        value = one.advance()
        if value is not None:
            squares.append(value)

    for name, one in red.items():
        steps[name] = functools.partial(advance, one)

    for name in ("small", "up", "sp", "down"):
        p.staged(name)
    pl.semaphore_wait(p.barrier, d.R - 1 + 3)
    p.start_tokens(0)
    p.share_pair()
    p.send_small()
    steps["b0"]()
    steps["b1"]()
    p.make_labels()
    for name in (ORDER if d.split else plain_order(d, len(flow)))[2:]:
        steps[name]()
    small = kept["small"]
    total = squares[0]
    for value in squares[1:]:
        total = total + value
    k.norm_rows[0] = total
    norm_one = p.to_rows(k.norm_rows)
    local, shared, extra = p.small_share(small)
    norm_one.wait()
    value = extra
    for i in range(d.R):
        value = value + k.norm_rows[lax.rem(i - r + 2 * d.R, d.R)]
    k.norm_blk[b] = value
    norm_two = p.to_blk(k.norm_blk.at[b], k.norm_blk.at[b])
    for one in red.values():
        one.end()
    local.wait()
    shared.wait()
    norm_two.wait()
    value = k.norm_blk[0]
    for i in range(1, 4):
        value = value + k.norm_blk[i]
    k.norm[...] = jnp.sqrt(jnp.full((8, LANES), jnp.sum(value), f32))
    p.finish_back()
    p.finish_tokens()
    comm.finish()

def adam_kernel(d, count, *refs):
    norm, out_in, ig_in = refs[:3]
    given = refs[3 : 3 + count]
    norm_out, out, ig = refs[3 + count : 6 + count]
    results = refs[6 + count : 18 + count]
    held = refs[18 + count : 18 + 2 * count]
    sems, turned, held_out, held_ig = refs[18 + 2 * count :]
    r = lax.axis_index("rows")
    through = [
        (pltpu.make_async_copy(src, held, sems.at[i]), pltpu.make_async_copy(held, dst, sems.at[i]))
        for i, (src, held, dst) in enumerate(((out_in, held_out, out), (ig_in, held_ig, ig)))
    ]
    loads = [pltpu.make_async_copy(src, dst, sems.at[2 + i]) for i, (src, dst) in enumerate(zip(given, held))]
    for copy in loads + [first for first, _ in through]:
        copy.start()
    value = norm[...]
    norm_out[0, 0] = norm[0, 0]
    factor = jnp.minimum(1.0, max_norm / (value + 1e-06))
    low_up, low_down, low_sp, gsmall = held[:4]
    params = held[4:]
    stores = []

    def step(ins, grad, rate, decay, place):
        weight, moment, square = (ref[place] for ref in ins)
        grad = grad * factor[0:1, :]
        moment_next = beta_one * moment + (1.0 - beta_one) * grad
        square_next = beta_two * square + (1.0 - beta_two) * grad * grad
        moment_hat = moment_next / (1.0 - beta_one**STEP)
        square_hat = square_next / (1.0 - beta_two**STEP)
        update = moment_hat / (jnp.sqrt(square_hat) + 1e-08) + decay * weight
        for ref, result in zip(ins, (weight - rate * update, moment_next, square_next)):
            ref[place] = result

    def store(i):
        for j in range(3):
            n = 3 * i + j
            copy = pltpu.make_async_copy(params[n], results[n], sems.at[2 + count + n])
            copy.start()
            stores.append(copy)

    def part(low, q, first, s, width):
        start = first + (2 * (q % 2) + q // 2) * (width // 4)
        for at in range(0, width // 4, LANES):
            grad = low[q, :, at : at + LANES].astype(f32)
            if d.pair > 1:
                turned[0 : d.pair * s, :] = grad
                grad = turned[pl.ds(pl.multiple_of(lax.rem(r, d.pair) * s, s), s), :]
            yield grad, (slice(0, s), slice(start + at, start + at + LANES))

    for i in (3, 13, 14, 15):
        loads[i].wait()
    grad = gsmall[pl.ds(r * d.ks, d.ks), :]
    step(params[9:12], grad, small_rate, 0.0, (slice(0, d.ks), slice(0, LANES)))
    store(3)
    for i in (1, 7, 8, 9):
        loads[i].wait()
    for q in range(4):
        start = (2 * (q % 2) + q // 2) * (d.D // 4)
        size = d.pd // d.down_parts
        for at in range(0, d.D // 4, LANES):
            cols = slice(start + at, start + at + LANES)
            for i in range(d.down_parts):
                grad = low_down[i, q, :, at : at + LANES].astype(f32)
                if d.pair == 1:
                    step(params[3:6], grad, weight_rate, weight_decay, (slice(i * size, (i + 1) * size), cols))
                else:
                    turned[i * size : (i + 1) * size, :] = grad
            if d.pair > 1:
                grad = turned[pl.ds(pl.multiple_of(lax.rem(r, d.pair) * d.sd, d.sd), d.sd), :]
                step(params[3:6], grad, weight_rate, weight_decay, (slice(0, d.sd), cols))
    store(1)
    for i in (2, 10, 11, 12):
        loads[i].wait()
    for q in range(4):
        for grad, place in part(low_sp, q, 0, d.ss, d.S):
            step(params[6:9], grad, weight_rate, weight_decay, place)
    store(2)
    for first, second in through:
        first.wait()
        second.start()
        stores.append(second)
    for i in (0, 4, 5, 6):
        loads[i].wait()
    for j in range(2 * d.chunks):
        for q in range(4):
            for grad, place in part(low_up.at[j], q, j * d.CH, d.su, d.CH):
                step(params[0:3], grad, weight_rate, weight_decay, place)
    store(0)
    for copy in stores:
        copy.wait()


def body(mesh, *arrays):
    (
        inputs,
        cotangent,
        lengths,
        up_weight,
        up_moment,
        up_square,
        down_weight,
        down_moment,
        down_square,
        spatial_weight,
        spatial_moment,
        spatial_square,
        small_params,
        small_moment,
        small_square,
    ) = arrays
    d = plan_of(
        mesh,
        dict(
            inputs=inputs.shape,
            up=up_weight.shape,
            down=down_weight.shape,
            spatial=spatial_weight.shape,
            small=small_params.shape,
        ),
    )
    S, H, T, D, G, FF, R = d.S, d.H, d.T, d.D, d.G, d.FF, d.R
    wire = bf16
    small_rows = d.nsmall // LANES
    quarter = small_rows // 4

    any_spec = pl.BlockSpec(memory_space=pl.ANY)
    vmem_spec = pl.BlockSpec(memory_space=VMEM)
    smem_spec = pl.BlockSpec(memory_space=pltpu.SMEM)

    ins = dict(
        x_in=(jnp.transpose(inputs, (1, 0, 2)), any_spec),
        c_in=(jnp.transpose(cotangent, (1, 0, 2)), any_spec),
        lengths_in=(lengths.T, any_spec),
        up_w=(up_weight, any_spec),
        down_w=(down_weight, any_spec),
        sp_w=(spatial_weight, any_spec),
        small_w=(small_params.reshape(d.ks, LANES), any_spec),
    )
    outs = dict(
        out=((d.rows_here, d.block, D), bf16, any_spec),
        ig=((d.rows_here, d.block, D), bf16, any_spec),
        norm=((8, LANES), f32, vmem_spec),
        gsmall=((small_rows, LANES), f32, any_spec),
        up_low=((2 * d.chunks, 4, d.pu, d.CH // 4), wire, any_spec),
        down_low=((d.down_parts, 4, d.pd // d.down_parts, D // 4), wire, any_spec),
        sp_low=((4, d.ps, S // 4), wire, any_spec),
    )
    scratch = dict(
        lengths=pltpu.SMEM(lengths.T.shape, jnp.int32),
        up_stage=VMEM((d.pu, FF), f32),
        down_stage=VMEM((d.pd, D), f32),
        sp_stage=VMEM((d.ps, S), f32),
        small_stage=VMEM((d.ks, LANES), f32),
        small_get=VMEM((R, 8, LANES), f32),
        SM=VMEM((8, d.nsmall), f32),
        SG=VMEM((8, d.nsmall), f32),
        UP=VMEM((D, FF), bf16),
        DOWN=VMEM((G, D), bf16),
        SP=VMEM((S, S), bf16),
        X=VMEM((T, D), bf16),
        C=VMEM((T, D), bf16),
        N=VMEM((T, D), bf16),
        NT=VMEM((D, T), bf16),
        F=VMEM((T, G), f32),
        FA=VMEM((T, 512), f32),
        FB=VMEM((T, 512), f32),
        DG=VMEM((T, G), bf16),
        XH=VMEM((T, G), bf16),
        RG=VMEM((T, LANES), f32),
        GATE=VMEM((2 * S, G), bf16),
        CT=VMEM((T, G), bf16),
        DC=VMEM((T, G), bf16),
        PR=VMEM((T, G), bf16),
        GS=VMEM((T, G), bf16),
        GB=VMEM((T, FF), bf16),
        GX=VMEM((H, G), bf16),
        GY=VMEM((H, G), bf16),
        BS=VMEM((T, LANES), f32),
        BSA=VMEM((T, LANES), f32),
        M=VMEM((T, S), bf16),
        MT=VMEM((S, S), bf16),
        MTB=VMEM((S, H), bf16),
        row_t=VMEM((2, 8, S), f32),
        row_s=VMEM((2, 8, S), f32),
        col_t=VMEM((2, S, LANES), f32),
        col_s=VMEM((2, S, LANES), f32),
        OT=VMEM((T, D), bf16),
        IT=VMEM((T, D), bf16),
        PU=VMEM((d.major, d.minor, d.pu, FF), wire),
        PD=VMEM((d.major, d.minor, d.pd, D), wire),
        PS=VMEM((d.major, d.minor, d.ps, S), wire),
        MU=VMEM((T, LANES), f32),
        RX=VMEM((T, LANES), f32),
        S1=VMEM((T, LANES), f32),
        S2=VMEM((T, LANES), f32),
        small_sum=VMEM((quarter, LANES), f32),
        small_part=VMEM((small_rows, LANES), f32),
        small_one=VMEM((3, quarter, LANES), f32),
        small_two=VMEM((R, quarter, LANES), f32),
        norm_rows=VMEM((R, 8, LANES), f32),
        norm_blk=VMEM((4, 8, LANES), f32),
    )
    sizes = {"sp": (S, d.ps)}
    for j in range(d.down_parts):
        sizes["dn%d" % j] = (D, d.pd // d.down_parts)
    for j in range(d.chunks):
        sizes["uc%d" % j] = sizes["ug%d" % j] = (d.CH, d.pu)
    d.routes = {name: ROUTES[name] for name in sizes}
    if d.pair > 1:
        d.routes = {name: route + "p" for name, route in d.routes.items()}
    for name, (width, s) in sizes.items():
        for i, shape in enumerate(reduce_shapes(d, width, s, d.routes[name])):
            scratch["%s_%d" % (name, i)] = VMEM(shape, wire)
    flows = 2 * d.chunks + 3 if d.split else 4
    sends = flows + len(sizes) + 9
    recvs = 4 * flows + len(sizes) * (2 + len(d.routes["sp"])) + 9
    scratch["send_sem"] = pltpu.SemaphoreType.DMA((sends,))
    scratch["recv_sem"] = pltpu.SemaphoreType.DMA((recvs,))
    scratch["token_sem"] = pltpu.SemaphoreType.DMA((8,))
    scratch["local_sem"] = pltpu.SemaphoreType.DMA((6 + len(sizes),))

    names = list(ins) + list(outs) + list(scratch)

    def kernel(*refs):
        refs = list(refs)
        have = dict(zip(names, refs))
        main_kernel(d, list(have), *have.values())

    results = pl.pallas_call(
        kernel,
        out_shape=[jax.ShapeDtypeStruct(shape, dtype) for shape, dtype, _ in outs.values()],
        in_specs=[spec for _, spec in ins.values()],
        out_specs=[spec for _, _, spec in outs.values()],
        scratch_shapes=list(scratch.values()),
        compiler_params=pltpu.CompilerParams(
            collective_id=0, has_side_effects=True, vmem_limit_bytes=63 * 1024 * 1024
        ),
        name="block_step",
    )(*[array for array, _ in ins.values()])
    got = dict(zip(outs, results))

    params = [
        up_weight,
        up_moment,
        up_square,
        down_weight,
        down_moment,
        down_square,
        spatial_weight,
        spatial_moment,
        spatial_square,
        small_params.reshape(d.ks, LANES),
        small_moment.reshape(d.ks, LANES),
        small_square.reshape(d.ks, LANES),
    ]
    passed = [got["up_low"], got["down_low"], got["sp_low"], got["gsmall"], *params]
    count = len(passed)
    updated = pl.pallas_call(
        functools.partial(adam_kernel, d, count),
        out_shape=[jax.ShapeDtypeStruct((1, 1), f32)]
        + [jax.ShapeDtypeStruct(got[name].shape, bf16) for name in ("out", "ig")]
        + [jax.ShapeDtypeStruct(p.shape, f32) for p in params],
        in_specs=[vmem_spec] + [any_spec] * (2 + count),
        out_specs=[smem_spec] + [any_spec] * (2 + len(params)),
        scratch_shapes=[VMEM(p.shape, p.dtype) for p in passed]
        + [pltpu.SemaphoreType.DMA((2 + count + 12,)), VMEM((max(d.pu, d.pd, d.ps), LANES), f32)]
        + [VMEM(got[name].shape, bf16) for name in ("out", "ig")],
        compiler_params=pltpu.CompilerParams(vmem_limit_bytes=63 * 1024 * 1024),
        name="adam_step",
    )(got["norm"], got["out"], got["ig"], *passed)
    norm, out, ig = updated[:3]
    updated = list(updated[3:12]) + [p.reshape(-1) for p in updated[12:]]
    return (
        jnp.transpose(out, (1, 0, 2)),
        jnp.transpose(ig, (1, 0, 2)),
        norm.reshape(()),
        *updated,
    )


def solution(mesh):
    rows = P("rows", None)
    flat = P("rows")
    tokens = P("blk", "rows", None)
    return jax.shard_map(
        functools.partial(body, mesh),
        mesh=mesh,
        in_specs=(tokens, tokens, rows) + (rows,) * 9 + (flat,) * 3,
        out_specs=(tokens, tokens, P()) + (rows,) * 9 + (flat,) * 3,
        check_vma=False,
    )
```

```python
import functools
import math
import types

import jax
import jax.numpy as jnp
from jax import lax
from jax.experimental import pallas as pl
from jax.experimental.pallas import tpu as pltpu
from jax.sharding import PartitionSpec as P

STEP = 10

beta_one = 0.9
beta_two = 0.999
max_norm = 1.0
weight_rate = 0.05
small_rate = 0.5
weight_decay = 0.01

MESH = pl.DeviceIdType.MESH
VMEM = pltpu.VMEM
bf16 = jnp.bfloat16
f32 = jnp.float32
LANES = 128


def loop(count, body):
    def step(i, carry):
        body(i)
        return carry

    lax.fori_loop(0, count, step, 0)


def span(start, size):
    return pl.ds(pl.multiple_of(start, size), size)


def rows_of(value, count):
    return jnp.concatenate([value] * (count // value.shape[0]), axis=0)


def lanes_of(value, count):
    return jnp.concatenate([value] * (count // value.shape[1]), axis=1)


def fold_rows(value):
    total = value[0:8]
    for first in range(8, value.shape[0], 8):
        total = total + value[first : first + 8]
    return total


def fold_lanes(value):
    total = value[:, 0:LANES]
    for first in range(LANES, value.shape[1], LANES):
        total = total + value[:, first : first + LANES]
    return total


def dot_nn(a, b):
    return lax.dot_general(a, b, (((1,), (0,)), ((), ())), preferred_element_type=f32)


def dot_nt(a, b):
    return lax.dot_general(a, b, (((1,), (1,)), ((), ())), preferred_element_type=f32)


def dot_tn(a, b):
    return lax.dot_general(a, b, (((0,), (0,)), ((), ())), preferred_element_type=f32)


def plan_of(mesh, shapes):
    d = types.SimpleNamespace()
    d.R = mesh.shape["rows"]
    d.minor = 1
    while d.minor * d.minor * 2 <= d.R:
        d.minor *= 2
    if d.minor * d.minor > d.R:
        d.minor //= 2
    d.major = d.R // d.minor
    d.block, d.rows_here, d.D = shapes["inputs"]
    d.S = d.block * mesh.shape["blk"]
    d.H = d.S // 2
    d.T = d.S + d.H
    d.FF = shapes["up"][1]
    d.G = d.FF // 2
    d.su, d.sd, d.ss = shapes["up"][0], shapes["down"][0], shapes["spatial"][0]
    d.ks = shapes["small"][0] // LANES
    d.nsmall = d.ks * d.R * LANES
    d.pair = 1
    while any(size * d.pair % 16 for size in (d.su, d.sd, d.ss)):
        d.pair *= 2
    d.minor = d.minor // d.pair
    d.pu, d.pd, d.ps = (size * d.pair for size in (d.su, d.sd, d.ss))
    d.CH = 512 if d.G % 512 == 0 else d.G
    d.chunks = d.G // d.CH
    d.split = d.R <= 16
    d.down_parts = 3 if d.pd % 48 == 0 else 1
    d.o_gain_in = 0
    d.o_shift_in = d.D
    d.o_bias_up = 2 * d.D
    d.o_gain_gate = d.o_bias_up + d.FF
    d.o_shift_gate = d.o_gain_gate + d.G
    d.o_bias_spatial = d.o_shift_gate + d.G
    d.o_bias_down = d.o_bias_spatial + d.S
    return d


class Comm:
    def __init__(self, send, recv, space):
        self.send, self.recv, self.space = send, recv, space
        self.sends, self.recvs, self.open = 0, 0, []

    def outgoing(self):
        made = Outgoing(self, self.send.at[self.sends])
        self.sends += 1
        self.open.append(made)
        return made

    def group(self, out=None):
        made = Group(self, out or self.outgoing(), self.recv.at[self.recvs])
        self.recvs += 1
        return made

    def wait(self, sem, size):
        cols = LANES
        while size // cols > self.space.shape[0]:
            cols += LANES
            while size % (cols * 16):
                cols += LANES
        ref = self.space.at[0 : size // cols, 0:cols]
        pltpu.make_async_copy(ref, ref, sem).wait()

    def finish(self):
        for made in self.open:
            self.wait(made.sem, made.size)


class Outgoing:
    def __init__(self, comm, sem):
        self.comm, self.sem, self.size = comm, sem, 0


class Group:
    def __init__(self, comm, out, sem):
        self.comm, self.out, self.sem, self.size = comm, out, sem, 0

    def start(self, src, dst, device):
        size = math.prod(src.shape) * (2 if src.dtype == f32 else 1)
        self.size += size
        self.out.size += size
        pltpu.make_async_remote_copy(
            src_ref=src,
            dst_ref=dst,
            send_sem=self.out.sem,
            recv_sem=self.sem,
            device_id=device,
            device_id_type=MESH,
        ).start()
        return self

    def wait(self):
        self.comm.wait(self.sem, self.size)


class Gather:
    def __init__(self, net, ref, s, first, width, by_y, fill):
        self.net, self.ref, self.s, self.first = net, ref, s, first
        self.half, self.by_y, self.fill = width // 2, by_y, fill
        self.size = self.half // 2 if by_y else self.half
        self.out = net.comm.outgoing()
        self.z, self.x, self.core = (net.comm.group(self.out) for _ in range(3))
        if by_y:
            self.y = net.comm.group(self.out)

    def region(self, owner, of_y=None):
        start = self.first + self.net.c * self.half
        if self.by_y:
            start = start + (self.net.y if of_y is None else of_y) * self.size
        cols = pl.ds(pl.multiple_of(start, LANES), self.size)
        return self.ref.at[span(owner * self.s, self.s), cols]

    def owner(self, dz, dx):
        n = self.net
        return lax.rem(n.zi - dz + n.major, n.major) * n.minor + lax.rem(n.xi - dx + n.minor, n.minor)

    def begin(self):
        n = self.net
        self.fill()
        mine = self.region(n.zi * n.minor + n.xi)
        for dz in range(1, n.major):
            self.z.start(mine, mine, n.at_z(dz))
        for dx in range(1, n.minor):
            self.x.start(mine, mine, n.at_x(dx))

    def onward(self, piece):
        if self.by_y:
            self.y.start(piece, piece, self.net.across)
        self.core.start(piece, piece, self.net.sibling)

    def minor(self):
        n = self.net
        self.z.wait()
        pieces = [self.region(self.owner(dz, 0)) for dz in range(1, n.major)]
        for piece in pieces:
            for dx in range(1, n.minor):
                self.x.start(piece, piece, n.at_x(dx))
        for piece in pieces:
            self.onward(piece)

    def last(self):
        n = self.net
        self.x.wait()
        for dz in range(n.major):
            for dx in range(1, n.minor):
                self.onward(self.region(self.owner(dz, dx)))

    def swap(self):
        n = self.net
        if self.by_y:
            self.y.wait()
            for dz in range(n.major):
                for dx in range(n.minor):
                    if dz or dx:
                        piece = self.region(self.owner(dz, dx), 1 - n.y)
                        self.core.start(piece, piece, n.sibling)

    def end(self):
        self.core.wait()


class Reduce:
    def __init__(self, net, part, rows, first, width, route, bufs, low):
        self.net, self.part, self.rows, self.first, self.route = net, part, rows, first, route
        self.half, self.quarter = width // 2, width // 4
        self.core, self.bufs, self.low = bufs[0], bufs[1:], low
        self.step, self.out = 0, net.comm.outgoing()

    def send(self, copies):
        self.waits = self.net.comm.group(self.out)
        for copy in copies:
            self.waits.start(*copy)

    def cols(self, start, size):
        return pl.ds(pl.multiple_of(self.first + start, LANES), size)

    def start(self):
        n, half = self.net, self.half
        src = self.part.at[:, :, self.rows, self.cols((1 - n.c) * half, half)]
        self.send([(src, self.core, n.sibling)])

    def advance(self):
        n = self.net
        self.waits.wait()
        if self.step == 0:
            mine = self.cols(n.c * self.half, self.half)
            self.zs, self.xs, self.width = n.major, n.minor, self.half

            def add(i, j):
                self.core[i, j] = self.part[i, j, self.rows, mine] + self.core[i, j]

            self.blocks(add)
            self.now = self.core
        else:
            kept, got = self.kept, self.got
            made = self.bufs[2 * self.step - 1]

            def add(i, j):
                if len(got) == 1:
                    made[i, j] = kept(i, j) + got[0][i, j]
                    return
                value = kept(i, j).astype(f32)
                for ref in got:
                    value = value + ref[i, j].astype(f32)
                made[i, j] = value.astype(made.dtype)

            self.blocks(add)
            self.now = made
        if self.step == len(self.route):
            return self.share()
        axis = self.route[self.step]
        now, into = self.now, self.bufs[2 * self.step]
        self.step += 1
        if axis == "x":
            self.send(
                (now.at[:, pl.ds(lax.rem(n.xi + dx, n.minor), 1)], into.at[dx - 1], n.at_x(dx))
                for dx in range(1, n.minor)
            )
            self.got = [into.at[dx - 1] for dx in range(1, n.minor)]
            self.kept = lambda i, j: now[i, n.xi]
            self.xs = 1
        elif axis == "z":
            self.send(
                (now.at[pl.ds(lax.rem(n.zi + dz, n.major), 1)], into.at[dz - 1], n.at_z(dz))
                for dz in range(1, n.major)
            )
            self.got = [into.at[dz - 1] for dz in range(1, n.major)]
            self.kept = lambda i, j: now[n.zi, j]
            self.zs = 1
        elif axis == "p":
            self.send((now, into.at[dp - 1], n.at_pair(dp)) for dp in range(1, n.pair))
            self.got = [into.at[dp - 1] for dp in range(1, n.pair)]
            self.kept = lambda i, j: now[i, j]
        else:
            width = self.width // 2
            theirs = pl.ds(pl.multiple_of((1 - n.y) * width, LANES), width)
            mine = pl.ds(pl.multiple_of(n.y * width, LANES), width)
            self.send([(now.at[:, :, :, theirs], into.at[0], n.across)])
            self.got = [into.at[0]]
            self.kept = lambda i, j: now[i, j, :, mine]
            self.width = width

    def blocks(self, add):
        zs, xs = self.zs, self.xs
        if zs * xs == 1:
            add(0, 0)
        else:
            loop(zs * xs, lambda i: add(i // xs, lax.rem(i, xs)))

    def share(self):
        n, mine = self.net, self.now.at[0, 0]
        self.local = pltpu.make_async_copy(mine, self.low.at[n.b], n.local_sem())
        self.local.start()
        self.send((mine, self.low.at[n.b], (n.r, lax.rem(n.b + db, 4))) for db in range(1, 4))
        kept = self.now[0, 0].astype(f32)
        return fold_lanes(fold_rows(kept * kept))

    def end(self):
        self.local.wait()
        self.waits.wait()


def reduce_shapes(d, width, s, route):
    zs, xs, wide = d.major, d.minor, width // 2
    shapes = [(zs, xs, s, wide)]
    for axis in route:
        if axis == "x":
            count, xs = max(d.minor - 1, 1), 1
        elif axis == "z":
            count, zs = max(d.major - 1, 1), 1
        elif axis == "p":
            count = d.pair - 1
        else:
            count, wide = 1, wide // 2
        shapes.append((count, zs, xs, s, wide))
        shapes.append((zs, xs, s, wide))
    return shapes


def main_kernel(d, names, *refs):
    k = types.SimpleNamespace(**dict(zip(names, refs)))
    comm = Comm(k.send_sem, k.recv_sem, k.GATE)
    r, b = lax.axis_index("rows"), lax.axis_index("blk")
    line = d.minor * d.pair
    zi, xi, xp = r // line, lax.rem(r, line) // d.pair, lax.rem(r, d.pair)
    y, c = b // 2, lax.rem(b, 2)
    S, H, T, D, G, FF, CH = d.S, d.H, d.T, d.D, d.G, d.FF, d.CH
    blk = d.block
    sibling = (r, 2 * y + 1 - c)
    across = (r, 2 * (1 - y) + c)

    def at_z(dz):
        return (lax.rem(zi + dz, d.major) * line + xi * d.pair + xp, b)

    def at_x(dx):
        return (zi * line + lax.rem(xi + dx, d.minor) * d.pair + xp, b)

    def at_pair(dp):
        return (zi * line + xi * d.pair + lax.rem(xp + dp, d.pair), b)

    used = [0]

    def local_sem():
        used[0] += 1
        return k.local_sem.at[used[0] - 1]

    net = types.SimpleNamespace(
        comm=comm, r=r, b=b, zi=zi, xi=xi, y=y, c=c, major=d.major, minor=d.minor,
        sibling=sibling, across=across, at_z=at_z, at_x=at_x, at_pair=at_pair, pair=d.pair, local_sem=local_sem,
    )

    barrier = pltpu.get_barrier_semaphore()
    for dr in range(1, d.R):
        pl.semaphore_signal(barrier, inc=1, device_id=(lax.rem(r + dr, d.R), b), device_id_type=MESH)
    for db in range(1, 4):
        pl.semaphore_signal(barrier, inc=1, device_id=(r, lax.rem(b + db, 4)), device_id_type=MESH)

    own = {}
    for name, rows in (("small", d.ks), ("up", d.su), ("sp", d.ss), ("down", d.sd)):
        stage = getattr(k, name + "_stage")
        if name != "small":
            stage = stage.at[span(xp * rows, rows)]
        own[name] = pltpu.make_async_copy(getattr(k, name + "_w"), stage, local_sem())
        own[name].start()

    def staged(name):
        own[name].wait()

    def share_pair():
        if d.pair == 1:
            return
        made = comm.group()
        for name, rows in (("up", d.su), ("sp", d.ss), ("down", d.sd)):
            mine = getattr(k, name + "_stage").at[span(xp * rows, rows)]
            for dp in range(1, d.pair):
                made.start(mine, mine, at_pair(dp))
        made.wait()

    def gather(name, ref, s, first, width, by_y):
        stage = getattr(k, name + "_stage")

        def fill():
            cols = slice(first, first + width)
            ref[span((zi * d.minor + xi) * s, s), cols] = stage[:, cols].astype(bf16)

        return Gather(net, ref, s, first, width, by_y, fill)

    def flow_of(name, i, by_y):
        if name == "ug" or name == "uc":
            step = CH if d.split else G
            return gather("up", k.UP, d.pu, (G if name == "ug" else 0) + i * step, step, by_y)
        if name == "sp":
            return gather("sp", k.SP, d.ps, 0, S, by_y)
        step = D // 2 if d.split else D
        return gather("down", k.DOWN, d.pd, i * step, step, by_y)

    flow = [flow_of(*one) for one in (FLOW if d.split else WHOLE_FLOW)]

    tokens = []
    for source, target in ((k.x_in, k.X), (k.c_in, k.C)):
        moves = []
        for g in range(4):
            moves.append((source.at[(g // 2) * 3 + g % 2], target.at[span(b * blk, blk), :], g))
        for half in range(2):
            moves.append((source.at[half * 3 + 2], target.at[span(S + c * blk, blk), :], 2 * half + y))
        tokens.append((moves, target))

    def send_blocks(moves, send, recv):
        for src, dst, g in moves:

            @pl.when(g == b)
            def _():
                pltpu.make_async_copy(src, dst, recv).start()

            @pl.when(g != b)
            def _():
                pltpu.make_async_remote_copy(
                    src_ref=src, dst_ref=dst, send_sem=send, recv_sem=recv, device_id=(r, g), device_id_type=MESH
                ).start()

    def sent_blocks(send):
        for here, count in ((y == c, 4), (y != c, 5)):

            @pl.when(here)
            def _():
                space = k.X.at[0 : count * blk, :]
                pltpu.make_async_copy(space, space, send).wait()

    def start_tokens(number):
        send_blocks(tokens[number][0], k.token_sem.at[number], k.token_sem.at[2 + number])

    def wait_tokens(number):
        target = tokens[number][1]
        pltpu.make_async_copy(target, target, k.token_sem.at[2 + number]).wait()

    def finish_tokens():
        for number in range(2):
            sent_blocks(k.token_sem.at[number])

    small_in = comm.group()

    def send_small():
        k.small_get[r] = jnp.zeros((8, LANES), f32)
        k.small_get[r, 0 : d.ks, :] = k.small_stage[...].astype(bf16).astype(f32)
        for dr in range(1, d.R):
            mine = k.small_get.at[r]
            small_in.start(mine, mine, (lax.rem(r + dr, d.R), b))

    def take_small():
        small_in.wait()
        for i in range(d.R):
            for j in range(d.ks):
                first = (i * d.ks + j) * LANES
                k.SM[:, first : first + LANES] = jnp.broadcast_to(k.small_get[i, j : j + 1, :], (8, LANES))

    def small(offset, width, rows):
        return rows_of(k.SM[:, offset : offset + width], rows)

    def label_of(places, ends, source):
        label = jnp.zeros(places.shape, f32)
        for end in ends:
            label = label + jnp.where(places >= end, 1.0, 0.0)
        if source:
            label = jnp.where(places < ends[-1], label, -1.0)
        return label

    lengths_copy = pltpu.make_async_copy(k.lengths_in, k.lengths, local_sem())
    lengths_copy.start()

    def make_labels():
        lengths_copy.wait()
        for which, row in enumerate((3 * y + c, 3 * y + 2)):
            ends = [k.lengths[0, row]]
            for n in range(1, k.lengths.shape[0]):
                ends.append(ends[-1] + k.lengths[n, row])
            lane = lax.broadcasted_iota(jnp.int32, (8, S), 1)
            k.row_t[which] = label_of(lane, ends, False)
            k.row_s[which] = label_of(lane, ends, True)
            for first in range(0, S, 64):
                place = lax.broadcasted_iota(jnp.int32, (64, LANES), 0) + first
                k.col_t[which, first : first + 64, :] = label_of(place, ends, False)
                k.col_s[which, first : first + 64, :] = label_of(place, ends, True)

    def make_mixing():
        k.FA[0:S, :] = k.SP[...].astype(f32)
        k.FB[0:S, :] = jnp.transpose(k.FA[0:S, :])

        def body(i):
            rows = span(i * 32, 32)
            keep = lanes_of(k.col_t[0, rows, :], S) == rows_of(k.row_s[0], 32)
            k.M[rows, :] = jnp.where(keep, k.FA[rows, :], 0.0).astype(bf16)
            keep = lanes_of(k.col_s[0, rows, :], S) == rows_of(k.row_t[0], 32)
            k.MT[rows, :] = jnp.where(keep, k.FB[rows, :], 0.0).astype(bf16)

        loop(S // 32, body)

        def shared(i):
            rows = span(c * H + i * 32, 32)
            keep = lanes_of(k.col_t[1, rows, :], S) == rows_of(k.row_s[1], 32)
            k.M[span(S + i * 32, 32), :] = jnp.where(keep, k.FA[rows, :], 0.0).astype(bf16)

        loop(H // 32, shared)
        own_half = pl.ds(pl.multiple_of(c * H, H), H)

        def turned(i):
            rows = span(i * 32, 32)
            keep = lanes_of(k.col_s[1, rows, :], H) == rows_of(k.row_t[1, :, own_half], 32)
            k.MTB[rows, :] = jnp.where(keep, k.FB[rows, own_half], 0.0).astype(bf16)

        loop(S // 32, turned)
        bias = k.SM[:, d.o_bias_spatial : d.o_bias_spatial + S]
        k.BS[0:S, :] = jnp.transpose(rows_of(bias, LANES))
        k.BS[S:T, :] = k.BS[span(c * H, H), :]

    def row_mean(ref, first, count, width, finish):
        def body(i):
            rows = span(first + i * 128, 128)
            total = jnp.sum(ref[rows, :], axis=1, keepdims=True) * (1.0 / width)
            ref[rows, :] = jnp.broadcast_to(finish(total), (128, LANES))

        loop(count // 128, body)

    def scale_of(spread):
        return lax.rsqrt(spread + 1e-05)

    def input_norm(at, count):
        def sums(i):
            rows = span(at + i * 64, 64)
            k.MU[rows, :] = fold_lanes(k.X[rows, :].astype(f32))

        loop(count // 64, sums)
        row_mean(k.MU, at, count, D, lambda v: v)

        def spreads(i):
            rows = span(at + i * 64, 64)
            centred = k.X[rows, :].astype(f32) - lanes_of(k.MU[rows, :], D)
            k.RX[rows, :] = fold_lanes(centred * centred)

        loop(count // 64, spreads)
        row_mean(k.RX, at, count, D, scale_of)

        def body(i):
            rows = span(at + i * 64, 64)
            centred = k.X[rows, :].astype(f32) - lanes_of(k.MU[rows, :], D)
            normed = centred * lanes_of(k.RX[rows, :], D)
            normed = normed * small(d.o_gain_in, D, 64) + small(d.o_shift_in, D, 64)
            k.N[rows, :] = normed.astype(bf16)

        loop(count // 64, body)

    def turn_normed():
        k.NT[...] = jnp.transpose(k.N[...].astype(f32)).astype(bf16)

    def gelu_parts(before):
        cdf = 0.5 + 0.5 * lax.erf(before * 0.7071067811865476)
        bell = jnp.exp(before * before * -0.5)
        return before * cdf, cdf + before * bell * 0.3989422804014327

    def up_gate(j):
        cols = slice(j * CH, (j + 1) * CH)
        at = G + j * CH
        k.F[:, cols] = dot_nn(k.N[...], k.UP[:, at : at + CH])
        bias = small(d.o_bias_up + at, CH, 16)
        for first in range(0, T, 16):
            rows = slice(first, first + 16)
            active, slope = gelu_parts(k.F[rows, cols] + bias)
            k.F[rows, cols] = active
            k.DG[rows, cols] = slope.astype(bf16)
            total = fold_lanes(active)
            k.S1[rows, :] = total if j == 0 else k.S1[rows, :] + total

    def gate_norm(first_row, count, place):
        row_mean(k.S1, first_row, count, G, lambda v: v)

        def spreads(i):
            rows = span(first_row + i * 32, 32)
            centred = k.F[rows, :] - lanes_of(k.S1[rows, :], G)
            k.RG[rows, :] = fold_lanes(centred * centred)

        loop(count // 32, spreads)
        row_mean(k.RG, first_row, count, G, scale_of)

        def body(i):
            rows = span(first_row + i * 32, 32)
            xhat = (k.F[rows, :] - lanes_of(k.S1[rows, :], G)) * lanes_of(k.RG[rows, :], G)
            k.XH[rows, :] = xhat.astype(bf16)
            gate = xhat * small(d.o_gain_gate, G, 32) + small(d.o_shift_gate, G, 32)
            k.GATE[span(place + i * 32, 32), :] = gate.astype(bf16)

        loop(count // 32, body)

    def up_content(j):
        cols = slice(j * CH, (j + 1) * CH)
        k.FA[...] = dot_nn(k.N[...], k.UP[:, cols])
        bias = small(d.o_bias_up + j * CH, CH, 16)
        for first in range(0, T, 16):
            rows = slice(first, first + 16)
            active, slope = gelu_parts(k.FA[rows, :] + bias)
            k.CT[rows, cols] = active.astype(bf16)
            k.DC[rows, cols] = slope.astype(bf16)

    def mix(j):
        cols = slice(j * CH, (j + 1) * CH)
        k.FA[0:S, :] = dot_nn(k.M[0:S, :], k.GATE[0:S, cols])
        k.FA[S:T, :] = dot_nn(k.M[S:T, :], k.GATE[S : 2 * S, cols])
        k.FB[...] = dot_nt(k.C[...], k.DOWN[cols, :])
        total = jnp.zeros((8, CH), f32)
        for first in range(0, T, 16):
            rows = slice(first, first + 16)
            out = k.FA[rows, :] + lanes_of(k.BS[rows, :], CH)
            grad = k.FB[rows, :]
            content = k.CT[rows, cols].astype(f32)
            k.PR[rows, cols] = (content * out).astype(bf16)
            grad_spatial = (grad * content).astype(bf16)
            k.GS[rows, cols] = grad_spatial
            along = fold_lanes(grad_spatial.astype(f32))
            k.BSA[rows, :] = along if j == 0 else k.BSA[rows, :] + along
            before = (grad * out * k.DC[rows, cols].astype(f32)).astype(bf16)
            k.GB[rows, cols] = before
            total = total + fold_rows(before.astype(f32))
        k.SG[:, d.o_bias_up + j * CH : d.o_bias_up + (j + 1) * CH] = total

    def project(i):
        rows = slice(i * 2 * blk, (i + 1) * 2 * blk)
        k.FA[rows, 0:D] = dot_nn(k.PR[rows, :], k.DOWN[...])
        for first in range(i * 2 * blk, (i + 1) * 2 * blk, 16):
            part = slice(first, first + 16)
            value = k.FA[part, 0:D] + small(d.o_bias_down, D, 16) + k.X[part, :].astype(f32)
            k.OT[part, :] = value.astype(bf16)

    def grad_down():
        step = d.pd * max(1, 384 // d.pd)
        for first in range(0, G, step):
            size = min(step, G - first)
            value = dot_tn(k.PR[:, first : first + size], k.C[...])
            for owner in range(first // d.pd, (first + size) // d.pd):
                at = owner * d.pd - first
                k.PD[owner // d.minor, owner % d.minor] = value[at : at + d.pd].astype(k.PD.dtype)

    def grad_up(first):
        cols = slice(first, first + CH)
        value = dot_nn(k.NT[...], k.GB[:, cols])
        k.PU[:, :, :, cols] = value.reshape(d.major, d.minor, d.pu, CH).astype(k.PU.dtype)

    def grad_spatial_weight():
        k.FA[0:S, 0:S] = dot_nt(k.GS[0:S, :], k.GATE[0:S, :])
        k.FB[0:H, 0:S] = dot_nt(k.GS[S:T, :], k.GATE[S : 2 * S, :])

        def body(i):
            rows = span(i * 32, 32)
            keep = lanes_of(k.col_t[0, rows, :], S) == rows_of(k.row_s[0], 32)
            k.FA[rows, 0:S] = jnp.where(keep, k.FA[rows, 0:S], 0.0)

        loop(S // 32, body)

        def shared(i):
            rows = span(c * H + i * 32, 32)
            keep = lanes_of(k.col_t[1, rows, :], S) == rows_of(k.row_s[1], 32)
            k.FA[rows, 0:S] = k.FA[rows, 0:S] + jnp.where(keep, k.FB[span(i * 32, 32), 0:S], 0.0)

        loop(H // 32, shared)
        k.PS[...] = k.FA[0:S, 0:S].reshape(d.major, d.minor, d.ps, S).astype(k.PS.dtype)

    def grad_gate_shared():
        other = span((1 - c) * H, H)
        for j in range(d.chunks):
            cols = slice(j * CH, (j + 1) * CH)
            k.GX[:, cols] = dot_nn(k.MTB[other, :], k.GS[S:T, cols]).astype(bf16)
        return comm.group().start(k.GX, k.GY, sibling)

    def gate_terms(rows, cols, grad, j, sums):
        xhat = k.XH[rows, cols].astype(f32)
        product = grad * xhat
        gain = small(d.o_gain_gate + j * CH, CH, 16)
        one, two = fold_lanes(grad * gain), fold_lanes(product * gain)
        k.S1[rows, :] = one if j == 0 else k.S1[rows, :] + one
        k.S2[rows, :] = two if j == 0 else k.S2[rows, :] + two
        return sums[0] + fold_rows(product), sums[1] + fold_rows(grad)

    def grad_gate(j):
        cols = slice(j * CH, (j + 1) * CH)
        mine = span(c * H, H)
        k.F[S:T, cols] = dot_nn(k.MTB[mine, :], k.GS[S:T, cols])
        k.F[0:S, cols] = dot_nn(k.MT[...], k.GS[0:S, cols])
        sums = (jnp.zeros((8, CH), f32), jnp.zeros((8, CH), f32))
        for first in range(0, S, 16):
            rows = slice(first, first + 16)
            sums = gate_terms(rows, cols, k.F[rows, cols], j, sums)
        for offset, total in zip((d.o_gain_gate, d.o_shift_gate), sums):
            k.SG[:, offset + j * CH : offset + (j + 1) * CH] = total

    def grad_gate_other(j):
        cols = slice(j * CH, (j + 1) * CH)
        sums = (jnp.zeros((8, CH), f32), jnp.zeros((8, CH), f32))
        for first in range(S, T, 16):
            rows = slice(first, first + 16)
            grad = k.F[rows, cols] + k.GY[first - S : first - S + 16, cols].astype(f32)
            k.F[rows, cols] = grad
            sums = gate_terms(rows, cols, grad, j, sums)
        for offset, total in zip((d.o_gain_gate, d.o_shift_gate), sums):
            at = slice(offset + j * CH, offset + (j + 1) * CH)
            k.SG[:, at] = k.SG[:, at] + total

    def gate_back(j):
        cols = slice(j * CH, (j + 1) * CH)
        gain = small(d.o_gain_gate + j * CH, CH, 16)
        total = jnp.zeros((8, CH), f32)
        for first in range(0, T, 16):
            rows = slice(first, first + 16)
            scaled = k.F[rows, cols] * gain - lanes_of(k.S1[rows, :], CH)
            back = scaled - k.XH[rows, cols].astype(f32) * lanes_of(k.S2[rows, :], CH)
            back = back * lanes_of(k.RG[rows, :], CH)
            before = (back * k.DG[rows, cols].astype(f32)).astype(bf16)
            k.GB[rows, G + j * CH : G + (j + 1) * CH] = before
            total = total + fold_rows(before.astype(f32))
        k.SG[:, d.o_bias_up + G + j * CH : d.o_bias_up + G + (j + 1) * CH] = total

    def grad_normed(i):
        rows = slice(i * 2 * blk, (i + 1) * 2 * blk)
        k.FB[rows, 0:D] = dot_nt(k.GB[rows, :], k.UP[...])

    def input_back(which):
        at = which * 2 * blk

        def parts(rows):
            xhat = (k.X[rows, :].astype(f32) - lanes_of(k.MU[rows, :], D)) * lanes_of(k.RX[rows, :], D)
            grad = k.FB[rows, 0:D]
            return xhat, grad, grad * small(d.o_gain_in, D, 64)

        def sums(i):
            rows = span(at + i * 64, 64)
            xhat, grad, scaled = parts(rows)
            k.S1[rows, :] = fold_lanes(scaled)
            k.S2[rows, :] = fold_lanes(scaled * xhat)

        loop(2 * blk // 64, sums)
        row_mean(k.S1, at, 2 * blk, D, lambda v: v)
        row_mean(k.S2, at, 2 * blk, D, lambda v: v)
        if which == 0:
            for offset in (d.o_gain_in, d.o_shift_in, d.o_bias_down):
                k.SG[:, offset : offset + D] = jnp.zeros((8, D), f32)

        def body(i):
            rows = span(at + i * 64, 64)
            xhat, grad, scaled = parts(rows)
            cot = k.C[rows, :].astype(f32)
            back = scaled - lanes_of(k.S1[rows, :], D) - xhat * lanes_of(k.S2[rows, :], D)
            k.IT[rows, :] = (back * lanes_of(k.RX[rows, :], D) + cot).astype(bf16)
            for offset, term in ((d.o_gain_in, grad * xhat), (d.o_shift_in, grad), (d.o_bias_down, cot)):
                k.SG[:, offset : offset + D] = k.SG[:, offset : offset + D] + fold_rows(term)

        loop(2 * blk // 64, body)

    back = []
    for source, target in ((k.OT, k.out), (k.IT, k.ig)):
        moves = []
        for g in range(4):
            moves.append((source.at[g * blk : (g + 1) * blk, :], target.at[3 * y + c], g))
        for half in range(2):
            here = source.at[S + half * blk : S + (half + 1) * blk, :]
            moves.append((here, target.at[3 * y + 2], 2 * c + half))
        back.append((moves, target))

    def start_back(number, part):
        moves = back[number][0][2 * part : 2 * part + 2]
        send_blocks(moves, k.token_sem.at[4 + number], k.token_sem.at[6 + number])

    def finish_back():
        for number in range(2):
            target = back[number][1]
            pltpu.make_async_copy(target, target, k.token_sem.at[6 + number]).wait()
            sent_blocks(k.token_sem.at[4 + number])

    def reduce(name, part, rows, first, width, low):
        route = d.routes[name]
        bufs = [getattr(k, "%s_%d" % (name, i)) for i in range(1 + 2 * len(route))]
        return Reduce(net, part, rows, first, width, route, bufs, low)

    red = {}
    for j in range(d.chunks):
        rows = slice(0, d.pu)
        red["uc%d" % j] = reduce("uc%d" % j, k.PU, rows, j * CH, CH, k.up_low.at[j])
        red["ug%d" % j] = reduce("ug%d" % j, k.PU, rows, G + j * CH, CH, k.up_low.at[d.chunks + j])
    size = d.pd // d.down_parts
    for j in range(d.down_parts):
        rows = slice(j * size, (j + 1) * size)
        red["dn%d" % j] = reduce("dn%d" % j, k.PD, rows, 0, D, k.down_low.at[j])
    red["sp"] = reduce("sp", k.PS, slice(0, d.ps), 0, S, k.sp_low)

    def column_sums():
        bias = jnp.sum(jnp.transpose(k.BSA[...]), axis=0, keepdims=True)
        k.SG[:, d.o_bias_spatial : d.o_bias_spatial + S] = jnp.zeros((8, S), f32)
        k.SG[0:1, d.o_bias_spatial : d.o_bias_spatial + S] = bias[:, 0:S]
        place = pl.ds(pl.multiple_of(d.o_bias_spatial + c * H, H), H)
        k.SG[0:1, place] = k.SG[0:1, place] + bias[:, S:T]
        for i in range(d.nsmall // LANES):
            total = jnp.sum(k.SG[:, i * LANES : (i + 1) * LANES], axis=0, keepdims=True)
            k.small_part[i : i + 1, :] = total

    quarter = d.nsmall // LANES // 4

    def small_blk():
        made = comm.group()
        for db in range(1, 4):
            other = lax.rem(b + db, 4)
            part = k.small_part.at[span(other * quarter, quarter), :]
            made.start(part, k.small_one.at[db - 1], (r, other))
        return made

    def to_rows(ref):
        made = comm.group()
        for dr in range(1, d.R):
            made.start(ref.at[0], ref.at[dr], (lax.rem(r + dr, d.R), b))
        return made

    def to_blk(src, dst):
        made = comm.group()
        for db in range(1, 4):
            made.start(src, dst, (r, lax.rem(b + db, 4)))
        return made

    def small_rows(before):
        before.wait()
        value = k.small_part[span(b * quarter, quarter), :]
        for i in range(3):
            value = value + k.small_one[i]
        k.small_two[0] = value
        return to_rows(k.small_two)

    def small_share(before):
        before.wait()
        value = k.small_two[0]
        for dr in range(1, d.R):
            value = value + k.small_two[dr]
        k.small_sum[...] = value
        mine = k.gsmall.at[span(b * quarter, quarter), :]
        local = pltpu.make_async_copy(k.small_sum, mine, local_sem())
        local.start()
        return local, to_blk(k.small_sum, mine), fold_rows(value * value)

    schedule(d, types.SimpleNamespace(**locals()))


ORDER = (
    "b0", "b1", "sm", "b2", "m0", "b3", "m1", "b4", "b5", "T0", "t1", "n0", "b6", "l0", "n1", "b7", "m2", "n2",
    "l1", "m3", "e0", "G0", "m4", "e1", "G1", "b8", "m5", "tn", "m6", "l2", "l3", "l4", "e2", "G2", "gs", "l5",
    "m7", "T1", "ga", "l6", "gw", "m8", "w3", "l7", "w4", "e3", "c0", "e7", "w5", "e4", "c1", "w6", "e5", "c2",
    "l8", "e6", "mx", "e8", "x0", "u0", "x1", "uc0", "u1", "x2", "uc1", "u2", "p0", "p1", "p2", "gx", "gd",
    "uc0", "uc2", "uc1", "S", "q0", "dn0", "dn1", "dn2", "ow", "q1", "uc2", "uc0", "sp", "q2", "ot", "dn1",
    "dn0", "uc1", "k0", "v0", "sp", "k1", "dn2", "uc2", "uc0", "v1", "ug0", "dn1", "uc1", "k2", "dn0", "ug1",
    "dn2", "v2", "uc2", "r0", "i0", "r1", "ug2", "ug0", "sp", "dn1", "dn0", "dn2", "i1", "ug1", "r2", "sp",
    "i2", "ug2", "ug0", "cs", "ug1", "ug2", "ug0", "sr", "ug1", "ug2",
)


ROUTES = dict(dn0="yzx", dn1="xzy", dn2="xyz", sp="xzy", uc0="xzy", uc1="yzx", uc2="xzy", ug0="xzy", ug1="xyz", ug2="xzy")
FLOW = (("ug", 0, False), ("ug", 1, False), ("ug", 2, False), ("uc", 0, True), ("uc", 1, True), ("uc", 2, True), ("sp", 0, True), ("dn", 0, False), ("dn", 1, False))
WHOLE_FLOW = (("ug", 0, False), ("sp", 0, False), ("dn", 0, False), ("uc", 0, False))


def plain_order(d, groups):
    order = ["b0", "b1", "sm", "T0", "n0", "n1", "n2", "tn", "t1"]
    for i in range(groups):
        order += ["m%d" % i, "l%d" % i, "w%d" % i, "e%d" % i]
        if i + 2 < groups:
            order.append("b%d" % (i + 2))
    each = range(d.chunks)
    order += ["G%d" % j for j in each] + ["gs", "ga", "mx", "T1", "gw"]
    for j in each:
        order += ["c%d" % j, "x%d" % j, "u%d" % j]
    order += ["p0", "p1", "p2", "gx", "gd"] + ["q%d" % j for j in each] + ["ow", "ot"]
    for j in each:
        order += ["k%d" % j, "v%d" % j]
    order += ["S", "r0", "i0", "r1", "i1", "r2", "i2", "cs", "sr"]
    sums = [n + str(j) for n in ("uc", "ug") for j in each] + ["dn%d" % j for j in range(d.down_parts)] + ["sp"]
    return order + sums * (4 + (d.pair > 1))


def schedule(d, p):
    k, comm, flow, red = p.k, p.comm, p.flow, p.red
    chunks, r, b, G, CH = d.chunks, p.r, p.b, d.G, d.CH
    kept = {}
    squares = []
    steps = {}

    def step(name):
        def add(function):
            steps[name] = function

        return add

    for i, one in enumerate(flow):
        for letter, function in zip("bmlwe", (one.begin, one.minor, one.last, one.swap, one.end)):
            steps[letter + str(i)] = function
    for i in range(2):
        steps["t%d" % i] = functools.partial(p.start_tokens, i)
        steps["T%d" % i] = functools.partial(p.wait_tokens, i)
    steps["sm"] = p.take_small
    for i in range(3):
        steps["n%d" % i] = functools.partial(p.input_norm, 2 * d.block * i, 2 * d.block)
    for j in range(chunks):
        steps["G%d" % j] = functools.partial(p.up_gate, j)
        steps["c%d" % j] = functools.partial(p.up_content, j)
        steps["x%d" % j] = functools.partial(p.mix, j)
        steps["q%d" % j] = functools.partial(p.grad_gate, j)
        steps["k%d" % j] = functools.partial(p.gate_back, j)

    @step("gs")
    def _():
        p.gate_norm(d.S, d.H, d.S + p.c * d.H)
        mine = k.GATE.at[span(d.S + p.c * d.H, d.H), :]
        kept["gate"] = comm.group().start(mine, mine, p.sibling)

    steps["ga"] = functools.partial(p.gate_norm, 0, d.S, 0)
    steps["gw"] = lambda: kept["gate"].wait()
    steps["tn"] = p.turn_normed
    steps["mx"] = p.make_mixing

    def grad_up(j, name, first):
        p.grad_up(first + j * CH)
        red[name + str(j)].start()

    for j in range(chunks):
        steps["u%d" % j] = functools.partial(grad_up, j, "uc", 0)
        steps["v%d" % j] = functools.partial(grad_up, j, "ug", G)

    def project(i):
        p.project(i)
        p.start_back(0, i)

    def input_back(i):
        p.input_back(i)
        p.start_back(1, i)

    for i in range(3):
        steps["p%d" % i] = functools.partial(project, i)
        steps["r%d" % i] = functools.partial(p.grad_normed, i)
        steps["i%d" % i] = functools.partial(input_back, i)

    @step("gx")
    def _():
        kept["gradient"] = p.grad_gate_shared()

    @step("gd")
    def _():
        p.grad_down()
        for j in range(d.down_parts):
            red["dn%d" % j].start()

    steps["ow"] = lambda: kept["gradient"].wait()

    @step("ot")
    def _():
        for j in range(chunks):
            p.grad_gate_other(j)
        p.row_mean(k.S1, 0, d.T, G, lambda v: v)
        p.row_mean(k.S2, 0, d.T, G, lambda v: v)

    @step("S")
    def _():
        p.grad_spatial_weight()
        red["sp"].start()

    @step("cs")
    def _():
        p.column_sums()
        kept["small"] = p.small_blk()

    @step("sr")
    def _():
        kept["small"] = p.small_rows(kept["small"])

    def advance(one):
        value = one.advance()
        if value is not None:
            squares.append(value)

    for name, one in red.items():
        steps[name] = functools.partial(advance, one)

    for name in ("small", "up", "sp", "down"):
        p.staged(name)
    pl.semaphore_wait(p.barrier, d.R - 1 + 3)
    p.start_tokens(0)
    p.share_pair()
    p.send_small()
    steps["b0"]()
    steps["b1"]()
    p.make_labels()
    for name in (ORDER if d.split else plain_order(d, len(flow)))[2:]:
        steps[name]()
    small = kept["small"]
    total = squares[0]
    for value in squares[1:]:
        total = total + value
    k.norm_rows[0] = total
    norm_one = p.to_rows(k.norm_rows)
    local, shared, extra = p.small_share(small)
    norm_one.wait()
    value = extra
    for i in range(d.R):
        value = value + k.norm_rows[lax.rem(i - r + 2 * d.R, d.R)]
    k.norm_blk[b] = value
    norm_two = p.to_blk(k.norm_blk.at[b], k.norm_blk.at[b])
    for one in red.values():
        one.end()
    local.wait()
    shared.wait()
    norm_two.wait()
    value = k.norm_blk[0]
    for i in range(1, 4):
        value = value + k.norm_blk[i]
    k.norm[...] = jnp.sqrt(jnp.full((8, LANES), jnp.sum(value), f32))
    p.finish_back()
    p.finish_tokens()
    comm.finish()

def adam_kernel(d, count, *refs):
    norm, out_in, ig_in = refs[:3]
    given = refs[3 : 3 + count]
    norm_out, out, ig = refs[3 + count : 6 + count]
    results = refs[6 + count : 18 + count]
    held = refs[18 + count : 18 + 2 * count]
    sems, turned, held_out, held_ig = refs[18 + 2 * count :]
    r = lax.axis_index("rows")
    through = [
        (pltpu.make_async_copy(src, held, sems.at[i]), pltpu.make_async_copy(held, dst, sems.at[i]))
        for i, (src, held, dst) in enumerate(((out_in, held_out, out), (ig_in, held_ig, ig)))
    ]
    loads = [pltpu.make_async_copy(src, dst, sems.at[2 + i]) for i, (src, dst) in enumerate(zip(given, held))]
    for copy in loads + [first for first, _ in through]:
        copy.start()
    value = norm[...]
    norm_out[0, 0] = norm[0, 0]
    factor = jnp.minimum(1.0, max_norm / (value + 1e-06))
    low_up, low_down, low_sp, gsmall = held[:4]
    params = held[4:]
    stores = []

    def step(ins, grad, rate, decay, place):
        weight, moment, square = (ref[place] for ref in ins)
        grad = grad * factor[0:1, :]
        moment_next = beta_one * moment + (1.0 - beta_one) * grad
        square_next = beta_two * square + (1.0 - beta_two) * grad * grad
        moment_hat = moment_next / (1.0 - beta_one**STEP)
        square_hat = square_next / (1.0 - beta_two**STEP)
        update = moment_hat / (jnp.sqrt(square_hat) + 1e-08) + decay * weight
        for ref, result in zip(ins, (weight - rate * update, moment_next, square_next)):
            ref[place] = result

    def store(i):
        for j in range(3):
            n = 3 * i + j
            copy = pltpu.make_async_copy(params[n], results[n], sems.at[2 + count + n])
            copy.start()
            stores.append(copy)

    def part(low, q, first, s, width):
        start = first + (2 * (q % 2) + q // 2) * (width // 4)
        for at in range(0, width // 4, LANES):
            grad = low[q, :, at : at + LANES].astype(f32)
            if d.pair > 1:
                turned[0 : d.pair * s, :] = grad
                grad = turned[pl.ds(pl.multiple_of(lax.rem(r, d.pair) * s, s), s), :]
            yield grad, (slice(0, s), slice(start + at, start + at + LANES))

    for i in (0, 4, 5, 6):
        loads[i].wait()
    for j in range(2 * d.chunks):
        for q in range(4):
            for grad, place in part(low_up.at[j], q, j * d.CH, d.su, d.CH):
                step(params[0:3], grad, weight_rate, weight_decay, place)
    store(0)
    for first, second in through:
        first.wait()
        second.start()
        stores.append(second)
    for i in (1, 7, 8, 9):
        loads[i].wait()
    for q in range(4):
        start = (2 * (q % 2) + q // 2) * (d.D // 4)
        size = d.pd // d.down_parts
        for at in range(0, d.D // 4, LANES):
            cols = slice(start + at, start + at + LANES)
            for i in range(d.down_parts):
                grad = low_down[i, q, :, at : at + LANES].astype(f32)
                if d.pair == 1:
                    step(params[3:6], grad, weight_rate, weight_decay, (slice(i * size, (i + 1) * size), cols))
                else:
                    turned[i * size : (i + 1) * size, :] = grad
            if d.pair > 1:
                grad = turned[pl.ds(pl.multiple_of(lax.rem(r, d.pair) * d.sd, d.sd), d.sd), :]
                step(params[3:6], grad, weight_rate, weight_decay, (slice(0, d.sd), cols))
    store(1)
    for i in (2, 10, 11, 12):
        loads[i].wait()
    for q in range(4):
        for grad, place in part(low_sp, q, 0, d.ss, d.S):
            step(params[6:9], grad, weight_rate, weight_decay, place)
    store(2)
    for i in (3, 13, 14, 15):
        loads[i].wait()
    grad = gsmall[pl.ds(r * d.ks, d.ks), :]
    step(params[9:12], grad, small_rate, 0.0, (slice(0, d.ks), slice(0, LANES)))
    store(3)
    for copy in stores:
        copy.wait()


def body(mesh, *arrays):
    (
        inputs,
        cotangent,
        lengths,
        up_weight,
        up_moment,
        up_square,
        down_weight,
        down_moment,
        down_square,
        spatial_weight,
        spatial_moment,
        spatial_square,
        small_params,
        small_moment,
        small_square,
    ) = arrays
    d = plan_of(
        mesh,
        dict(
            inputs=inputs.shape,
            up=up_weight.shape,
            down=down_weight.shape,
            spatial=spatial_weight.shape,
            small=small_params.shape,
        ),
    )
    S, H, T, D, G, FF, R = d.S, d.H, d.T, d.D, d.G, d.FF, d.R
    wire = bf16
    small_rows = d.nsmall // LANES
    quarter = small_rows // 4

    any_spec = pl.BlockSpec(memory_space=pl.ANY)
    vmem_spec = pl.BlockSpec(memory_space=VMEM)
    smem_spec = pl.BlockSpec(memory_space=pltpu.SMEM)

    ins = dict(
        x_in=(jnp.transpose(inputs, (1, 0, 2)), any_spec),
        c_in=(jnp.transpose(cotangent, (1, 0, 2)), any_spec),
        lengths_in=(lengths.T, any_spec),
        up_w=(up_weight, any_spec),
        down_w=(down_weight, any_spec),
        sp_w=(spatial_weight, any_spec),
        small_w=(small_params.reshape(d.ks, LANES), any_spec),
    )
    outs = dict(
        out=((d.rows_here, d.block, D), bf16, any_spec),
        ig=((d.rows_here, d.block, D), bf16, any_spec),
        norm=((8, LANES), f32, vmem_spec),
        gsmall=((small_rows, LANES), f32, any_spec),
        up_low=((2 * d.chunks, 4, d.pu, d.CH // 4), wire, any_spec),
        down_low=((d.down_parts, 4, d.pd // d.down_parts, D // 4), wire, any_spec),
        sp_low=((4, d.ps, S // 4), wire, any_spec),
    )
    scratch = dict(
        lengths=pltpu.SMEM(lengths.T.shape, jnp.int32),
        up_stage=VMEM((d.pu, FF), f32),
        down_stage=VMEM((d.pd, D), f32),
        sp_stage=VMEM((d.ps, S), f32),
        small_stage=VMEM((d.ks, LANES), f32),
        small_get=VMEM((R, 8, LANES), f32),
        SM=VMEM((8, d.nsmall), f32),
        SG=VMEM((8, d.nsmall), f32),
        UP=VMEM((D, FF), bf16),
        DOWN=VMEM((G, D), bf16),
        SP=VMEM((S, S), bf16),
        X=VMEM((T, D), bf16),
        C=VMEM((T, D), bf16),
        N=VMEM((T, D), bf16),
        NT=VMEM((D, T), bf16),
        F=VMEM((T, G), f32),
        FA=VMEM((T, 512), f32),
        FB=VMEM((T, 512), f32),
        DG=VMEM((T, G), bf16),
        XH=VMEM((T, G), bf16),
        RG=VMEM((T, LANES), f32),
        GATE=VMEM((2 * S, G), bf16),
        CT=VMEM((T, G), bf16),
        DC=VMEM((T, G), bf16),
        PR=VMEM((T, G), bf16),
        GS=VMEM((T, G), bf16),
        GB=VMEM((T, FF), bf16),
        GX=VMEM((H, G), bf16),
        GY=VMEM((H, G), bf16),
        BS=VMEM((T, LANES), f32),
        BSA=VMEM((T, LANES), f32),
        M=VMEM((T, S), bf16),
        MT=VMEM((S, S), bf16),
        MTB=VMEM((S, H), bf16),
        row_t=VMEM((2, 8, S), f32),
        row_s=VMEM((2, 8, S), f32),
        col_t=VMEM((2, S, LANES), f32),
        col_s=VMEM((2, S, LANES), f32),
        OT=VMEM((T, D), bf16),
        IT=VMEM((T, D), bf16),
        PU=VMEM((d.major, d.minor, d.pu, FF), wire),
        PD=VMEM((d.major, d.minor, d.pd, D), wire),
        PS=VMEM((d.major, d.minor, d.ps, S), wire),
        MU=VMEM((T, LANES), f32),
        RX=VMEM((T, LANES), f32),
        S1=VMEM((T, LANES), f32),
        S2=VMEM((T, LANES), f32),
        small_sum=VMEM((quarter, LANES), f32),
        small_part=VMEM((small_rows, LANES), f32),
        small_one=VMEM((3, quarter, LANES), f32),
        small_two=VMEM((R, quarter, LANES), f32),
        norm_rows=VMEM((R, 8, LANES), f32),
        norm_blk=VMEM((4, 8, LANES), f32),
    )
    sizes = {"sp": (S, d.ps)}
    for j in range(d.down_parts):
        sizes["dn%d" % j] = (D, d.pd // d.down_parts)
    for j in range(d.chunks):
        sizes["uc%d" % j] = sizes["ug%d" % j] = (d.CH, d.pu)
    d.routes = {name: ROUTES[name] for name in sizes}
    if d.pair > 1:
        d.routes = {name: route + "p" for name, route in d.routes.items()}
    for name, (width, s) in sizes.items():
        for i, shape in enumerate(reduce_shapes(d, width, s, d.routes[name])):
            scratch["%s_%d" % (name, i)] = VMEM(shape, wire)
    flows = 2 * d.chunks + 3 if d.split else 4
    sends = flows + len(sizes) + 9
    recvs = 4 * flows + len(sizes) * (2 + len(d.routes["sp"])) + 9
    scratch["send_sem"] = pltpu.SemaphoreType.DMA((sends,))
    scratch["recv_sem"] = pltpu.SemaphoreType.DMA((recvs,))
    scratch["token_sem"] = pltpu.SemaphoreType.DMA((8,))
    scratch["local_sem"] = pltpu.SemaphoreType.DMA((6 + len(sizes),))

    names = list(ins) + list(outs) + list(scratch)

    def kernel(*refs):
        refs = list(refs)
        have = dict(zip(names, refs))
        main_kernel(d, list(have), *have.values())

    results = pl.pallas_call(
        kernel,
        out_shape=[jax.ShapeDtypeStruct(shape, dtype) for shape, dtype, _ in outs.values()],
        in_specs=[spec for _, spec in ins.values()],
        out_specs=[spec for _, _, spec in outs.values()],
        scratch_shapes=list(scratch.values()),
        compiler_params=pltpu.CompilerParams(
            collective_id=0, has_side_effects=True, vmem_limit_bytes=63 * 1024 * 1024
        ),
        name="block_step",
    )(*[array for array, _ in ins.values()])
    got = dict(zip(outs, results))

    params = [
        up_weight,
        up_moment,
        up_square,
        down_weight,
        down_moment,
        down_square,
        spatial_weight,
        spatial_moment,
        spatial_square,
        small_params.reshape(d.ks, LANES),
        small_moment.reshape(d.ks, LANES),
        small_square.reshape(d.ks, LANES),
    ]
    passed = [got["up_low"], got["down_low"], got["sp_low"], got["gsmall"], *params]
    count = len(passed)
    updated = pl.pallas_call(
        functools.partial(adam_kernel, d, count),
        out_shape=[jax.ShapeDtypeStruct((1, 1), f32)]
        + [jax.ShapeDtypeStruct(got[name].shape, bf16) for name in ("out", "ig")]
        + [jax.ShapeDtypeStruct(p.shape, f32) for p in params],
        in_specs=[vmem_spec] + [any_spec] * (2 + count),
        out_specs=[smem_spec] + [any_spec] * (2 + len(params)),
        scratch_shapes=[VMEM(p.shape, p.dtype) for p in passed]
        + [pltpu.SemaphoreType.DMA((2 + count + 12,)), VMEM((max(d.pu, d.pd, d.ps), LANES), f32)]
        + [VMEM(got[name].shape, bf16) for name in ("out", "ig")],
        compiler_params=pltpu.CompilerParams(vmem_limit_bytes=63 * 1024 * 1024),
        name="adam_step",
    )(got["norm"], got["out"], got["ig"], *passed)
    norm, out, ig = updated[:3]
    updated = list(updated[3:12]) + [p.reshape(-1) for p in updated[12:]]
    return (
        jnp.transpose(out, (1, 0, 2)),
        jnp.transpose(ig, (1, 0, 2)),
        norm.reshape(()),
        *updated,
    )


def solution(mesh):
    rows = P("rows", None)
    flat = P("rows")
    tokens = P("blk", "rows", None)
    return jax.shard_map(
        functools.partial(body, mesh),
        mesh=mesh,
        in_specs=(tokens, tokens, rows) + (rows,) * 9 + (flat,) * 3,
        out_specs=(tokens, tokens, P()) + (rows,) * 9 + (flat,) * 3,
        check_vma=False,
    )
```
